32 devices in a mesh: dp: 8 (over z, x), tensor: 4 (over y, core).
Axes of the slice: x: 2, y: 2, z: 4, core: 2. Of those that a mesh axis runs over, the one named last changes fastest.
Arguments:
- text_embed: bfloat16 [8192, 768], P(('dp', 'tensor')), may hold values from -6 to 6
- vision_embed: bfloat16 [8192, 768], P(('dp', 'tensor')), may hold values from -6 to 6
- region_mask: int32 [8192], P('dp'), may hold values from 0 to 1, as said below
- modality: int32 [8192], P('dp'), may hold values from 0 to 1, as said below
- doc_split: int32 [64], P('dp'), may hold values from 0 to 1
- norm_gain: float32 [2, 2, 768], replicated, may hold values from 0.5 to 1.5
- norm_bias: float32 [2, 2, 768], replicated, may hold values from -4 to 4
- qkv_weight: bfloat16 [2, 3, 768, 768], P(None, None, None, 'tensor'), may hold values from -0.21875 to 0.21875
- qv_bias: float32 [2, 2, 768], P(None, None, 'tensor'), may hold values from -4 to 4
- out_weight: bfloat16 [2, 768, 768], P(None, 'tensor'), may hold values from -1.25 to 1.25
- out_bias: float32 [2, 768], replicated, may hold values from -4 to 4
- gates: float32 [2, 4, 768], replicated, may hold values from -6 to 6
- up_weight: bfloat16 [2, 768, 3072], P(None, None, 'tensor'), may hold values from -0.21875 to 0.21875
- up_bias: float32 [2, 3072], P(None, 'tensor'), may hold values from -6 to 6
- down_weight: bfloat16 [2, 3072, 768], P(None, 'tensor'), may hold values from -0.109375 to 0.109375
- down_bias: float32 [2, 768], replicated, may hold values from -4 to 4
- cotangent: bfloat16 [8192, 768], P(('dp', 'tensor')), may hold values from -6 to 6
Outputs:
- joined: bfloat16 [8192, 768], P(('dp', 'tensor'))
- text_grad: float32 [8192, 768], P(('dp', 'tensor'))
- vision_grad: float32 [8192, 768], P(('dp', 'tensor'))
- norm_gain_grad: float32 [2, 2, 768], replicated
- norm_bias_grad: float32 [2, 2, 768], replicated
- qkv_weight_grad: float32 [2, 3, 768, 768], P(None, None, None, 'tensor')
- qv_bias_grad: float32 [2, 2, 768], P(None, None, 'tensor')
- out_weight_grad: float32 [2, 768, 768], P(None, 'tensor')
- out_bias_grad: float32 [2, 768], replicated
- gates_grad: float32 [2, 4, 768], replicated
- up_weight_grad: float32 [2, 768, 3072], P(None, None, 'tensor')
- up_bias_grad: float32 [2, 3072], P(None, 'tensor')
- down_weight_grad: float32 [2, 3072, 768], P(None, 'tensor')
- down_bias_grad: float32 [2, 768], replicated
The draws below stay inside these ranges and needn't reach their ends.
Inputs may be any that keep to these rules, and one draw needn't show every extreme that they name: `region_mask`: in every aligned block of 64 slots the real regions come first and number 16 or more. In every aligned block of 64 slots, slot 0 has modality 0 and slot 1 has modality 1.
All inputs are finite; a program needn't handle non-finite values.
Results may differ from the reference program's by a relative error of at most 0.025.
Values may be sent and summed in bfloat16 or wider, within the bound.
No kernel may reach another device: no remote copies, remote signals or barrier semaphores. Data moves between devices by JAX's collectives and lax.ppermute only.
A program may use at most 128 MiB of HBM per device.

```python
import math
import jax
import jax.numpy as jnp
from jax import lax

D = 768
HEADS = 12
HEAD_DIM = 64
FF = 3072
LAYERS = 2
SLOTS = 128
TOKENS = 8192
GROUPS = 64
N_TENSOR = 4


def draw_region_mask(key, part):
    key = jax.random.fold_in(key, 11)
    blocks = TOKENS // (SLOTS // 2)
    counts = jax.random.randint(key, (blocks, 1), 16, SLOTS // 2 + 1)
    places = jnp.arange(SLOTS // 2, dtype=jnp.int32)[None, :]
    return (places < counts).astype(jnp.int32).reshape(TOKENS)


def draw_modality(key, part):
    key = jax.random.fold_in(key, 23)
    blocks = TOKENS // (SLOTS // 2)
    kinds = jax.random.randint(key, (blocks, SLOTS // 2), 0, 2)
    places = jnp.arange(SLOTS // 2, dtype=jnp.int32)[None, :]
    kinds = jnp.where(places == 0, 0, jnp.where(places == 1, 1, kinds))
    return kinds.astype(jnp.int32).reshape(TOKENS)


def place_ends(values, rng, low, high):
    shape = values.shape
    index_at = [jax.random.randint(jax.random.fold_in(rng, axis), (), 0, shape[axis]) for axis in range(len(shape))]
    values = values.at[tuple(index_at)].set(low)
    longest = shape.index(max(shape))
    index_at[longest] = (index_at[longest] + 1) % shape[longest]
    return values.at[tuple(index_at)].set(high)


def level_of(own_key, dims, pieces, low, top_value):
    def one(position, parts):
        steps = jax.random.uniform(jax.random.fold_in(jax.random.fold_in(own_key, 6), position), (parts,), jnp.float32, low / len(pieces), top_value / len(pieces))
        return jnp.repeat(jnp.exp(steps), dims[position] // parts).reshape((-1,) + (1,) * (len(dims) - position - 1))

    level = one(*pieces[0])
    for cut in pieces[1:]:
        level = level * one(*cut)
    return level


def bell_draw(own_key, dims, scale, limit, cuts=(), kind=jnp.bfloat16):
    values = scale * jax.random.normal(own_key, dims, jnp.float32)
    if cuts:
        values = values * level_of(own_key, dims, cuts, -0.22, 0.18)
    return jnp.clip(values, -limit, limit).astype(kind)


def setup_inputs(seed: int = 0) -> dict:
    streams_of = jax.random.split(jax.random.key(seed), 18)
    text_embed = bell_draw(streams_of[0], (TOKENS, D), 1.0, 6.0, ((0, 32),))
    vision_embed = bell_draw(streams_of[1], (TOKENS, D), 1.0, 6.0, ((0, 32),))
    region_mask = draw_region_mask(jax.random.fold_in(streams_of[17], 71), 0)
    modality = draw_modality(jax.random.fold_in(streams_of[17], 71), 0)
    doc_split = place_ends(jax.random.randint(streams_of[4], (GROUPS,), 0, 2), jax.random.fold_in(streams_of[4], 1), 0, 1).astype(jnp.int32)
    norm_gain = jnp.clip(1.0 + 0.1 * jax.random.normal(streams_of[5], (LAYERS, 2, D), jnp.float32), 0.5, 1.5)
    norm_bias = bell_draw(streams_of[6], (LAYERS, 2, D), 0.3, 4.0, (), jnp.float32)
    qkv_weight = bell_draw(streams_of[7], (LAYERS, 3, D, D), D ** -0.5, 0.21875, ((3, 4),))
    qv_bias = bell_draw(streams_of[8], (LAYERS, 2, D), 0.3, 4.0, ((2, 4),), jnp.float32)
    out_weight = bell_draw(streams_of[9], (LAYERS, D, D), (D // 32) ** -0.5, 1.25, ((1, 4),))
    out_bias = bell_draw(streams_of[10], (LAYERS, D), 0.3, 4.0, (), jnp.float32)
    gates = bell_draw(streams_of[11], (LAYERS, 4, D), 1.5, 6.0, (), jnp.float32)
    up_weight = bell_draw(streams_of[12], (LAYERS, D, FF), D ** -0.5, 0.21875, ((2, 4),))
    up_bias = bell_draw(streams_of[13], (LAYERS, FF), 0.5, 6.0, ((1, 4),), jnp.float32)
    down_weight = bell_draw(streams_of[14], (LAYERS, FF, D), FF ** -0.5, 0.109375, ((1, 4),))
    down_bias = bell_draw(streams_of[15], (LAYERS, D), 0.3, 4.0, (), jnp.float32)
    cotangent = bell_draw(streams_of[16], (TOKENS, D), 1.0, 6.0, ((0, 32),))
    return {"text_embed": text_embed, "vision_embed": vision_embed, "region_mask": region_mask, "modality": modality, "doc_split": doc_split, "norm_gain": norm_gain, "norm_bias": norm_bias, "qkv_weight": qkv_weight, "qv_bias": qv_bias, "out_weight": out_weight, "out_bias": out_bias, "gates": gates, "up_weight": up_weight, "up_bias": up_bias, "down_weight": down_weight, "down_bias": down_bias, "cotangent": cotangent}


epsilon = 1e-05
far_value = -1000000000.0
highest = lax.Precision.HIGHEST

@jax.custom_vjp
def low(v):
    return lax.optimization_barrier(v.astype(jnp.bfloat16)).astype(jnp.float32)

@jax.custom_vjp
def low_back(v):
    return v

def low_keep(v):
    return (low(v), None)

def low_pass(kept, grad):
    return (grad,)

def back_keep(v):
    return (v, None)

def back_low(kept, grad):
    return (low(grad),)
low.defvjp(low_keep, low_pass)
low_back.defvjp(back_keep, back_low)

def layer_norm(values, gain, shift):
    center = values - lax.optimization_barrier(jnp.mean(values, axis=-1, keepdims=True))
    spread = lax.optimization_barrier(jnp.mean(center * center, axis=-1, keepdims=True))
    return center * lax.rsqrt(spread + epsilon) * gain + shift

def logistic(values):
    return 1.0 / (1.0 + jnp.exp(-values))

def gelu_exact(values):
    return 0.5 * values * (1.0 + lax.erf(values * 0.7071067811865476))

def build_masks(region_mask, modality, doc_split):
    groups = doc_split.shape[0]
    places = jnp.arange(SLOTS, dtype=jnp.int32) // (SLOTS // 2)
    documents = doc_split[:, None] * places[None, :]
    same_doc = documents[:, :, None] == documents[:, None, :]
    real_keys = (region_mask.reshape(groups, SLOTS) == 1)[:, None, :]
    kinds = modality.reshape(groups, SLOTS)
    crossing = kinds[:, :, None] != kinds[:, None, :]
    within = jnp.logical_and(same_doc, real_keys)
    return (jnp.logical_and(within, crossing), within)

def grouped_copies(values):
    return low_back(jnp.broadcast_to(values[None], (N_TENSOR,) + values.shape))

def attend(query, keys, values, allowed):
    groups = allowed.shape[0]
    shape = (groups, SLOTS, HEADS, HEAD_DIM)
    raw = jnp.einsum('gqhd,gkhd->ghqk', query.reshape(shape), keys.reshape(shape), precision=highest) * HEAD_DIM ** (-0.5)
    scores = jnp.where(allowed[:, None], low_back(raw), far_value)
    top_score = lax.optimization_barrier(jnp.max(scores, axis=-1, keepdims=True))
    exponent = jnp.exp(scores - top_score)
    probs = low(exponent / lax.optimization_barrier(jnp.sum(exponent, axis=-1, keepdims=True)))
    mixed = jnp.einsum('ghqk,gkhd->gqhd', probs, values.reshape(shape), precision=highest)
    return mixed.reshape(groups * SLOTS, HEADS * HEAD_DIM)

def residual_block(state, is_text, allowed, layer, params):
    gains, shifts, qkv, qv_shift, w_out, out_shift, gate_table, w_up, up_shift, w_down, down_shift = params
    nrows = state.shape[0]
    part = D // N_TENSOR
    part_ff = FF // N_TENSOR
    normed = low(layer_norm(state, gains[layer, 0], shifts[layer, 0]))
    copies = grouped_copies(normed)
    projected = jnp.einsum('gtd,cdge->ctge', copies, qkv[layer].reshape(3, D, N_TENSOR, part), precision=highest).reshape(3, nrows, D)
    query = low(low_back(projected[0] + qv_shift[layer, 0]))
    keys = low(low_back(projected[1]))
    values = low(low_back(projected[2] + qv_shift[layer, 1]))
    mixed = low(low_back(attend(query, keys, values, allowed)))
    partial_value = jnp.einsum('tge,ged->gtd', mixed.reshape(nrows, N_TENSOR, part), w_out[layer].reshape(N_TENSOR, part, D), precision=highest)
    attention_out = low_back(lax.optimization_barrier(jnp.sum(low(partial_value), axis=0)) + out_shift[layer])
    gate_attn = logistic(jnp.where(is_text, gate_table[layer, 0], gate_table[layer, 1]))
    middle = state + gate_attn * attention_out
    normed_ff = low(layer_norm(middle, gains[layer, 1], shifts[layer, 1]))
    copies_ff = grouped_copies(normed_ff)
    pre = jnp.einsum('gtd,dgf->tgf', copies_ff, w_up[layer].reshape(D, N_TENSOR, part_ff), precision=highest).reshape(nrows, FF)
    hidden_pre = low_back(pre + up_shift[layer])
    hidden = low(low_back(gelu_exact(hidden_pre)))
    partial_ff = jnp.einsum('tgf,gfe->gte', hidden.reshape(nrows, N_TENSOR, part_ff), w_down[layer].reshape(N_TENSOR, part_ff, D), precision=highest)
    feed_out = low_back(lax.optimization_barrier(jnp.sum(low(partial_ff), axis=0)) + down_shift[layer])
    gate_ff = logistic(jnp.where(is_text, gate_table[layer, 2], gate_table[layer, 3]))
    return middle + gate_ff * feed_out

def reference(text_embed, vision_embed, region_mask, modality, doc_split, norm_gain, norm_bias, qkv_weight, qv_bias, out_weight, out_bias, gates, up_weight, up_bias, down_weight, down_bias, cotangent):
    params = tuple((entry.astype(jnp.float32) for entry in (norm_gain, norm_bias, qkv_weight, qv_bias, out_weight, out_bias, gates, up_weight, up_bias, down_weight, down_bias)))
    block = math.gcd(TOKENS, 4096)
    blocks = TOKENS // block
    groups = block // SLOTS
    texts = text_embed.astype(jnp.float32).reshape(blocks, block, D)
    visions = vision_embed.astype(jnp.float32).reshape(blocks, block, D)
    reals = region_mask.reshape(blocks, block)
    kinds = modality.reshape(blocks, block)
    splits = doc_split.reshape(blocks, groups)
    upstreams = cotangent.astype(jnp.float32).reshape(blocks, block, D)

    def step(totals, item):
        text_part, vision_part, real_part, kind_part, split_part, upstream = item
        cross_mask, self_mask = build_masks(real_part, kind_part, split_part)
        is_text = (kind_part == 0)[:, None]

        def forward(text_in, vision_in, *weights):
            state = jnp.where(is_text, text_in, vision_in)
            for layer in range(LAYERS):
                allowed = cross_mask if layer % 2 == 0 else self_mask
                state = residual_block(state, is_text, allowed, layer, weights)
            return state
        result, pull = jax.vjp(forward, text_part, vision_part, *params)
        grads = pull(upstream)
        totals = tuple((total + extra for total, extra in zip(totals, grads[2:])))
        return (totals, (result.astype(jnp.bfloat16), grads[0], grads[1]))
    zeros = tuple((jnp.zeros(entry.shape, jnp.float32) for entry in params))
    totals, outputs = lax.scan(step, zeros, (texts, visions, reals, kinds, splits, upstreams))
    joined = outputs[0].reshape(TOKENS, D)
    text_grad = outputs[1].reshape(TOKENS, D)
    vision_grad = outputs[2].reshape(TOKENS, D)
    return (joined, text_grad, vision_grad, totals[0], totals[1], totals[2], totals[3], totals[4], totals[5], totals[6], totals[7], totals[8], totals[9], totals[10])
```

```python
import jax
import jax.numpy as jnp
from jax import lax
from jax.sharding import PartitionSpec as P

HEAD_DIM = 64
LAYERS = 2
SLOTS = 128
SCALE = HEAD_DIM ** (-0.5)

epsilon = 1e-05
far_value = -1000000000.0
bf16 = jnp.bfloat16
f32 = jnp.float32


def logistic(values):
    return 1.0 / (1.0 + jnp.exp(-values))


def gelu_pair(values):
    cdf = 0.5 * (1.0 + lax.erf(values * 0.7071067811865476))
    density = 0.3989422804014327 * jnp.exp(-0.5 * values * values)
    return values * cdf, cdf + values * density


def norm_parts(values):
    center = values - jnp.mean(values, axis=-1, keepdims=True)
    spread = jnp.mean(center * center, axis=-1, keepdims=True)
    scale = lax.rsqrt(spread + epsilon)
    return center * scale, scale


def norm_back(grad, xhat, scale, gain):
    scaled = grad * gain
    inner = jnp.mean(scaled, axis=-1, keepdims=True)
    cross = jnp.mean(scaled * xhat, axis=-1, keepdims=True)
    return (
        scale * (scaled - inner - xhat * cross),
        jnp.sum(grad * xhat, axis=0),
        jnp.sum(grad, axis=0),
    )


def mm(left, right):
    return jnp.dot(left, right, preferred_element_type=f32)


def mm_nt(left, right):
    return lax.dot_general(left, right, (((1,), (1,)), ((), ())), preferred_element_type=f32)


def mm_tn(left, right):
    return lax.dot_general(left, right, (((0,), (0,)), ((), ())), preferred_element_type=f32)


def swap(value, axis, size, bit):
    return lax.ppermute(value, axis, [(i, i ^ bit) for i in range(size)])


def halves(value, upper):
    half = value.shape[0] // 2
    keep = lax.dynamic_slice_in_dim(value, jnp.where(upper, half, 0), half, 0)
    send = lax.dynamic_slice_in_dim(value, jnp.where(upper, 0, half), half, 0)
    return keep, send


def reduce_over(value, axis, size, order):
    me = lax.axis_index(axis)
    current = value
    for bit in order:
        keep, send = halves(current, (me & bit) != 0)
        got = swap(send.astype(bf16), axis, size, bit)
        current = keep.astype(f32) + got.astype(f32)
    current = current.astype(bf16)
    for bit in reversed(order):
        got = swap(current, axis, size, bit)
        upper = (me & bit) != 0
        current = jnp.concatenate(
            [jnp.where(upper, got, current), jnp.where(upper, current, got)], axis=0
        )
    return current.astype(f32)


def body(
    text_embed,
    vision_embed,
    region_mask,
    modality,
    doc_split,
    norm_gain,
    norm_bias,
    qkv_weight,
    qv_bias,
    out_weight,
    out_bias,
    gates,
    up_weight,
    up_bias,
    down_weight,
    down_bias,
    cotangent,
    dp_size,
    tensor_size,
):
    rows, width = text_embed.shape
    here = rows // SLOTS
    quarter = qkv_weight.shape[3]
    hidden_quarter = up_weight.shape[2]
    heads = 2 * quarter // HEAD_DIM
    me = lax.axis_index("tensor")
    across = me ^ 2

    def to_core(value):
        return swap(value, "tensor", tensor_size, 1)

    def to_side(value):
        return swap(value, "tensor", tensor_size, 2)

    def rows_of(array, index):
        return lax.dynamic_slice_in_dim(array, index * rows, rows, 0)

    def masks_of(index):
        kinds = rows_of(modality, index).reshape(here, SLOTS)
        real = rows_of(region_mask, index).reshape(here, SLOTS) == 1
        split = lax.dynamic_slice_in_dim(doc_split, index * here, here, 0)
        places = jnp.arange(SLOTS, dtype=jnp.int32) // (SLOTS // 2)
        documents = split[:, None] * places[None, :]
        within = (documents[:, :, None] == documents[:, None, :]) & real[:, None, :]
        crossing = kinds[:, :, None] != kinds[:, None, :]
        return within & crossing, within

    masks = [masks_of(me), masks_of(across)]
    is_text = (rows_of(modality, me) == 0)[:, None]

    full = []
    for layer in range(LAYERS):
        qkv = jnp.concatenate([qkv_weight[layer], to_core(qkv_weight[layer])], axis=2)
        qv = jnp.concatenate([qv_bias[layer], to_core(qv_bias[layer])], axis=1)
        out = jnp.concatenate([out_weight[layer], to_core(out_weight[layer])], axis=0)
        up = jnp.concatenate([up_weight[layer], to_core(up_weight[layer])], axis=1)
        shift = jnp.concatenate([up_bias[layer], to_core(up_bias[layer])], axis=0)
        down = jnp.concatenate([down_weight[layer], to_core(down_weight[layer])], axis=0)
        full.append((qkv, qv, out, up, shift, down))

    def heads_of(value):
        return value.reshape(here, SLOTS, heads, HEAD_DIM)

    def attend(normed, layer, allowed):
        qkv, qv, out, _, _, _ = full[layer]
        query = (mm(normed, qkv[0]) + qv[0]).astype(bf16)
        keys = mm(normed, qkv[1]).astype(bf16)
        values = (mm(normed, qkv[2]) + qv[1]).astype(bf16)
        raw = jnp.einsum(
            "gqhd,gkhd->ghqk", heads_of(query), heads_of(keys), preferred_element_type=f32
        )
        scores = jnp.where(allowed[:, None], raw * SCALE, far_value)
        exponent = jnp.exp(scores - jnp.max(scores, axis=-1, keepdims=True))
        probs = (exponent / jnp.sum(exponent, axis=-1, keepdims=True)).astype(bf16)
        mixed = jnp.einsum(
            "ghqk,gkhd->gqhd", probs, heads_of(values), preferred_element_type=f32
        )
        mixed = mixed.reshape(rows, heads * HEAD_DIM).astype(bf16)
        return (query, keys, values, probs, mixed), mm(mixed, out)

    def attend_back(grad, layer, kept):
        query, keys, values, probs, mixed = kept
        out = full[layer][2]
        mixed_grad = heads_of(mm_nt(grad, out).astype(bf16))
        value_grad = jnp.einsum("ghqk,gqhd->gkhd", probs, mixed_grad, preferred_element_type=f32)
        prob_grad = jnp.einsum(
            "gqhd,gkhd->ghqk", mixed_grad, heads_of(values), preferred_element_type=f32
        )
        weights = probs.astype(f32)
        score_grad = (
            weights * (prob_grad - jnp.sum(weights * prob_grad, axis=-1, keepdims=True))
        ).astype(bf16)
        query_grad = SCALE * jnp.einsum(
            "ghqk,gkhd->gqhd", score_grad, heads_of(keys), preferred_element_type=f32
        )
        key_grad = SCALE * jnp.einsum(
            "ghqk,gqhd->gkhd", score_grad, heads_of(query), preferred_element_type=f32
        )
        return [
            value.reshape(rows, heads * HEAD_DIM).astype(bf16)
            for value in (query_grad, key_grad, value_grad)
        ]

    def attend_input(parts, layer):
        qkv = full[layer][0]
        return mm_nt(parts[0], qkv[0]) + mm_nt(parts[1], qkv[1]) + mm_nt(parts[2], qkv[2])

    state = jnp.where(is_text, text_embed, vision_embed).astype(f32)
    saved = []
    for layer in range(LAYERS):
        _, _, _, up, shift, down = full[layer]
        xhat, scale = norm_parts(state)
        normed = (xhat * norm_gain[layer, 0] + norm_bias[layer, 0]).astype(bf16)
        inputs = [normed, to_side(normed)]
        kept_far, far = attend(inputs[1], layer, masks[1][layer % 2])
        kept_near, near = attend(inputs[0], layer, masks[0][layer % 2])
        attention_out = near + to_side(far.astype(bf16)).astype(f32) + out_bias[layer]
        gate_attn = logistic(jnp.where(is_text, gates[layer, 0], gates[layer, 1]))
        middle = state + gate_attn * attention_out
        xhat_ff, scale_ff = norm_parts(middle)
        normed_ff = (xhat_ff * norm_gain[layer, 1] + norm_bias[layer, 1]).astype(bf16)
        inputs_ff = [normed_ff, to_side(normed_ff)]
        hidden, slope, totals = [], [], []
        for value in inputs_ff:
            act, deriv = gelu_pair(mm(value, up) + shift)
            hidden.append(act.astype(bf16))
            slope.append(deriv.astype(bf16))
            totals.append(mm(hidden[-1], down))
        feed_out = totals[0] + to_side(totals[1].astype(bf16)).astype(f32) + down_bias[layer]
        gate_ff = logistic(jnp.where(is_text, gates[layer, 2], gates[layer, 3]))
        saved.append(
            (
                state,
                middle,
                attention_out,
                gate_attn,
                feed_out,
                gate_ff,
                inputs,
                inputs_ff,
                (kept_near, kept_far),
                hidden,
                slope,
            )
        )
        state = middle + gate_ff * feed_out
    joined = state.astype(bf16)

    def reduce_weights(mine, other, order):
        total = mine + to_core(other.astype(bf16)).astype(f32)
        return reduce_over(total, "dp", dp_size, order)

    bits = [1 << b for b in range(dp_size.bit_length() - 1)]
    late = bits[1:] + bits[:1]
    upstream = cotangent.astype(f32)
    weight_grads = [None] * LAYERS
    shared = [None] * LAYERS
    owned = [None] * LAYERS
    for layer in reversed(range(LAYERS)):
        (
            state_in,
            middle,
            attention_out,
            gate_attn,
            feed_out,
            gate_ff,
            inputs,
            inputs_ff,
            kept,
            hidden,
            slope,
        ) = saved[layer]
        _, _, _, up, shift, down = full[layer]
        feed_grad = upstream * gate_ff
        feed_gate = feed_grad * feed_out * (1.0 - gate_ff)
        feed_low = feed_grad.astype(bf16)
        grads_ff = [feed_low, to_side(feed_low)]
        down_shift_grad = jnp.sum(feed_low.astype(f32), axis=0)
        pre_grads, totals = [], []
        for value, deriv in zip(grads_ff, slope):
            back = mm_nt(value, down).astype(bf16).astype(f32)
            pre_grads.append((back * deriv.astype(f32)).astype(bf16))
            totals.append(mm_nt(pre_grads[-1], up))
        normed_ff_grad = totals[0] + to_side(totals[1].astype(bf16)).astype(f32)
        down_grad = mm_tn(hidden[0], grads_ff[0]) + mm_tn(hidden[1], grads_ff[1])
        up_grad = mm_tn(inputs_ff[0], pre_grads[0]) + mm_tn(inputs_ff[1], pre_grads[1])
        up_shift_grad = sum(jnp.sum(value.astype(f32), axis=0) for value in pre_grads)
        hq = hidden_quarter
        down_total = reduce_weights(down_grad[:hq], down_grad[hq:], bits)
        up_total = reduce_weights(up_grad[:, :hq], up_grad[:, hq:], bits if layer else late)
        xhat_ff, scale_ff = norm_parts(middle)
        middle_grad, gain_ff_grad, shift_ff_grad = norm_back(
            normed_ff_grad, xhat_ff, scale_ff, norm_gain[layer, 1]
        )
        middle_grad = middle_grad + upstream
        branch_grad = middle_grad * gate_attn
        attn_gate = branch_grad * attention_out * (1.0 - gate_attn)
        branch_low = branch_grad.astype(bf16)
        grads_attn = [branch_low, to_side(branch_low)]
        out_shift_grad = jnp.sum(branch_low.astype(f32), axis=0)
        parts_far = attend_back(grads_attn[1], layer, kept[1])
        far = attend_input(parts_far, layer)
        parts_near = attend_back(grads_attn[0], layer, kept[0])
        near = attend_input(parts_near, layer)
        normed_grad = near + to_side(far.astype(bf16)).astype(f32)
        out_grad = mm_tn(kept[0][4], grads_attn[0]) + mm_tn(kept[1][4], grads_attn[1])
        qkv_grads = [
            mm_tn(part_near, inputs[0]) + mm_tn(part_far, inputs[1])
            for part_near, part_far in zip(parts_near, parts_far)
        ]
        q = quarter
        pieces = qkv_grads + [out_grad]
        attn_total = reduce_weights(
            jnp.concatenate([piece[:q] for piece in pieces], axis=0),
            jnp.concatenate([piece[q:] for piece in pieces], axis=0),
            bits,
        )
        qv_shift_grad = jnp.stack(
            [
                jnp.sum(parts_near[i].astype(f32), axis=0) + jnp.sum(parts_far[i].astype(f32), axis=0)
                for i in (0, 2)
            ]
        )
        xhat, scale = norm_parts(state_in)
        state_grad, gain_attn_grad, shift_attn_grad = norm_back(
            normed_grad, xhat, scale, norm_gain[layer, 0]
        )
        upstream = state_grad + middle_grad
        shared[layer] = jnp.stack(
            [
                gain_attn_grad,
                gain_ff_grad,
                shift_attn_grad,
                shift_ff_grad,
                jnp.sum(jnp.where(is_text, attn_gate, 0.0), axis=0),
                jnp.sum(jnp.where(is_text, 0.0, attn_gate), axis=0),
                jnp.sum(jnp.where(is_text, feed_gate, 0.0), axis=0),
                jnp.sum(jnp.where(is_text, 0.0, feed_gate), axis=0),
                out_shift_grad,
                down_shift_grad,
            ]
        )
        owned[layer] = [
            jnp.concatenate([up_shift_grad[s * hq : (s + 1) * hq], qv_shift_grad[:, s * q : (s + 1) * q].reshape(-1)])
            for s in range(2)
        ]
        weight_grads[layer] = (attn_total, up_total, down_total)
    small = jnp.stack(shared).reshape(LAYERS * 10, width)
    mine = jnp.stack([entry[0] for entry in owned])
    other = jnp.stack([entry[1] for entry in owned])
    small = small + to_core(small)
    mine = mine + to_core(other)
    small = small + to_side(small)
    for bit in bits:
        small = small + swap(small, "dp", dp_size, bit)
        mine = mine + swap(mine, "dp", dp_size, bit)
    small = small.reshape(LAYERS, 10, width)
    q = quarter
    attn_all = jnp.stack([entry[0] for entry in weight_grads])
    qkv_all = attn_all[:, : 3 * q].reshape(LAYERS, 3, q, width).transpose(0, 1, 3, 2)
    return (
        joined,
        jnp.where(is_text, upstream, 0.0),
        jnp.where(is_text, 0.0, upstream),
        small[:, 0:2],
        small[:, 2:4],
        qkv_all,
        mine[:, hidden_quarter:].reshape(LAYERS, 2, q),
        attn_all[:, 3 * q :],
        small[:, 8],
        small[:, 4:8],
        jnp.stack([entry[1] for entry in weight_grads]),
        mine[:, :hidden_quarter],
        jnp.stack([entry[2] for entry in weight_grads]),
        small[:, 9],
    )


def solution(mesh):
    sizes = dict(mesh.shape)

    def run(*arrays):
        return body(*arrays, dp_size=sizes["dp"], tensor_size=sizes["tensor"])

    placed = (
        P(("dp", "tensor"), None),
        P(("dp", "tensor"), None),
        P("dp"),
        P("dp"),
        P("dp"),
        P(),
        P(),
        P(None, None, None, "tensor"),
        P(None, None, "tensor"),
        P(None, "tensor", None),
        P(),
        P(),
        P(None, None, "tensor"),
        P(None, "tensor"),
        P(None, "tensor", None),
        P(),
        P(("dp", "tensor"), None),
    )
    return jax.shard_map(
        run,
        mesh=mesh,
        in_specs=placed,
        out_specs=(
            P(("dp", "tensor"), None),
            P(("dp", "tensor"), None),
            P(("dp", "tensor"), None),
            P(),
            P(),
            P(None, None, None, "tensor"),
            P(None, None, "tensor"),
            P(None, "tensor", None),
            P(),
            P(),
            P(None, None, "tensor"),
            P(None, "tensor"),
            P(None, "tensor", None),
            P(),
        ),
        check_vma=False,
    )
```

```python
import functools

import jax
import jax.numpy as jnp
from jax import lax
from jax.experimental import pallas as pl
from jax.experimental.pallas import tpu as pltpu
from jax.sharding import PartitionSpec as P

HEAD_DIM = 64
LAYERS = 2
SLOTS = 128
SCALE = HEAD_DIM ** (-0.5)
PAIR = 2 * HEAD_DIM

epsilon = 1e-05
far_value = -1000000000.0
bf16 = jnp.bfloat16
f32 = jnp.float32


def logistic(values):
    return 1.0 / (1.0 + jnp.exp(-values))


def gelu_pair(values):
    size = jnp.abs(values)
    base = 1.0 + 0.23164189 * size
    t = pl.reciprocal(base, approx=True)
    t = t * (2.0 - base * t)
    bell = jnp.exp(-0.5 * (values * values))
    series = 0.5307027145 * t - 0.7265760135
    series = series * t + 0.7107068705
    series = series * t - 0.142248368
    series = series * t + 0.127414796
    tail = series * t * bell
    cdf = jnp.where(values < 0.0, tail, 1.0 - tail)
    return values * cdf, cdf + 0.3989422804014327 * (values * bell)


def norm_parts(values):
    center = values - jnp.mean(values, axis=-1, keepdims=True)
    spread = jnp.mean(center * center, axis=-1, keepdims=True)
    scale = lax.rsqrt(spread + epsilon)
    return center * scale, scale


def norm_back(grad, xhat, scale, gain):
    scaled = grad * gain
    inner = jnp.mean(scaled, axis=-1, keepdims=True)
    cross = jnp.mean(scaled * xhat, axis=-1, keepdims=True)
    return scale * (scaled - inner - xhat * cross)


def column(values):
    return jnp.sum(values, axis=0, keepdims=True)


def mm(left, right):
    return jnp.dot(left, right, preferred_element_type=f32)


def mm_nt(left, right):
    return lax.dot_general(left, right, (((1,), (1,)), ((), ())), preferred_element_type=f32)


def mm_tn(left, right):
    return lax.dot_general(left, right, (((0,), (0,)), ((), ())), preferred_element_type=f32)


def shape(dims, kind):
    return jax.ShapeDtypeStruct(dims, kind)


def call(kernel, outs, args, flops=0, traffic=1 << 20, scalars=0, scratch=(), room=20, home=False):
    keep = lambda entry: pltpu.VMEM(entry.shape, entry.dtype) if home else entry
    outs = [keep(entry) for entry in outs] if isinstance(outs, list) else keep(outs)
    args = [
        entry
        for i, entry in enumerate(args)
    ]
    return pl.pallas_call(
        kernel,
        out_shape=outs,
        in_specs=[SCALARS] * scalars + [WHOLE] * (len(args) - scalars),
        scratch_shapes=scratch,
        compiler_params=pltpu.CompilerParams(vmem_limit_bytes=room << 20),
        cost_estimate=pl.CostEstimate(flops=flops, bytes_accessed=traffic, transcendentals=0),
    )(*args)


SCALARS = pl.BlockSpec(memory_space=pltpu.SMEM)
WHOLE = pl.BlockSpec(memory_space=pltpu.VMEM)


def as_column(row):
    across = lax.broadcasted_iota(jnp.int32, (SLOTS, SLOTS), 1)
    down = lax.broadcasted_iota(jnp.int32, (SLOTS, SLOTS), 0)
    return jnp.sum(jnp.where(across == down, row, 0.0), axis=1, keepdims=True)


def gate_of(gates, layer, index, vision):
    return jnp.where(
        vision, logistic(gates[layer, index + 1 : index + 2]), logistic(gates[layer, index : index + 1])
    )


def start_kernel(place, kinds, text, vision, gain, shift, state_out, normed_out, kind_out, *, here):
    for g in range(here):
        span = slice(g * SLOTS, (g + 1) * SLOTS)
        kind = as_column(kinds[pl.ds(place[0] * here + g, 1), :].astype(f32))
        kind_out[span, :] = kind
        state = jnp.where(kind > 0.5, vision[span, :].astype(f32), text[span, :].astype(f32))
        state_out[span, :] = state
        xhat, _ = norm_parts(state)
        normed_out[span, :] = (xhat * gain[0, 0:1] + shift[0, 0:1]).astype(bf16)


def mask_kernel(place, splits, kinds, reals, cotangent, kind, gates, near_cross, near_self, far_cross, far_self, feed_out, *, here, layer):
    across = lax.broadcasted_iota(jnp.int32, (SLOTS, SLOTS), 1) // (SLOTS // 2)
    down = lax.broadcasted_iota(jnp.int32, (SLOTS, SLOTS), 0) // (SLOTS // 2)
    block = jnp.where(across == down, 1.0, 0.0)
    for side, (cross_out, self_out) in enumerate(((near_cross, near_self), (far_cross, far_self))):
        for g in range(here):
            index = place[side] * here + g
            row = kinds[pl.ds(index, 1), :].astype(f32)
            real = reals[pl.ds(index, 1), :].astype(f32)
            split = (splits[index] != 0).astype(f32)
            within = jnp.maximum(block, 1.0 - split) * jnp.where(real == 1.0, 1.0, 0.0)
            self_out[g] = within
            cross_out[g] = jnp.where(as_column(row) != row, within, 0.0)
    gate = gate_of(gates, layer, 2, kind[...] > 0.5)
    feed_out[...] = (cotangent[...].astype(f32) * gate).astype(bf16)


def mid_kernel(state, near, far, bias, gates, kind, gain, shift, state_out, normed_out, *, layer, branch):
    total = near[...].astype(f32) + far[...].astype(f32) + bias[layer : layer + 1]
    gate = gate_of(gates, layer, 2 * branch, kind[...] > 0.5)
    value = state[...] + gate * total
    state_out[...] = value
    xhat, _ = norm_parts(value)
    nl, ni = (layer, 1) if branch == 0 else (layer + 1, 0)
    normed_out[...] = (xhat * gain[nl, ni : ni + 1] + shift[nl, ni : ni + 1]).astype(bf16)


def gate_sums(grad, total, gate, vision):
    full = grad * total * (1.0 - gate)
    return [column(jnp.where(vision, 0.0, full)), column(jnp.where(vision, full, 0.0))]


def put_rows(out, rows):
    rows = rows + [jnp.zeros_like(rows[0])] * (8 - len(rows))
    for i, row in enumerate(rows):
        out[i : i + 1, :] = row


def last_kernel(state, near, far, bias, gates, kind, cotangent, joined_out, sums_out, *, layer):
    total = near[...].astype(f32) + far[...].astype(f32) + bias[layer : layer + 1]
    vision = kind[...] > 0.5
    gate = gate_of(gates, layer, 2, vision)
    joined_out[...] = (state[...] + gate * total).astype(bf16)
    grad = cotangent[...].astype(f32) * gate
    sums = gate_sums(grad, total, gate, vision)
    put_rows(sums_out, sums + [column(grad.astype(bf16).astype(f32))])


def back_mid_kernel(near, far, middle, upstream, kind, gates, gain, attn_near, attn_far, bias, grad_out, low_out, sums_out, *, layer):
    grad = near[...].astype(f32) + far[...].astype(f32)
    xhat, scale = norm_parts(middle[...])
    total = norm_back(grad, xhat, scale, gain[layer, 1:2]) + upstream[...].astype(f32)
    grad_out[...] = total
    vision = kind[...] > 0.5
    gate = gate_of(gates, layer, 0, vision)
    branch = total * gate
    low = branch.astype(bf16)
    low_out[...] = low
    attn = attn_near[...].astype(f32) + attn_far[...].astype(f32) + bias[layer : layer + 1]
    put_rows(
        sums_out,
        [column(grad * xhat), column(grad)]
        + gate_sums(branch, attn, gate, vision)
        + [column(low.astype(f32))],
    )


def back_end_kernel(near, far, state, middle_grad, kind, gates, gain, feed_near, feed_far, bias, grad_out, low_out, sums_out, *, layer):
    grad = near[...].astype(f32) + far[...].astype(f32)
    xhat, scale = norm_parts(state[...])
    total = norm_back(grad, xhat, scale, gain[layer, 0:1]) + middle_grad[...]
    grad_out[...] = total
    vision = kind[...] > 0.5
    below = layer - 1
    gate = gate_of(gates, below, 2, vision)
    branch = total * gate
    low = branch.astype(bf16)
    low_out[...] = low
    feed = feed_near[...].astype(f32) + feed_far[...].astype(f32) + bias[below : below + 1]
    put_rows(
        sums_out,
        [column(grad * xhat), column(grad)]
        + gate_sums(branch, feed, gate, vision)
        + [column(low.astype(f32))],
    )


def finish_kernel(near, far, state, middle_grad, kind, gain, text_out, vision_out, sums_out):
    grad = near[...].astype(f32) + far[...].astype(f32)
    xhat, scale = norm_parts(state[...])
    total = norm_back(grad, xhat, scale, gain[0, 0:1]) + middle_grad[...]
    vision = kind[...] > 0.5
    text_out[...] = jnp.where(vision, 0.0, total)
    vision_out[...] = jnp.where(vision, total, 0.0)
    put_rows(sums_out, [column(grad * xhat), column(grad)])


def head_masks():
    lane = lax.broadcasted_iota(jnp.int32, (1, PAIR), 1)
    low = (lane < HEAD_DIM).astype(f32)
    return low.astype(bf16), (1.0 - low).astype(bf16)


def doubled(value, masks):
    return jnp.concatenate([value * masks[0], value * masks[1]], axis=0)


def join_kernel(qkv_mine, qkv_other, out_mine, out_other, qkv, out, *, layer, quarter):
    rest = quarter - PAIR
    sources = [(qkv_mine[layer, i], qkv_other[i], qkv, 2 * quarter * i) for i in range(3)]
    sources.append((out_mine[layer], out_other[layer], out, 0))
    for mine, other, joined, base in sources:
        joined[base : base + PAIR, :] = mine[:PAIR]
        joined[base + PAIR : base + 2 * PAIR, :] = other[:PAIR]
        joined[base + 2 * PAIR : base + 2 * PAIR + rest, :] = mine[PAIR:]
        joined[base + 2 * PAIR + rest : base + 2 * quarter, :] = other[PAIR:]


def attn_kernel(normed, qkv, shifts, out, allowed, qkv_out, probs_out, mixed_out, total_out, *, here, pairs):
    wide = pairs * PAIR
    projected = mm_nt(normed[...], qkv[...])
    qkv_out[:, :wide] = (projected[:, :wide] + shifts[0:1]).astype(bf16)
    qkv_out[:, wide : 2 * wide] = projected[:, wide : 2 * wide].astype(bf16)
    qkv_out[:, 2 * wide :] = (projected[:, 2 * wide :] + shifts[1:2]).astype(bf16)
    masks = head_masks()
    for g in range(here):
        rows = slice(g * SLOTS, (g + 1) * SLOTS)
        open_here = allowed[g] > 0.5
        for p in range(pairs):
            q, k, v = [qkv_out[rows, i * wide + p * PAIR : i * wide + (p + 1) * PAIR] for i in range(3)]
            raw = mm_nt(q, doubled(k, masks))
            parts = []
            for h in range(2):
                scores = jnp.where(open_here, raw[:, h * SLOTS : (h + 1) * SLOTS] * SCALE, far_value)
                exponent = jnp.exp(scores - jnp.max(scores, axis=-1, keepdims=True))
                inverse = 1.0 / jnp.sum(exponent, axis=-1, keepdims=True)
                parts.append((exponent * inverse).astype(bf16))
            probs = jnp.concatenate(parts, axis=1)
            probs_out[g, p] = probs
            mixed_out[rows, p * PAIR : (p + 1) * PAIR] = mm(probs, doubled(v, masks)).astype(bf16)
    total_out[...] = mm(mixed_out[...], out[...]).astype(bf16)


def attn_back_kernel(grad, qkv, out, qkv_in, probs_in, grads_out, total_out, mixed_grad, *, here, pairs):
    wide = pairs * PAIR
    mixed_grad[...] = mm_nt(grad[...], out[...]).astype(bf16)
    masks = head_masks()
    low_lanes = lax.broadcasted_iota(jnp.int32, (SLOTS, PAIR), 1) < HEAD_DIM
    for g in range(here):
        rows = slice(g * SLOTS, (g + 1) * SLOTS)
        for p in range(pairs):
            spans = [slice(i * wide + p * PAIR, i * wide + (p + 1) * PAIR) for i in range(3)]
            q, k, v = [qkv_in[rows, span] for span in spans]
            probs = probs_in[g, p]
            back = mixed_grad[rows, spans[0]]
            both = mm_tn(probs, back)
            grads_out[rows, spans[2]] = jnp.where(low_lanes, both[:SLOTS], both[SLOTS:]).astype(bf16)
            prob_grad = mm_nt(back, doubled(v, masks))
            weights = probs.astype(f32)
            product = weights * prob_grad
            parts = []
            for h in range(2):
                span = slice(h * SLOTS, (h + 1) * SLOTS)
                total = jnp.sum(product[:, span], axis=-1, keepdims=True)
                parts.append((product[:, span] - weights[:, span] * total).astype(bf16))
            score_grad = jnp.concatenate(parts, axis=1)
            grads_out[rows, spans[0]] = (SCALE * mm(score_grad, doubled(k, masks))).astype(bf16)
            both = SCALE * mm_tn(score_grad, q)
            grads_out[rows, spans[1]] = jnp.where(low_lanes, both[:SLOTS], both[SLOTS:]).astype(bf16)
    total_out[...] = mm(grads_out[...], qkv[...]).astype(bf16)


def attn_weights_kernel(normed_n, normed_f, grad_n, grad_f, mixed_n, mixed_f, dqkv_n, dqkv_f, mine_out, other_out, shifts_out, *, quarter):
    rest = quarter - PAIR
    wide = 2 * quarter
    for i in range(4):
        if i < 3:
            span = slice(i * wide, (i + 1) * wide)
            total = mm_tn(dqkv_n[:, span], normed_n[...]) + mm_tn(dqkv_f[:, span], normed_f[...])
        else:
            total = mm_tn(mixed_n[...], grad_n[...]) + mm_tn(mixed_f[...], grad_f[...])
        total = total.astype(bf16)
        base = i * quarter
        mine_out[base : base + PAIR, :] = total[:PAIR]
        mine_out[base + PAIR : base + quarter, :] = total[2 * PAIR : 2 * PAIR + rest]
        other_out[base : base + PAIR, :] = total[PAIR : 2 * PAIR]
        other_out[base + PAIR : base + quarter, :] = total[2 * PAIR + rest :]
    for j, i in enumerate((0, 2)):
        span = slice(i * wide, (i + 1) * wide)
        shifts_out[j : j + 1, :] = column(dqkv_n[:, span].astype(f32)) + column(dqkv_f[:, span].astype(f32))


def feed_kernel(normed, up_mine, up_other, shift_mine, shift_other, down_mine, down_other, hidden_out, slope_out, total_out, *, layer):
    hq = up_mine.shape[2]
    total = None
    for i, (up, shift, down) in enumerate(((up_mine, shift_mine, down_mine), (up_other, shift_other, down_other))):
        span = slice(i * hq, (i + 1) * hq)
        act, slope = gelu_pair(mm(normed[...], up[layer]) + shift[layer : layer + 1])
        hidden_out[:, span] = act.astype(bf16)
        slope_out[:, span] = slope.astype(bf16)
        part = mm(hidden_out[:, span], down[layer])
        total = part if total is None else total + part
    total_out[...] = total.astype(bf16)


def feed_back_kernel(grad, slope, up_mine, up_other, down_mine, down_other, pre_out, total_out, *, layer):
    hq = up_mine.shape[2]
    total = None
    for i, (up, down) in enumerate(((up_mine, down_mine), (up_other, down_other))):
        span = slice(i * hq, (i + 1) * hq)
        back = mm_nt(grad[...], down[layer]).astype(bf16).astype(f32)
        pre_out[:, span] = (back * slope[:, span].astype(f32)).astype(bf16)
        part = mm_nt(pre_out[:, span], up[layer])
        total = part if total is None else total + part
    total_out[...] = total.astype(bf16)


def feed_weights_kernel(hidden_n, hidden_f, grad_n, grad_f, normed_n, normed_f, pre_n, pre_f, down_mine, down_other, up_mine, up_other, shifts_out):
    hq = down_mine.shape[0]
    for i, (down, up) in enumerate(((down_mine, up_mine), (down_other, up_other))):
        span = slice(i * hq, (i + 1) * hq)
        down[...] = (mm_tn(hidden_n[:, span], grad_n[...]) + mm_tn(hidden_f[:, span], grad_f[...])).astype(bf16)
        up[...] = (mm_tn(normed_n[...], pre_n[:, span]) + mm_tn(normed_f[...], pre_f[:, span])).astype(bf16)
    shifts_out[...] = column(pre_n[...].astype(f32)) + column(pre_f[...].astype(f32))


def swap(value, axis, size, bit):
    return lax.ppermute(value, axis, [(i, i ^ bit) for i in range(size)])


def add_split_kernel(place, left, right, keep_out, send_out, *, half):
    total = lambda start: left[pl.ds(start, half), :].astype(f32) + right[pl.ds(start, half), :].astype(f32)
    keep_out[...] = total(pl.multiple_of(place[0] * half, 16)).astype(bf16)
    send_out[...] = total(pl.multiple_of((1 - place[0]) * half, 16)).astype(bf16)


def add_kernel(left, right, total_out):
    total_out[...] = (left[...].astype(f32) + right[...].astype(f32)).astype(bf16)


def join_rows_kernel(upper, lower, out):
    out[: upper.shape[0], :] = upper[...]
    out[upper.shape[0] :, :] = lower[...]


def add_split(left, right, upper):
    height, width = left.shape
    part = shape((height // 2, width), bf16)
    return call(
        functools.partial(add_split_kernel, half=height // 2),
        [part, part],
        (upper.astype(jnp.int32).reshape(1), left, right),
        scalars=1,
        traffic=6 * height * width,
    )


def added(left, right):
    return call(add_kernel, shape(left.shape, bf16), (left, right), traffic=6 * left.size)


def join_rows(upper, lower):
    height, width = upper.shape
    return call(join_rows_kernel, shape((2 * height, width), bf16), (upper, lower), traffic=8 * upper.size)


def reduce_over(mine, other, axis, size, order):
    me = lax.axis_index(axis)
    height = mine.shape[0]
    if size != 1 << len(order) or height % (16 * size):
        return [lax.psum(added(mine, other), axis)], [0]
    left, right = mine, other
    for bit in order:
        keep, send = add_split(left, right, (me & bit) != 0)
        left, right = keep, swap(send, axis, size, bit)
    current, masks = added(left, right), [0]
    for i, bit in enumerate(reversed(order)):
        got = swap(current, axis, size, bit)
        masks = masks + [mask ^ bit for mask in masks]
        pieces = [current, got]
        if i + 1 < len(order):
            current = join_rows(current, got)
    starts = []
    for mask in masks:
        start, span = 0, height
        for bit in order:
            span //= 2
            start = start + jnp.where(((me ^ mask) & bit) != 0, span, 0)
        starts.append(start)
    return pieces, starts


def placed_parts(starts, refs, count, total, layer):
    each = total // count
    index = 0
    for ref in refs:
        part = ref.shape[0] // each
        for j in range(each):
            start = pl.multiple_of(starts[layer * total + index], 16)
            yield start, ref[j * part : (j + 1) * part, :]
            index += 1


def square_kernel(starts, *refs, count, total):
    out = refs[-1]
    for layer in range(LAYERS):
        own = refs[layer * count : (layer + 1) * count]
        for start, part in placed_parts(starts, own, count, total, layer):
            out[layer, pl.ds(start, part.shape[0]), :] = part.astype(f32)


def grouped_kernel(starts, *refs, count, total, quarter):
    qkv_out, out_out, whole = refs[-3:]
    for layer in range(LAYERS):
        own = refs[layer * count : (layer + 1) * count]
        for start, part in placed_parts(starts, own, count, total, layer):
            whole[pl.ds(start, part.shape[0]), :] = part.astype(f32)
        for i in range(3):
            qkv_out[layer, i] = whole[i * quarter : (i + 1) * quarter, :]
        out_out[layer] = whole[3 * quarter :, :]


def flat_pieces(entries):
    pieces = [piece for entry in entries for piece in entry[0]]
    starts = jnp.stack([jnp.asarray(start, jnp.int32) for entry in entries for start in entry[1]])
    return starts, pieces, len(entries[0][0]), len(entries[0][1])


def square_output(entries, height, width):
    starts, pieces, count, total = flat_pieces(entries)
    return call(
        functools.partial(square_kernel, count=count, total=total),
        shape((LAYERS, height, width), f32),
        (starts, *pieces),
        scalars=1,
        traffic=12 * height * width,
        room=20,
        home=False,
    )


def grouped_output(entries, quarter, width):
    starts, pieces, count, total = flat_pieces(entries)
    return call(
        functools.partial(grouped_kernel, count=count, total=total, quarter=quarter),
        [shape((LAYERS, 3, quarter, width), f32), shape((LAYERS, quarter, width), f32)],
        (starts, *pieces),
        scalars=1,
        scratch=[pltpu.VMEM((4 * quarter, width), f32)],
        traffic=12 * 4 * quarter * width,
        room=20,
        home=False,
    )


def pack_kernel(*refs, quarter, hq):
    shared_out, mine_out, other_out = refs[-3:]
    rest = quarter - PAIR
    for layer in range(LAYERS):
        end, mid, feed, feed_row, up, qv = refs[layer * 5], refs[layer * 5 + 1], refs[layer * 5 + 2], 2 * (layer == 0), refs[layer * 5 + 3], refs[layer * 5 + 4]
        base = layer * 12
        shared_out[base : base + 1, :] = end[0:1]
        shared_out[base + 1 : base + 2, :] = mid[0:1]
        shared_out[base + 2 : base + 3, :] = end[1:2]
        shared_out[base + 3 : base + 4, :] = mid[1:2]
        shared_out[base + 4 : base + 6, :] = mid[2:4]
        shared_out[base + 6 : base + 8, :] = feed[feed_row : feed_row + 2]
        shared_out[base + 8 : base + 9, :] = mid[4:5]
        shared_out[base + 9 : base + 10, :] = feed[feed_row + 2 : feed_row + 3]
        shared_out[base + 10 : base + 12, :] = jnp.zeros_like(mid[0:2])
        for out, up_start, pair_start, rest_start in (
            (mine_out, 0, 0, 2 * PAIR),
            (other_out, hq, PAIR, 2 * PAIR + rest),
        ):
            base = layer * 4
            out[base : base + 4, :] = jnp.zeros_like(mid[0:4])
            out[base : base + 1, :hq] = up[0:1, up_start : up_start + hq]
            out[base + 1 : base + 3, :PAIR] = qv[0:2, pair_start : pair_start + PAIR]
            out[base + 1 : base + 3, PAIR : PAIR + rest] = qv[0:2, rest_start : rest_start + rest]


def unpack_kernel(total, gain, shift, qv, out, gates, up, down, *, quarter, hq):
    for layer in range(LAYERS):
        base = layer * 12
        gain[layer] = total[base : base + 2, :]
        shift[layer] = total[base + 2 : base + 4, :]
        gates[layer] = total[base + 4 : base + 8, :]
        out[layer : layer + 1, :] = total[base + 8 : base + 9, :]
        down[layer : layer + 1, :] = total[base + 9 : base + 10, :]
        base = LAYERS * 12 + layer * 4
        up[layer : layer + 1, :] = total[base : base + 1, :hq]
        qv[layer] = total[base + 1 : base + 3, :quarter]


def body(
    text_embed,
    vision_embed,
    region_mask,
    modality,
    doc_split,
    norm_gain,
    norm_bias,
    qkv_weight,
    qv_bias,
    out_weight,
    out_bias,
    gates,
    up_weight,
    up_bias,
    down_weight,
    down_bias,
    cotangent,
    dp_size,
    tensor_size,
):
    rows, width = text_embed.shape
    here = rows // SLOTS
    quarter = qkv_weight.shape[3]
    hq = up_weight.shape[2]
    wide = 2 * quarter
    pairs = wide // PAIR
    me = lax.axis_index("tensor")
    place = jnp.stack([me, me ^ 2]).astype(jnp.int32)

    def to_core(value):
        return swap(value, "tensor", tensor_size, 1)

    def to_side(value):
        return swap(value, "tensor", tensor_size, 2)

    kinds = modality.reshape(-1, SLOTS)
    reals = region_mask.reshape(-1, SLOTS)
    row_f32, row_bf16 = shape((rows, width), f32), shape((rows, width), bf16)
    wide_bf16, hidden_bf16 = shape((rows, wide), bf16), shape((rows, 2 * hq), bf16)
    sums = shape((8, width), f32)

    state, normed, kind = call(
        functools.partial(start_kernel, here=here),
        [row_f32, row_bf16, shape((rows, 1), f32)],
        (place, kinds, text_embed, vision_embed, norm_gain, norm_bias),
        scalars=1,
        traffic=3 << 20,
    )
    inputs = [normed, to_side(normed)]

    qkv_weight = jnp.swapaxes(qkv_weight, 2, 3)
    qkv_weight, out_weight, up_weight, down_weight, qv_bias, up_bias, _ = lax.optimization_barrier(
        (qkv_weight, out_weight, up_weight, down_weight, qv_bias, up_bias, normed)
    )
    qkv_other = [to_core(qkv_weight[layer]) for layer in range(LAYERS)]
    out_other, up_other, down_other = to_core(out_weight), to_core(up_weight), to_core(down_weight)
    qv_other, shift_other = to_core(qv_bias), to_core(up_bias)
    qv_all = jnp.concatenate(
        [qv_bias[..., :PAIR], qv_other[..., :PAIR], qv_bias[..., PAIR:], qv_other[..., PAIR:]], axis=-1
    )

    tile = shape((here, SLOTS, SLOTS), f32)
    near_cross, near_self, far_cross, far_self, feed_low = call(
        functools.partial(mask_kernel, here=here, layer=LAYERS - 1),
        [tile, tile, tile, tile, row_bf16],
        (place, doc_split, kinds, reals, cotangent, kind, gates),
        scalars=2,
        traffic=2 << 20,
    )
    masks = [(near_cross, far_cross), (near_self, far_self)]

    joined_weights = [
        call(
            functools.partial(join_kernel, layer=layer, quarter=quarter),
            [shape((3 * wide, width), bf16), shape((wide, width), bf16)],
            (qkv_weight, qkv_other[layer], out_weight, out_other),
            traffic=6 << 20,
        )
        for layer in range(LAYERS)
    ]
    triple = shape((rows, 3 * wide), bf16)

    def attend(value, layer, allowed):
        qkv, out = joined_weights[layer]
        return call(
            functools.partial(attn_kernel, here=here, pairs=pairs),
            [triple, shape((here, pairs, SLOTS, 2 * SLOTS), bf16), wide_bf16, row_bf16],
            (value, qkv, qv_all[layer], out, allowed),
            flops=2 * rows * width * wide * 4 + 4 * rows * SLOTS * wide * 2,
            traffic=5 << 20,
        )

    def attend_back(grad, layer, kept):
        qkv, out = joined_weights[layer]
        return call(
            functools.partial(attn_back_kernel, here=here, pairs=pairs),
            [triple, row_bf16],
            (grad, qkv, out, kept[0], kept[1]),
            flops=2 * rows * width * wide * 4 + 8 * rows * SLOTS * wide * 2,
            traffic=5 << 20,
            scratch=[pltpu.VMEM((rows, wide), bf16)],
        )

    def feed(value, layer):
        return call(
            functools.partial(feed_kernel, layer=layer),
            [hidden_bf16, hidden_bf16, row_bf16],
            (value, up_weight, up_other, up_bias, shift_other, down_weight, down_other),
            flops=2 * rows * width * 2 * hq * 2,
            traffic=7 << 20,
        )

    def feed_back(grad, slope, layer):
        return call(
            functools.partial(feed_back_kernel, layer=layer),
            [hidden_bf16, row_bf16],
            (grad, slope, up_weight, up_other, down_weight, down_other),
            flops=2 * rows * width * 2 * hq * 2,
            traffic=7 << 20,
        )

    def feed_weights(hidden, grads, normed, pre):
        square = shape((hq, width), bf16)
        across = shape((width, hq), bf16)
        return call(
            feed_weights_kernel,
            [square, square, across, across, shape((1, 2 * hq), f32)],
            (*hidden, *grads, *normed, *pre),
            flops=2 * 2 * rows * width * 2 * hq * 2,
            traffic=10 << 20,
        )

    def attn_weights(normed, grads, mixed, parts):
        grouped = shape((4 * quarter, width), bf16)
        return call(
            functools.partial(attn_weights_kernel, quarter=quarter),
            [grouped, grouped, shape((2, wide), f32)],
            (*normed, *grads, *mixed, *parts),
            flops=2 * 2 * rows * width * wide * 4,
            traffic=7 << 20,
        )

    saved = []
    for layer in range(LAYERS):
        near_mask, far_mask = masks[layer % 2]
        kept_near = attend(inputs[0], layer, near_mask)
        kept_far = attend(inputs[1], layer, far_mask)
        attn = (kept_near[3], to_side(kept_far[3]))
        middle, normed_ff = call(
            functools.partial(mid_kernel, layer=layer, branch=0),
            [row_f32, row_bf16],
            (state, *attn, out_bias, gates, kind, norm_gain, norm_bias),
            traffic=3 << 20,
        )
        inputs_ff = [normed_ff, to_side(normed_ff)]
        feed_near = feed(inputs_ff[0], layer)
        feed_far = feed(inputs_ff[1], layer)
        fed = (feed_near[2], to_side(feed_far[2]))
        saved.append(
            (
                state,
                middle,
                attn,
                fed,
                inputs,
                inputs_ff,
                (kept_near, kept_far),
                (feed_near[0], feed_far[0]),
                (feed_near[1], feed_far[1]),
            )
        )
        if layer + 1 < LAYERS:
            state, normed = call(
                functools.partial(mid_kernel, layer=layer, branch=1),
                [row_f32, row_bf16],
                (middle, *fed, down_bias, gates, kind, norm_gain, norm_bias),
                traffic=3 << 20,
            )
            inputs = [normed, to_side(normed)]
    top = LAYERS - 1
    joined, feed_sums = call(
        functools.partial(last_kernel, layer=top),
        [row_bf16, sums],
        (saved[top][1], *saved[top][3], down_bias, gates, kind, cotangent),
        traffic=3 << 20,
        home=False,
    )

    def reduce_weights(mine, other, order):
        return reduce_over(mine, to_core(other), "dp", dp_size, order)

    bits = [1 << b for b in range(dp_size.bit_length() - 1)]
    late = bits[1:] + bits[:1]
    upstream = cotangent
    weight_grads = [None] * LAYERS
    small_parts = [None] * LAYERS
    for layer in reversed(range(LAYERS)):
        state_in, middle, attn, fed, inputs, inputs_ff, kept, hidden, slope = saved[layer]
        grads_ff = [feed_low, to_side(feed_low)]
        pre_far, back_far = feed_back(grads_ff[1], slope[1], layer)
        pre_near, back_near = feed_back(grads_ff[0], slope[0], layer)
        back_far = to_side(back_far)
        down_mine, down_rest, up_mine, up_rest, up_shift_grad = feed_weights(
            hidden, grads_ff, inputs_ff, (pre_near, pre_far)
        )
        down_total = reduce_weights(down_mine, down_rest, bits)
        up_total = reduce_weights(up_mine, up_rest, late)
        middle_grad, branch_low, mid_sums = call(
            functools.partial(back_mid_kernel, layer=layer),
            [row_f32, row_bf16, sums],
            (back_near, back_far, middle, upstream, kind, gates, norm_gain, *attn, out_bias),
            traffic=5 << 20,
        )
        grads_attn = [branch_low, to_side(branch_low)]
        parts_far = attend_back(grads_attn[1], layer, kept[1])
        parts_near = attend_back(grads_attn[0], layer, kept[0])
        back_near, back_far = parts_near[1], to_side(parts_far[1])
        attn_mine, attn_rest, qv_shift_grad = attn_weights(
            inputs, grads_attn, (kept[0][2], kept[1][2]), (parts_near[0], parts_far[0])
        )
        attn_total = reduce_weights(attn_mine, attn_rest, bits)
        down_sums = feed_sums
        if layer:
            upstream, feed_low, end_sums = call(
                functools.partial(back_end_kernel, layer=layer),
                [row_f32, row_bf16, sums],
                (back_near, back_far, state_in, middle_grad, kind, gates, norm_gain, *saved[layer - 1][3], down_bias),
                traffic=5 << 20,
            )
            feed_sums = end_sums
        else:
            text_grad, vision_grad, end_sums = call(
                finish_kernel,
                [row_f32, row_f32, sums],
                (back_near, back_far, state_in, middle_grad, kind, norm_gain),
                traffic=5 << 20,
                home=False,
            )
        small_parts[layer] = (end_sums, mid_sums, down_sums, up_shift_grad, qv_shift_grad)
        weight_grads[layer] = (attn_total, up_total, down_total)
    packed = shape((LAYERS * 4, width), f32)
    small, mine, other = call(
        functools.partial(pack_kernel, quarter=quarter, hq=hq),
        [shape((LAYERS * 12, width), f32), packed, packed],
        [entry for parts in small_parts for entry in parts],
    )
    total = jnp.concatenate([small, mine], axis=0) + to_core(jnp.concatenate([small, other], axis=0))
    small, mine = total[: LAYERS * 12], total[LAYERS * 12 :]
    total = jnp.concatenate([small + to_side(small), mine], axis=0)
    for bit in bits:
        total = total + swap(total, "dp", dp_size, bit)
    q = quarter
    flat = shape((LAYERS, width), f32)
    pair = shape((LAYERS, 2, width), f32)
    gain_grad, shift_grad, qv_grad, out_shift, gates_grad, up_shift, down_shift = call(
        functools.partial(unpack_kernel, quarter=q, hq=hq),
        [pair, pair, shape((LAYERS, 2, q), f32), flat, shape((LAYERS, 4, width), f32), shape((LAYERS, hq), f32), flat],
        (total,),
        home=False,
    )
    qkv_grad, out_grad = grouped_output([entry[0] for entry in weight_grads], q, width)
    return (
        joined,
        text_grad,
        vision_grad,
        gain_grad,
        shift_grad,
        jnp.swapaxes(qkv_grad, 2, 3),
        qv_grad,
        out_grad,
        out_shift,
        gates_grad,
        square_output([entry[1] for entry in weight_grads], width, hq),
        up_shift,
        square_output([entry[2] for entry in weight_grads], hq, width),
        down_shift,
    )


def solution(mesh):
    sizes = dict(mesh.shape)

    def run(*arrays):
        return body(*arrays, dp_size=sizes["dp"], tensor_size=sizes["tensor"])

    placed = (
        P(("dp", "tensor"), None),
        P(("dp", "tensor"), None),
        P("dp"),
        P("dp"),
        P("dp"),
        P(),
        P(),
        P(None, None, None, "tensor"),
        P(None, None, "tensor"),
        P(None, "tensor", None),
        P(),
        P(),
        P(None, None, "tensor"),
        P(None, "tensor"),
        P(None, "tensor", None),
        P(),
        P(("dp", "tensor"), None),
    )
    return jax.shard_map(
        run,
        mesh=mesh,
        in_specs=placed,
        out_specs=(
            P(("dp", "tensor"), None),
            P(("dp", "tensor"), None),
            P(("dp", "tensor"), None),
            P(),
            P(),
            P(None, None, None, "tensor"),
            P(None, None, "tensor"),
            P(None, "tensor", None),
            P(),
            P(),
            P(None, None, "tensor"),
            P(None, "tensor"),
            P(None, "tensor", None),
            P(),
        ),
        check_vma=False,
    )
```

```python
import functools

import jax
import jax.numpy as jnp
from jax import lax
from jax.experimental import pallas as pl
from jax.experimental.pallas import tpu as pltpu
from jax.sharding import PartitionSpec as P

HEAD_DIM = 64
LAYERS = 2
SLOTS = 128
SCALE = HEAD_DIM ** (-0.5)
PAIR = 2 * HEAD_DIM

epsilon = 1e-05
far_value = -1000000000.0
bf16 = jnp.bfloat16
f32 = jnp.float32


def logistic(values):
    return 1.0 / (1.0 + jnp.exp(-values))


def gelu_pair(values):
    size = jnp.abs(values)
    base = 1.0 + 0.23164189 * size
    t = pl.reciprocal(base, approx=True)
    t = t * (2.0 - base * t)
    bell = jnp.exp(-0.5 * (values * values))
    series = 0.5307027145 * t - 0.7265760135
    series = series * t + 0.7107068705
    series = series * t - 0.142248368
    series = series * t + 0.127414796
    tail = series * t * bell
    cdf = jnp.where(values < 0.0, tail, 1.0 - tail)
    return values * cdf, cdf + 0.3989422804014327 * (values * bell)


def norm_parts(values):
    center = values - jnp.mean(values, axis=-1, keepdims=True)
    spread = jnp.mean(center * center, axis=-1, keepdims=True)
    scale = lax.rsqrt(spread + epsilon)
    return center * scale, scale


def norm_back(grad, xhat, scale, gain):
    scaled = grad * gain
    inner = jnp.mean(scaled, axis=-1, keepdims=True)
    cross = jnp.mean(scaled * xhat, axis=-1, keepdims=True)
    return scale * (scaled - inner - xhat * cross)


def column(values):
    return jnp.sum(values, axis=0, keepdims=True)


def mm(left, right):
    return jnp.dot(left, right, preferred_element_type=f32)


def mm_nt(left, right):
    return lax.dot_general(left, right, (((1,), (1,)), ((), ())), preferred_element_type=f32)


def mm_tn(left, right):
    return lax.dot_general(left, right, (((0,), (0,)), ((), ())), preferred_element_type=f32)


def shape(dims, kind):
    return jax.ShapeDtypeStruct(dims, kind)


def call(kernel, outs, args, flops=0, traffic=1 << 20, scalars=0, scratch=(), room=20):
    return pl.pallas_call(
        kernel,
        out_shape=outs,
        in_specs=[SCALARS] * scalars + [WHOLE] * (len(args) - scalars),
        scratch_shapes=scratch,
        compiler_params=pltpu.CompilerParams(vmem_limit_bytes=room << 20),
        cost_estimate=pl.CostEstimate(flops=16 * flops, bytes_accessed=16 * traffic, transcendentals=0),
    )(*args)


SCALARS = pl.BlockSpec(memory_space=pltpu.SMEM)
WHOLE = pl.BlockSpec(memory_space=pltpu.VMEM)


def as_column(row):
    across = lax.broadcasted_iota(jnp.int32, (SLOTS, SLOTS), 1)
    down = lax.broadcasted_iota(jnp.int32, (SLOTS, SLOTS), 0)
    return jnp.sum(jnp.where(across == down, row, 0.0), axis=1, keepdims=True)


def gate_of(gates, layer, index, vision):
    return jnp.where(
        vision, logistic(gates[layer, index + 1 : index + 2]), logistic(gates[layer, index : index + 1])
    )


def start_kernel(place, kinds, text, vision, gain, shift, state_out, normed_out, kind_out, *, here):
    for g in range(here):
        span = slice(g * SLOTS, (g + 1) * SLOTS)
        kind = as_column(kinds[pl.ds(place[0] * here + g, 1), :].astype(f32))
        kind_out[span, :] = kind
        state = jnp.where(kind > 0.5, vision[span, :].astype(f32), text[span, :].astype(f32))
        state_out[span, :] = state
        xhat, _ = norm_parts(state)
        normed_out[span, :] = (xhat * gain[0, 0:1] + shift[0, 0:1]).astype(bf16)


def mask_kernel(place, splits, kinds, reals, cotangent, kind, gates, near_cross, near_self, far_cross, far_self, feed_out, *, here, layer):
    across = lax.broadcasted_iota(jnp.int32, (SLOTS, SLOTS), 1) // (SLOTS // 2)
    down = lax.broadcasted_iota(jnp.int32, (SLOTS, SLOTS), 0) // (SLOTS // 2)
    block = jnp.where(across == down, 1.0, 0.0)
    for side, (cross_out, self_out) in enumerate(((near_cross, near_self), (far_cross, far_self))):
        for g in range(here):
            index = place[side] * here + g
            row = kinds[pl.ds(index, 1), :].astype(f32)
            real = reals[pl.ds(index, 1), :].astype(f32)
            split = (splits[index] != 0).astype(f32)
            within = jnp.maximum(block, 1.0 - split) * jnp.where(real == 1.0, 1.0, 0.0)
            self_out[g] = within
            cross_out[g] = jnp.where(as_column(row) != row, within, 0.0)
    gate = gate_of(gates, layer, 2, kind[...] > 0.5)
    feed_out[...] = (cotangent[...].astype(f32) * gate).astype(bf16)


def mid_kernel(state, near, far, bias, gates, kind, gain, shift, state_out, normed_out, *, layer, branch):
    total = near[...].astype(f32) + far[...].astype(f32) + bias[layer : layer + 1]
    gate = gate_of(gates, layer, 2 * branch, kind[...] > 0.5)
    value = state[...] + gate * total
    state_out[...] = value
    xhat, _ = norm_parts(value)
    nl, ni = (layer, 1) if branch == 0 else (layer + 1, 0)
    normed_out[...] = (xhat * gain[nl, ni : ni + 1] + shift[nl, ni : ni + 1]).astype(bf16)


def gate_sums(grad, total, gate, vision):
    full = grad * total * (1.0 - gate)
    return [column(jnp.where(vision, 0.0, full)), column(jnp.where(vision, full, 0.0))]


def put_rows(out, rows):
    rows = rows + [jnp.zeros_like(rows[0])] * (8 - len(rows))
    for i, row in enumerate(rows):
        out[i : i + 1, :] = row


def last_kernel(state, near, far, bias, gates, kind, cotangent, joined_out, sums_out, *, layer):
    total = near[...].astype(f32) + far[...].astype(f32) + bias[layer : layer + 1]
    vision = kind[...] > 0.5
    gate = gate_of(gates, layer, 2, vision)
    joined_out[...] = (state[...] + gate * total).astype(bf16)
    grad = cotangent[...].astype(f32) * gate
    sums = gate_sums(grad, total, gate, vision)
    put_rows(sums_out, sums + [column(grad.astype(bf16).astype(f32))])


def back_mid_kernel(near, far, middle, upstream, kind, gates, gain, attn_near, attn_far, bias, grad_out, low_out, sums_out, *, layer):
    grad = near[...].astype(f32) + far[...].astype(f32)
    xhat, scale = norm_parts(middle[...])
    total = norm_back(grad, xhat, scale, gain[layer, 1:2]) + upstream[...].astype(f32)
    grad_out[...] = total
    vision = kind[...] > 0.5
    gate = gate_of(gates, layer, 0, vision)
    branch = total * gate
    low = branch.astype(bf16)
    low_out[...] = low
    attn = attn_near[...].astype(f32) + attn_far[...].astype(f32) + bias[layer : layer + 1]
    put_rows(
        sums_out,
        [column(grad * xhat), column(grad)]
        + gate_sums(branch, attn, gate, vision)
        + [column(low.astype(f32))],
    )


def back_end_kernel(near, far, state, middle_grad, kind, gates, gain, feed_near, feed_far, bias, grad_out, low_out, sums_out, *, layer):
    grad = near[...].astype(f32) + far[...].astype(f32)
    xhat, scale = norm_parts(state[...])
    total = norm_back(grad, xhat, scale, gain[layer, 0:1]) + middle_grad[...]
    grad_out[...] = total
    vision = kind[...] > 0.5
    below = layer - 1
    gate = gate_of(gates, below, 2, vision)
    branch = total * gate
    low = branch.astype(bf16)
    low_out[...] = low
    feed = feed_near[...].astype(f32) + feed_far[...].astype(f32) + bias[below : below + 1]
    put_rows(
        sums_out,
        [column(grad * xhat), column(grad)]
        + gate_sums(branch, feed, gate, vision)
        + [column(low.astype(f32))],
    )


def finish_kernel(near, far, state, middle_grad, kind, gain, text_out, vision_out, sums_out):
    grad = near[...].astype(f32) + far[...].astype(f32)
    xhat, scale = norm_parts(state[...])
    total = norm_back(grad, xhat, scale, gain[0, 0:1]) + middle_grad[...]
    vision = kind[...] > 0.5
    text_out[...] = jnp.where(vision, 0.0, total)
    vision_out[...] = jnp.where(vision, total, 0.0)
    put_rows(sums_out, [column(grad * xhat), column(grad)])


def head_masks():
    lane = lax.broadcasted_iota(jnp.int32, (1, PAIR), 1)
    low = (lane < HEAD_DIM).astype(f32)
    return low.astype(bf16), (1.0 - low).astype(bf16)


def doubled(value, masks):
    return jnp.concatenate([value * masks[0], value * masks[1]], axis=0)


def join_kernel(qkv_mine, qkv_other, out_mine, out_other, qkv, out, *, layer, quarter):
    rest = quarter - PAIR
    sources = [(qkv_mine[layer, i], qkv_other[i], qkv, 2 * quarter * i) for i in range(3)]
    sources.append((out_mine[layer], out_other[layer], out, 0))
    for mine, other, joined, base in sources:
        joined[base : base + PAIR, :] = mine[:PAIR]
        joined[base + PAIR : base + 2 * PAIR, :] = other[:PAIR]
        joined[base + 2 * PAIR : base + 2 * PAIR + rest, :] = mine[PAIR:]
        joined[base + 2 * PAIR + rest : base + 2 * quarter, :] = other[PAIR:]


def attn_kernel(normed, qkv, shifts, out, allowed, qkv_out, probs_out, mixed_out, total_out, *, here, pairs):
    wide = pairs * PAIR
    projected = mm_nt(normed[...], qkv[...])
    qkv_out[:, :wide] = (projected[:, :wide] + shifts[0:1]).astype(bf16)
    qkv_out[:, wide : 2 * wide] = projected[:, wide : 2 * wide].astype(bf16)
    qkv_out[:, 2 * wide :] = (projected[:, 2 * wide :] + shifts[1:2]).astype(bf16)
    masks = head_masks()
    for g in range(here):
        rows = slice(g * SLOTS, (g + 1) * SLOTS)
        open_here = allowed[g] > 0.5
        for p in range(pairs):
            q, k, v = [qkv_out[rows, i * wide + p * PAIR : i * wide + (p + 1) * PAIR] for i in range(3)]
            raw = mm_nt(q, doubled(k, masks))
            parts = []
            for h in range(2):
                scores = jnp.where(open_here, raw[:, h * SLOTS : (h + 1) * SLOTS] * SCALE, far_value)
                exponent = jnp.exp(scores - jnp.max(scores, axis=-1, keepdims=True))
                inverse = 1.0 / jnp.sum(exponent, axis=-1, keepdims=True)
                parts.append((exponent * inverse).astype(bf16))
            probs = jnp.concatenate(parts, axis=1)
            probs_out[g, p] = probs
            mixed_out[rows, p * PAIR : (p + 1) * PAIR] = mm(probs, doubled(v, masks)).astype(bf16)
    total_out[...] = mm(mixed_out[...], out[...]).astype(bf16)


def attn_back_kernel(grad, qkv, out, qkv_in, probs_in, grads_out, total_out, mixed_grad, *, here, pairs):
    wide = pairs * PAIR
    mixed_grad[...] = mm_nt(grad[...], out[...]).astype(bf16)
    masks = head_masks()
    low_lanes = lax.broadcasted_iota(jnp.int32, (SLOTS, PAIR), 1) < HEAD_DIM
    for g in range(here):
        rows = slice(g * SLOTS, (g + 1) * SLOTS)
        for p in range(pairs):
            spans = [slice(i * wide + p * PAIR, i * wide + (p + 1) * PAIR) for i in range(3)]
            q, k, v = [qkv_in[rows, span] for span in spans]
            probs = probs_in[g, p]
            back = mixed_grad[rows, spans[0]]
            both = mm_tn(probs, back)
            grads_out[rows, spans[2]] = jnp.where(low_lanes, both[:SLOTS], both[SLOTS:]).astype(bf16)
            prob_grad = mm_nt(back, doubled(v, masks))
            weights = probs.astype(f32)
            product = weights * prob_grad
            parts = []
            for h in range(2):
                span = slice(h * SLOTS, (h + 1) * SLOTS)
                total = jnp.sum(product[:, span], axis=-1, keepdims=True)
                parts.append((product[:, span] - weights[:, span] * total).astype(bf16))
            score_grad = jnp.concatenate(parts, axis=1)
            grads_out[rows, spans[0]] = (SCALE * mm(score_grad, doubled(k, masks))).astype(bf16)
            both = SCALE * mm_tn(score_grad, q)
            grads_out[rows, spans[1]] = jnp.where(low_lanes, both[:SLOTS], both[SLOTS:]).astype(bf16)
    total_out[...] = mm(grads_out[...], qkv[...]).astype(bf16)


def attn_weights_kernel(normed_n, normed_f, grad_n, grad_f, mixed_n, mixed_f, dqkv_n, dqkv_f, mine_out, other_out, shifts_out, *, quarter):
    rest = quarter - PAIR
    wide = 2 * quarter
    for i in range(4):
        if i < 3:
            span = slice(i * wide, (i + 1) * wide)
            total = mm_tn(dqkv_n[:, span], normed_n[...]) + mm_tn(dqkv_f[:, span], normed_f[...])
        else:
            total = mm_tn(mixed_n[...], grad_n[...]) + mm_tn(mixed_f[...], grad_f[...])
        total = total.astype(bf16)
        base = i * quarter
        mine_out[base : base + PAIR, :] = total[:PAIR]
        mine_out[base + PAIR : base + quarter, :] = total[2 * PAIR : 2 * PAIR + rest]
        other_out[base : base + PAIR, :] = total[PAIR : 2 * PAIR]
        other_out[base + PAIR : base + quarter, :] = total[2 * PAIR + rest :]
    for j, i in enumerate((0, 2)):
        span = slice(i * wide, (i + 1) * wide)
        shifts_out[j : j + 1, :] = column(dqkv_n[:, span].astype(f32)) + column(dqkv_f[:, span].astype(f32))


def feed_kernel(normed, up_mine, up_other, shift_mine, shift_other, down_mine, down_other, hidden_out, slope_out, total_out, *, layer):
    hq = up_mine.shape[2]
    total = None
    for i, (up, shift, down) in enumerate(((up_mine, shift_mine, down_mine), (up_other, shift_other, down_other))):
        span = slice(i * hq, (i + 1) * hq)
        act, slope = gelu_pair(mm(normed[...], up[layer]) + shift[layer : layer + 1])
        hidden_out[:, span] = act.astype(bf16)
        slope_out[:, span] = slope.astype(bf16)
        part = mm(hidden_out[:, span], down[layer])
        total = part if total is None else total + part
    total_out[...] = total.astype(bf16)


def feed_back_kernel(grad, slope, up_mine, up_other, down_mine, down_other, pre_out, total_out, *, layer):
    hq = up_mine.shape[2]
    total = None
    for i, (up, down) in enumerate(((up_mine, down_mine), (up_other, down_other))):
        span = slice(i * hq, (i + 1) * hq)
        back = mm_nt(grad[...], down[layer]).astype(bf16).astype(f32)
        pre_out[:, span] = (back * slope[:, span].astype(f32)).astype(bf16)
        part = mm_nt(pre_out[:, span], up[layer])
        total = part if total is None else total + part
    total_out[...] = total.astype(bf16)


def down_weights_kernel(hidden_n, hidden_f, grad_n, grad_f, mine, other):
    hq = mine.shape[0]
    for i, out in enumerate((mine, other)):
        span = slice(i * hq, (i + 1) * hq)
        out[...] = (mm_tn(hidden_n[:, span], grad_n[...]) + mm_tn(hidden_f[:, span], grad_f[...])).astype(bf16)


def up_weights_kernel(normed_n, normed_f, pre_n, pre_f, mine, other, shifts_out):
    hq = mine.shape[1]
    for i, out in enumerate((mine, other)):
        span = slice(i * hq, (i + 1) * hq)
        out[...] = (mm_tn(normed_n[...], pre_n[:, span]) + mm_tn(normed_f[...], pre_f[:, span])).astype(bf16)
    shifts_out[...] = column(pre_n[...].astype(f32)) + column(pre_f[...].astype(f32))


def swap(value, axis, size, bit):
    return lax.ppermute(value, axis, [(i, i ^ bit) for i in range(size)])


def added_rows(left, right, start, height):
    return left[pl.ds(start, height), :].astype(f32) + right[pl.ds(start, height), :].astype(f32)


def split_kernel(flags, left, right, keep_out, send_out, *, step):
    half = keep_out.shape[0]
    keep_out[...] = added_rows(left, right, pl.multiple_of(flags[step] * half, 16), half).astype(bf16)
    send_out[...] = added_rows(left, right, pl.multiple_of((1 - flags[step]) * half, 16), half).astype(bf16)


def split_two_kernel(flags, left, left_other, right, right_other, keep_out, send_out):
    first = left[...].astype(f32) + left_other[...].astype(f32)
    second = right[...].astype(f32) + right_other[...].astype(f32)
    upper = flags[0] == 1
    keep_out[...] = jnp.where(upper, second, first).astype(bf16)
    send_out[...] = jnp.where(upper, first, second).astype(bf16)


def add_kernel(left, right, total_out):
    total_out[...] = (left[...].astype(f32) + right[...].astype(f32)).astype(total_out.dtype)


def join_kernel_rows(upper, lower, out):
    out[: upper.shape[0], :] = upper[...]
    out[upper.shape[0] :, :] = lower[...]


class Order:
    def __init__(self):
        self.token = None

    def after(self, values):
        if self.token is None:
            return values
        values, _ = lax.optimization_barrier((values, self.token))
        return values

    def run(self, kernel, outs, args, **more):
        results = call(kernel, outs, self.after(tuple(args)), **more)
        self.token = results[-1] if isinstance(results, (list, tuple)) else results
        return results


class Lanes:
    def __init__(self, orders, dp_size, tensor_size):
        self.orders, self.dp_size, self.tensor_size = orders, dp_size, tensor_size
        self.steps = len(orders[0])
        place = lax.axis_index("dp")
        odd = lax.axis_index("tensor") % 2
        flags = [jnp.where(odd == 1, (place // b) % 2, (place // a) % 2) for a, b in zip(*orders)]
        self.flags = jnp.stack(flags).astype(jnp.int32)

    def swap(self, value, step):
        pairs = [
            (d * self.tensor_size + t, (d ^ self.orders[t % 2][step]) * self.tensor_size + t)
            for d in range(self.dp_size)
            for t in range(self.tensor_size)
        ]
        return lax.ppermute(value, ("dp", "tensor"), pairs)


class Summed:
    def __init__(self, addends, lanes, order):
        self.addends, self.lanes, self.order = addends, lanes, order
        self.height = sum(entry[0].shape[0] for entry in addends)
        self.step = 0
        self.masks = [0]

    def advance(self):
        lanes, steps, step = self.lanes, self.lanes.steps, self.step
        if step == 0 and len(self.addends) == 2:
            args = [entry for pair in self.addends for entry in pair]
        elif step == 0:
            args = list(self.addends[0])
        else:
            args = [self.held, self.got]
        height, width = args[0].shape
        traffic = 6 * height * width
        if step < steps:
            half = shape((self.height // (2 << step), width), bf16)
            work = split_two_kernel if len(args) == 4 else functools.partial(split_kernel, step=step)
            self.held, send = self.order.run(work, [half, half], (lanes.flags, *args), scalars=1, traffic=traffic)
            self.got = lanes.swap(send, step)
        elif step == steps:
            self.held = self.order.run(add_kernel, shape((height, width), bf16), args, traffic=traffic)
        else:
            self.held = self.order.run(join_kernel_rows, shape((2 * height, width), bf16), args, traffic=traffic)
        if step >= steps:
            back = 2 * steps - 1 - step
            self.got = lanes.swap(self.held, back)
            self.masks = self.masks + [mask ^ (1 << back) for mask in self.masks]
        self.step += 1

    def finish(self):
        starts = []
        for mask in self.masks:
            start, span = 0, self.height
            for step in range(self.lanes.steps):
                span //= 2
                flag = self.lanes.flags[step]
                start = start + span * ((1 - flag) if mask >> step & 1 else flag)
            starts.append(start)
        return [self.held, self.got], starts


class Whole:
    def __init__(self, addends):
        totals = [call(add_kernel, shape(a.shape, bf16), (a, b)) for a, b in addends]
        self.total = lax.psum(jnp.concatenate(totals, axis=0), "dp")
        self.height = self.total.shape[0]

    def advance(self):
        pass

    def finish(self):
        return [self.total], [0]


def placed_parts(starts, refs, count, total, layer):
    each = total // count
    index = 0
    for ref in refs:
        part = ref.shape[0] // each
        for j in range(each):
            start = pl.multiple_of(starts[layer * total + index], 16)
            yield start, ref[j * part : (j + 1) * part, :]
            index += 1


def square_kernel(starts, *refs, count, total):
    down_out, up_out, whole = refs[-3:]
    for start, part in placed_parts(starts, refs[:count], count, total, 0):
        whole[pl.ds(start, part.shape[0]), :] = part
    height = down_out.shape[1]
    down_out[0] = whole[:height, :].astype(f32)
    up_out[0] = whole[height:, :].astype(f32)


def grouped_kernel(starts, *refs, count, total, quarter):
    qkv_out, out_out, whole = refs[-3:]
    for start, part in placed_parts(starts, refs[:count], count, total, 0):
        whole[pl.ds(start, part.shape[0]), :] = part
    for i in range(3):
        qkv_out[0, i] = whole[i * quarter : (i + 1) * quarter, :].astype(f32)
    out_out[0] = whole[3 * quarter :, :].astype(f32)


def at_layer(array_shape, layer):
    zeros = (0,) * (len(array_shape) - 1)
    return pl.BlockSpec((1,) + array_shape[1:], lambda i: (layer,) + zeros)


def layer_output(kernel, outs, item, layer, before):
    pieces, starts = item.finish()
    starts = jnp.stack([jnp.asarray(start, jnp.int32) for start in starts])
    count, total = len(pieces), starts.shape[0]
    before = before or []
    whole = [pl.BlockSpec(piece.shape, lambda i: (0, 0)) for piece in pieces]
    return pl.pallas_call(
        functools.partial(kernel, count=count, total=total),
        out_shape=outs,
        grid=(1,),
        in_specs=[SCALARS] + whole + [pl.BlockSpec(memory_space=pl.ANY)] * len(before),
        out_specs=[at_layer(entry.shape, layer) for entry in outs],
        scratch_shapes=[pltpu.VMEM((item.height, pieces[0].shape[1]), bf16)],
        input_output_aliases={1 + count + i: i for i in range(len(before))},
        compiler_params=pltpu.CompilerParams(vmem_limit_bytes=24 << 20),
        cost_estimate=pl.CostEstimate(flops=0, bytes_accessed=sum(entry.size for entry in outs) * 3, transcendentals=0),
    )(starts, *pieces, *before)


def pack_kernel(*refs, quarter, hq):
    shared_out, mine_out, other_out = refs[-3:]
    rest = quarter - PAIR
    for layer in range(LAYERS):
        end, mid, feed, feed_row, up, qv = refs[layer * 5], refs[layer * 5 + 1], refs[layer * 5 + 2], 2 * (layer == 0), refs[layer * 5 + 3], refs[layer * 5 + 4]
        base = layer * 12
        shared_out[base : base + 1, :] = end[0:1]
        shared_out[base + 1 : base + 2, :] = mid[0:1]
        shared_out[base + 2 : base + 3, :] = end[1:2]
        shared_out[base + 3 : base + 4, :] = mid[1:2]
        shared_out[base + 4 : base + 6, :] = mid[2:4]
        shared_out[base + 6 : base + 8, :] = feed[feed_row : feed_row + 2]
        shared_out[base + 8 : base + 9, :] = mid[4:5]
        shared_out[base + 9 : base + 10, :] = feed[feed_row + 2 : feed_row + 3]
        shared_out[base + 10 : base + 12, :] = jnp.zeros_like(mid[0:2])
        for out, up_start, pair_start, rest_start in (
            (mine_out, 0, 0, 2 * PAIR),
            (other_out, hq, PAIR, 2 * PAIR + rest),
        ):
            base = layer * 4
            out[base : base + 4, :] = jnp.zeros_like(mid[0:4])
            out[base : base + 1, :hq] = up[0:1, up_start : up_start + hq]
            out[base + 1 : base + 3, :PAIR] = qv[0:2, pair_start : pair_start + PAIR]
            out[base + 1 : base + 3, PAIR : PAIR + rest] = qv[0:2, rest_start : rest_start + rest]


def unpack_kernel(total, gain, shift, qv, out, gates, up, down, *, quarter, hq):
    for layer in range(LAYERS):
        base = layer * 12
        gain[layer] = total[base : base + 2, :]
        shift[layer] = total[base + 2 : base + 4, :]
        gates[layer] = total[base + 4 : base + 8, :]
        out[layer : layer + 1, :] = total[base + 8 : base + 9, :]
        down[layer : layer + 1, :] = total[base + 9 : base + 10, :]
        base = LAYERS * 12 + layer * 4
        up[layer : layer + 1, :] = total[base : base + 1, :hq]
        qv[layer] = total[base + 1 : base + 3, :quarter]


def body(
    text_embed,
    vision_embed,
    region_mask,
    modality,
    doc_split,
    norm_gain,
    norm_bias,
    qkv_weight,
    qv_bias,
    out_weight,
    out_bias,
    gates,
    up_weight,
    up_bias,
    down_weight,
    down_bias,
    cotangent,
    dp_size,
    tensor_size,
):
    rows, width = text_embed.shape
    here = rows // SLOTS
    quarter = qkv_weight.shape[3]
    hq = up_weight.shape[2]
    wide = 2 * quarter
    pairs = wide // PAIR
    me = lax.axis_index("tensor")
    place = jnp.stack([me, me ^ 2]).astype(jnp.int32)

    def to_core(value):
        return swap(value, "tensor", tensor_size, 1)

    def to_side(value):
        return swap(value, "tensor", tensor_size, 2)

    kinds = modality.reshape(-1, SLOTS)
    reals = region_mask.reshape(-1, SLOTS)
    row_f32, row_bf16 = shape((rows, width), f32), shape((rows, width), bf16)
    wide_bf16, hidden_bf16 = shape((rows, wide), bf16), shape((rows, 2 * hq), bf16)
    sums = shape((8, width), f32)

    state, normed, kind = call(
        functools.partial(start_kernel, here=here),
        [row_f32, row_bf16, shape((rows, 1), f32)],
        (place, kinds, text_embed, vision_embed, norm_gain, norm_bias),
        scalars=1,
        traffic=3 << 20,
    )
    inputs = [normed, to_side(normed)]
    qkv_weight = jnp.swapaxes(qkv_weight, 2, 3)
    qkv_other = [to_core(qkv_weight[0])]
    out_other, qv_other = to_core(out_weight), to_core(qv_bias)
    up_later, down_later, qkv_later, shift_later, inputs[1] = lax.optimization_barrier(
        (up_weight, down_weight, qkv_weight, up_bias, inputs[1])
    )
    up_other, down_other, shift_other = to_core(up_later), to_core(down_later), to_core(shift_later)
    qkv_other = qkv_other + [to_core(qkv_later[layer]) for layer in range(1, LAYERS)]
    qv_all = jnp.concatenate(
        [qv_bias[..., :PAIR], qv_other[..., :PAIR], qv_bias[..., PAIR:], qv_other[..., PAIR:]], axis=-1
    )

    tile = shape((here, SLOTS, SLOTS), f32)
    near_cross, near_self, far_cross, far_self, feed_low = call(
        functools.partial(mask_kernel, here=here, layer=LAYERS - 1),
        [tile, tile, tile, tile, row_bf16],
        (place, doc_split, kinds, reals, cotangent, kind, gates),
        scalars=2,
        traffic=2 << 20,
    )
    masks = [(near_cross, far_cross), (near_self, far_self)]
    feed_far_low, _ = lax.optimization_barrier((feed_low, inputs[1]))
    feed_far_low = to_side(feed_far_low)

    joined_weights = [
        call(
            functools.partial(join_kernel, layer=layer, quarter=quarter),
            [shape((3 * wide, width), bf16), shape((wide, width), bf16)],
            (qkv_weight, qkv_other[layer], out_weight, out_other),
            traffic=6 << 20,
        )
        for layer in range(LAYERS)
    ]
    triple = shape((rows, 3 * wide), bf16)

    def attend(value, layer, allowed):
        qkv, out = joined_weights[layer]
        return call(
            functools.partial(attn_kernel, here=here, pairs=pairs),
            [triple, shape((here, pairs, SLOTS, 2 * SLOTS), bf16), wide_bf16, row_bf16],
            (value, qkv, qv_all[layer], out, allowed),
            flops=2 * rows * width * wide * 4 + 4 * rows * SLOTS * wide * 2,
            traffic=5 << 20,
        )

    def attend_back(grad, layer, kept, run):
        qkv, out = joined_weights[layer]
        return run(
            functools.partial(attn_back_kernel, here=here, pairs=pairs),
            [triple, row_bf16],
            (grad, qkv, out, kept[0], kept[1]),
            flops=2 * rows * width * wide * 4 + 8 * rows * SLOTS * wide * 2,
            traffic=5 << 20,
            scratch=[pltpu.VMEM((rows, wide), bf16)],
        )

    def feed(value, layer):
        return call(
            functools.partial(feed_kernel, layer=layer),
            [hidden_bf16, hidden_bf16, row_bf16],
            (value, up_weight, up_other, up_bias, shift_other, down_weight, down_other),
            flops=2 * rows * width * 2 * hq * 2,
            traffic=7 << 20,
        )

    def feed_back(grad, slope, layer, run):
        return run(
            functools.partial(feed_back_kernel, layer=layer),
            [hidden_bf16, row_bf16],
            (grad, slope, up_weight, up_other, down_weight, down_other),
            flops=2 * rows * width * 2 * hq * 2,
            traffic=7 << 20,
        )

    def down_weights(hidden, grads, run):
        square = shape((hq, width), bf16)
        return run(
            down_weights_kernel,
            [square, square],
            (*hidden, *grads),
            flops=2 * rows * width * 2 * hq * 2,
            traffic=5 << 20,
        )

    def up_weights(normed, pre, run):
        across = shape((width, hq), bf16)
        return run(
            up_weights_kernel,
            [across, across, shape((1, 2 * hq), f32)],
            (*normed, *pre),
            flops=2 * rows * width * 2 * hq * 2,
            traffic=5 << 20,
        )

    def attn_weights(normed, grads, mixed, parts, run):
        grouped = shape((4 * quarter, width), bf16)
        return run(
            functools.partial(attn_weights_kernel, quarter=quarter),
            [grouped, grouped, shape((2, wide), f32)],
            (*normed, *grads, *mixed, *parts),
            flops=2 * 2 * rows * width * wide * 4,
            traffic=7 << 20,
        )

    saved = []
    for layer in range(LAYERS):
        near_mask, far_mask = masks[layer % 2]
        kept_near = attend(inputs[0], layer, near_mask)
        kept_far = attend(inputs[1], layer, far_mask)
        attn = (kept_near[3], to_side(kept_far[3]))
        middle, normed_ff = call(
            functools.partial(mid_kernel, layer=layer, branch=0),
            [row_f32, row_bf16],
            (state, *attn, out_bias, gates, kind, norm_gain, norm_bias),
            traffic=3 << 20,
        )
        inputs_ff = [normed_ff, to_side(normed_ff)]
        feed_near = feed(inputs_ff[0], layer)
        feed_far = feed(inputs_ff[1], layer)
        fed = (feed_near[2], to_side(feed_far[2]))
        saved.append(
            (
                state,
                middle,
                attn,
                fed,
                inputs,
                inputs_ff,
                (kept_near, kept_far),
                (feed_near[0], feed_far[0]),
                (feed_near[1], feed_far[1]),
            )
        )
        if layer + 1 < LAYERS:
            state, normed = call(
                functools.partial(mid_kernel, layer=layer, branch=1),
                [row_f32, row_bf16],
                (middle, *fed, down_bias, gates, kind, norm_gain, norm_bias),
                traffic=3 << 20,
            )
            inputs = [normed, to_side(normed)]
    top = LAYERS - 1
    joined, feed_sums = call(
        functools.partial(last_kernel, layer=top),
        [row_bf16, sums],
        (saved[top][1], *saved[top][3], down_bias, gates, kind, cotangent),
        traffic=3 << 20,
    )

    bits = [1 << b for b in range(dp_size.bit_length() - 1)]
    stepped = dp_size == 1 << len(bits) and width % (16 * dp_size) == 0 and len(bits) > 1
    order = Order()
    lanes = Lanes((bits, [bits[1], bits[0]] + bits[2:]), dp_size, tensor_size) if stepped else None

    def summed(*addends):
        return Summed(addends, lanes, order) if stepped else Whole(addends)

    squares = [shape((LAYERS, hq, width), f32), shape((LAYERS, width, hq), f32)]
    grouped = [shape((LAYERS, 3, quarter, width), f32), shape((LAYERS, quarter, width), f32)]
    group_work = functools.partial(grouped_kernel, quarter=quarter)

    def back_mid(layer, near, far, upstream):
        _, middle, attn = saved[layer][:3]
        return order.run(
            functools.partial(back_mid_kernel, layer=layer),
            [row_f32, row_bf16, sums],
            (near, far, middle, upstream, kind, gates, norm_gain, *attn, out_bias),
            traffic=5 << 20,
        )

    def do_feed_back(side, layer, grad):
        return feed_back(grad, saved[layer][8][side], layer, order.run)

    def do_feed_weights(layer, grads, pre):
        _, _, _, _, _, inputs_ff, _, hidden, _ = saved[layer]
        down_mine, down_rest = down_weights(hidden, grads, order.run)
        down_rest = to_core(down_rest)
        up_mine, up_rest, shift_grad = up_weights(inputs_ff, pre, order.run)
        return summed((down_mine, down_rest), (up_mine, to_core(up_rest))), shift_grad

    def do_attn_back(side, layer, grad):
        return attend_back(grad, layer, saved[layer][6][side], order.run)

    def do_attn_weights(layer, grads, parts):
        kept, inputs = saved[layer][6], saved[layer][4]
        mine, rest, shift_grad = attn_weights(inputs, grads, (kept[0][2], kept[1][2]), parts, order.run)
        return summed((mine, to_core(rest))), shift_grad

    low = [feed_low, feed_far_low]
    pre_far, far = do_feed_back(1, 1, low[1])
    far = to_side(far)
    pre_near, near = do_feed_back(0, 1, low[0])
    feed_1, up_shift_1 = do_feed_weights(1, low, (pre_near, pre_far))
    middle_grad, low, mid_sums_1 = back_mid(1, near, far, cotangent)
    low = [low, to_side(low)]
    part_near, near = do_attn_back(0, 1, low[0])
    feed_1.advance()
    part_far, far = do_attn_back(1, 1, low[1])
    far = to_side(far)
    attn_1, qv_shift_1 = do_attn_weights(1, low, (part_near, part_far))
    feed_1.advance()
    state_in = saved[1][0]
    upstream, low, end_sums_1 = order.run(
        functools.partial(back_end_kernel, layer=1),
        [row_f32, row_bf16, sums],
        (near, far, state_in, middle_grad, kind, gates, norm_gain, *saved[0][3], down_bias),
        traffic=5 << 20,
    )
    low = [low, to_side(low)]
    pre_near, near = do_feed_back(0, 0, low[0])
    attn_1.advance()
    feed_1.advance()
    pre_far, far = do_feed_back(1, 0, low[1])
    far = to_side(far)
    feed_0, up_shift_0 = do_feed_weights(0, low, (pre_near, pre_far))
    attn_1.advance()
    feed_1.advance()
    middle_grad, low, mid_sums_0 = back_mid(0, near, far, upstream)
    low = [low, to_side(low)]
    part_near, near = do_attn_back(0, 0, low[0])
    feed_0.advance()
    attn_1.advance()
    feed_1.advance()
    part_far, far = do_attn_back(1, 0, low[1])
    far = to_side(far)
    attn_0, qv_shift_0 = do_attn_weights(0, low, (part_near, part_far))
    feed_0.advance()
    attn_1.advance()
    feed_1.advance()
    text_grad, vision_grad, end_sums_0 = order.run(
        finish_kernel,
        [row_f32, row_f32, sums],
        (near, far, saved[0][0], middle_grad, kind, norm_gain),
        traffic=5 << 20,
    )
    attn_0.advance()
    packed = shape((LAYERS * 4, width), f32)
    small, mine, other = order.run(
        functools.partial(pack_kernel, quarter=quarter, hq=hq),
        [shape((LAYERS * 12, width), f32), packed, packed],
        (
            end_sums_0, mid_sums_0, end_sums_1, up_shift_0, qv_shift_0,
            end_sums_1, mid_sums_1, feed_sums, up_shift_1, qv_shift_1,
        ),
    )
    head = LAYERS * 12
    sent = to_core(jnp.concatenate([small, other], axis=0))
    little = jnp.concatenate([small, mine], axis=0)

    def add_little(value, got):
        return order.run(add_kernel, shape(value.shape, f32), (value, got))

    feed_0.advance()
    attn_1.advance()
    attn_0.advance()
    little = add_little(little, sent)
    got = jnp.concatenate([to_side(little[:head]), jnp.zeros_like(little[head:])], axis=0)
    feed_0.advance()
    attn_1.advance()
    upper_squares = layer_output(square_kernel, squares, feed_1, 1, None)
    attn_0.advance()
    little = add_little(little, got)
    if stepped:
        got = lanes.swap(little, 0)
    feed_0.advance()
    upper_grouped = layer_output(group_work, grouped, attn_1, 1, None)
    for i in range(1, 3):
        attn_0.advance()
        if stepped and i < len(bits):
            little = add_little(little, got)
            got = lanes.swap(little, i)
        if i == 1:
            feed_0.advance()
    total = add_little(little, got) if stepped else lax.psum(little, "dp")
    attn_0.advance()
    down_grad, up_grad = layer_output(square_kernel, squares, feed_0, 0, upper_squares)
    qkv_grad, out_grad = layer_output(group_work, grouped, attn_0, 0, upper_grouped)
    q = quarter
    flat = shape((LAYERS, width), f32)
    pair = shape((LAYERS, 2, width), f32)
    gain_grad, shift_grad, qv_grad, out_shift, gates_grad, up_shift, down_shift = call(
        functools.partial(unpack_kernel, quarter=q, hq=hq),
        [pair, pair, shape((LAYERS, 2, q), f32), flat, shape((LAYERS, 4, width), f32), shape((LAYERS, hq), f32), flat],
        (total,),
    )
    return (
        joined,
        text_grad,
        vision_grad,
        gain_grad,
        shift_grad,
        jnp.swapaxes(qkv_grad, 2, 3),
        qv_grad,
        out_grad,
        out_shift,
        gates_grad,
        up_grad,
        up_shift,
        down_grad,
        down_shift,
    )


def solution(mesh):
    sizes = dict(mesh.shape)

    def run(*arrays):
        return body(*arrays, dp_size=sizes["dp"], tensor_size=sizes["tensor"])

    placed = (
        P(("dp", "tensor"), None),
        P(("dp", "tensor"), None),
        P("dp"),
        P("dp"),
        P("dp"),
        P(),
        P(),
        P(None, None, None, "tensor"),
        P(None, None, "tensor"),
        P(None, "tensor", None),
        P(),
        P(),
        P(None, None, "tensor"),
        P(None, "tensor"),
        P(None, "tensor", None),
        P(),
        P(("dp", "tensor"), None),
    )
    return jax.shard_map(
        run,
        mesh=mesh,
        in_specs=placed,
        out_specs=(
            P(("dp", "tensor"), None),
            P(("dp", "tensor"), None),
            P(("dp", "tensor"), None),
            P(),
            P(),
            P(None, None, None, "tensor"),
            P(None, None, "tensor"),
            P(None, "tensor", None),
            P(),
            P(),
            P(None, None, "tensor"),
            P(None, "tensor"),
            P(None, "tensor", None),
            P(),
        ),
        check_vma=False,
    )
```

```python
import functools

import jax
import jax.numpy as jnp
from jax import lax
from jax.experimental import pallas as pl
from jax.experimental.pallas import tpu as pltpu
from jax.sharding import PartitionSpec as P

HEAD_DIM = 64
LAYERS = 2
SLOTS = 128
SCALE = HEAD_DIM ** (-0.5)
PAIR = 2 * HEAD_DIM

epsilon = 1e-05
far_value = -1000000000.0
bf16 = jnp.bfloat16
f32 = jnp.float32


def logistic(values):
    return 1.0 / (1.0 + jnp.exp(-values))


def gelu_pair(values):
    size = jnp.abs(values)
    base = 1.0 + 0.23164189 * size
    t = pl.reciprocal(base, approx=True)
    t = t * (2.0 - base * t)
    bell = jnp.exp(-0.5 * (values * values))
    series = 0.5307027145 * t - 0.7265760135
    series = series * t + 0.7107068705
    series = series * t - 0.142248368
    series = series * t + 0.127414796
    tail = series * t * bell
    cdf = jnp.where(values < 0.0, tail, 1.0 - tail)
    return values * cdf, cdf + 0.3989422804014327 * (values * bell)


def norm_parts(values):
    center = values - jnp.mean(values, axis=-1, keepdims=True)
    spread = jnp.mean(center * center, axis=-1, keepdims=True)
    scale = lax.rsqrt(spread + epsilon)
    return center * scale, scale


def norm_back(grad, xhat, scale, gain):
    scaled = grad * gain
    inner = jnp.mean(scaled, axis=-1, keepdims=True)
    cross = jnp.mean(scaled * xhat, axis=-1, keepdims=True)
    return scale * (scaled - inner - xhat * cross)


def column(values):
    return jnp.sum(values, axis=0, keepdims=True)


def mm(left, right):
    return jnp.dot(left, right, preferred_element_type=f32)


def mm_nt(left, right):
    return lax.dot_general(left, right, (((1,), (1,)), ((), ())), preferred_element_type=f32)


def mm_tn(left, right):
    return lax.dot_general(left, right, (((0,), (0,)), ((), ())), preferred_element_type=f32)


def shape(dims, kind):
    return jax.ShapeDtypeStruct(dims, kind)


def call(kernel, outs, args, flops=0, traffic=1 << 20, scalars=0, scratch=(), room=20):
    return pl.pallas_call(
        kernel,
        out_shape=outs,
        in_specs=[SCALARS] * scalars + [WHOLE] * (len(args) - scalars),
        scratch_shapes=scratch,
        compiler_params=pltpu.CompilerParams(vmem_limit_bytes=room << 20),
        cost_estimate=pl.CostEstimate(flops=16 * flops, bytes_accessed=16 * traffic, transcendentals=0),
    )(*args)


SCALARS = pl.BlockSpec(memory_space=pltpu.SMEM)
WHOLE = pl.BlockSpec(memory_space=pltpu.VMEM)


def as_column(row):
    across = lax.broadcasted_iota(jnp.int32, (SLOTS, SLOTS), 1)
    down = lax.broadcasted_iota(jnp.int32, (SLOTS, SLOTS), 0)
    return jnp.sum(jnp.where(across == down, row, 0.0), axis=1, keepdims=True)


def gate_of(gates, layer, index, vision):
    return jnp.where(
        vision, logistic(gates[layer, index + 1 : index + 2]), logistic(gates[layer, index : index + 1])
    )


def start_kernel(place, kinds, text, vision, gain, shift, state_out, normed_out, kind_out, *, here):
    for g in range(here):
        span = slice(g * SLOTS, (g + 1) * SLOTS)
        kind = as_column(kinds[pl.ds(place[0] * here + g, 1), :].astype(f32))
        kind_out[span, :] = kind
        state = jnp.where(kind > 0.5, vision[span, :].astype(f32), text[span, :].astype(f32))
        state_out[span, :] = state
        xhat, _ = norm_parts(state)
        normed_out[span, :] = (xhat * gain[0, 0:1] + shift[0, 0:1]).astype(bf16)


def mask_kernel(place, splits, kinds, reals, cotangent, kind, gates, near_cross, near_self, far_cross, far_self, feed_out, *, here, layer):
    across = lax.broadcasted_iota(jnp.int32, (SLOTS, SLOTS), 1) // (SLOTS // 2)
    down = lax.broadcasted_iota(jnp.int32, (SLOTS, SLOTS), 0) // (SLOTS // 2)
    block = jnp.where(across == down, 1.0, 0.0)
    for side, (cross_out, self_out) in enumerate(((near_cross, near_self), (far_cross, far_self))):
        for g in range(here):
            index = place[side] * here + g
            row = kinds[pl.ds(index, 1), :].astype(f32)
            real = reals[pl.ds(index, 1), :].astype(f32)
            split = (splits[index] != 0).astype(f32)
            within = jnp.maximum(block, 1.0 - split) * jnp.where(real == 1.0, 1.0, 0.0)
            self_out[g] = within
            cross_out[g] = jnp.where(as_column(row) != row, within, 0.0)
    gate = gate_of(gates, layer, 2, kind[...] > 0.5)
    feed_out[...] = (cotangent[...].astype(f32) * gate).astype(bf16)


def mid_kernel(state, near, far, bias, gates, kind, gain, shift, state_out, normed_out, *, layer, branch):
    total = near[...].astype(f32) + far[...].astype(f32) + bias[layer : layer + 1]
    gate = gate_of(gates, layer, 2 * branch, kind[...] > 0.5)
    value = state[...] + gate * total
    state_out[...] = value
    xhat, _ = norm_parts(value)
    nl, ni = (layer, 1) if branch == 0 else (layer + 1, 0)
    normed_out[...] = (xhat * gain[nl, ni : ni + 1] + shift[nl, ni : ni + 1]).astype(bf16)


def gate_sums(grad, total, gate, vision):
    full = grad * total * (1.0 - gate)
    return [column(jnp.where(vision, 0.0, full)), column(jnp.where(vision, full, 0.0))]


def put_rows(out, rows):
    rows = rows + [jnp.zeros_like(rows[0])] * (8 - len(rows))
    for i, row in enumerate(rows):
        out[i : i + 1, :] = row


def last_kernel(state, near, far, bias, gates, kind, cotangent, joined_out, sums_out, *, layer):
    total = near[...].astype(f32) + far[...].astype(f32) + bias[layer : layer + 1]
    vision = kind[...] > 0.5
    gate = gate_of(gates, layer, 2, vision)
    joined_out[...] = (state[...] + gate * total).astype(bf16)
    grad = cotangent[...].astype(f32) * gate
    sums = gate_sums(grad, total, gate, vision)
    put_rows(sums_out, sums + [column(grad.astype(bf16).astype(f32))])


def back_mid_kernel(near, far, middle, upstream, kind, gates, gain, attn_near, attn_far, bias, grad_out, low_out, sums_out, *, layer):
    grad = near[...].astype(f32) + far[...].astype(f32)
    xhat, scale = norm_parts(middle[...])
    total = norm_back(grad, xhat, scale, gain[layer, 1:2]) + upstream[...].astype(f32)
    grad_out[...] = total
    vision = kind[...] > 0.5
    gate = gate_of(gates, layer, 0, vision)
    branch = total * gate
    low = branch.astype(bf16)
    low_out[...] = low
    attn = attn_near[...].astype(f32) + attn_far[...].astype(f32) + bias[layer : layer + 1]
    put_rows(
        sums_out,
        [column(grad * xhat), column(grad)]
        + gate_sums(branch, attn, gate, vision)
        + [column(low.astype(f32))],
    )


def back_end_kernel(near, far, state, middle_grad, kind, gates, gain, feed_near, feed_far, bias, grad_out, low_out, sums_out, *, layer):
    grad = near[...].astype(f32) + far[...].astype(f32)
    xhat, scale = norm_parts(state[...])
    total = norm_back(grad, xhat, scale, gain[layer, 0:1]) + middle_grad[...]
    grad_out[...] = total
    vision = kind[...] > 0.5
    below = layer - 1
    gate = gate_of(gates, below, 2, vision)
    branch = total * gate
    low = branch.astype(bf16)
    low_out[...] = low
    feed = feed_near[...].astype(f32) + feed_far[...].astype(f32) + bias[below : below + 1]
    put_rows(
        sums_out,
        [column(grad * xhat), column(grad)]
        + gate_sums(branch, feed, gate, vision)
        + [column(low.astype(f32))],
    )


def finish_kernel(near, far, state, middle_grad, kind, gain, text_out, vision_out, sums_out):
    grad = near[...].astype(f32) + far[...].astype(f32)
    xhat, scale = norm_parts(state[...])
    total = norm_back(grad, xhat, scale, gain[0, 0:1]) + middle_grad[...]
    vision = kind[...] > 0.5
    text_out[...] = jnp.where(vision, 0.0, total)
    vision_out[...] = jnp.where(vision, total, 0.0)
    put_rows(sums_out, [column(grad * xhat), column(grad)])


def head_masks():
    lane = lax.broadcasted_iota(jnp.int32, (1, PAIR), 1)
    low = (lane < HEAD_DIM).astype(f32)
    return low.astype(bf16), (1.0 - low).astype(bf16)


def doubled(value, masks):
    return jnp.concatenate([value * masks[0], value * masks[1]], axis=0)


def join_kernel(qkv_mine, qkv_other, out_mine, out_other, qkv, out, *, layer, quarter):
    rest = quarter - PAIR
    sources = [(qkv_mine[layer, i], qkv_other[layer, i], qkv, 2 * quarter * i) for i in range(3)]
    sources.append((out_mine[layer], out_other[layer], out, 0))
    for mine, other, joined, base in sources:
        joined[base : base + PAIR, :] = mine[:PAIR]
        joined[base + PAIR : base + 2 * PAIR, :] = other[:PAIR]
        joined[base + 2 * PAIR : base + 2 * PAIR + rest, :] = mine[PAIR:]
        joined[base + 2 * PAIR + rest : base + 2 * quarter, :] = other[PAIR:]


def attn_kernel(normed, qkv, shifts, out, allowed, qkv_out, probs_out, mixed_out, total_out, *, here, pairs):
    wide = pairs * PAIR
    projected = mm_nt(normed[...], qkv[...])
    qkv_out[:, :wide] = (projected[:, :wide] + shifts[0:1]).astype(bf16)
    qkv_out[:, wide : 2 * wide] = projected[:, wide : 2 * wide].astype(bf16)
    qkv_out[:, 2 * wide :] = (projected[:, 2 * wide :] + shifts[1:2]).astype(bf16)
    masks = head_masks()
    for g in range(here):
        rows = slice(g * SLOTS, (g + 1) * SLOTS)
        open_here = allowed[g] > 0.5
        for p in range(pairs):
            q, k, v = [qkv_out[rows, i * wide + p * PAIR : i * wide + (p + 1) * PAIR] for i in range(3)]
            raw = mm_nt(q, doubled(k, masks))
            parts = []
            for h in range(2):
                scores = jnp.where(open_here, raw[:, h * SLOTS : (h + 1) * SLOTS] * SCALE, far_value)
                exponent = jnp.exp(scores - jnp.max(scores, axis=-1, keepdims=True))
                inverse = 1.0 / jnp.sum(exponent, axis=-1, keepdims=True)
                parts.append((exponent * inverse).astype(bf16))
            probs = jnp.concatenate(parts, axis=1)
            probs_out[g, p] = probs
            mixed_out[rows, p * PAIR : (p + 1) * PAIR] = mm(probs, doubled(v, masks)).astype(bf16)
    total_out[...] = mm(mixed_out[...], out[...]).astype(bf16)


def attn_back_kernel(grad, qkv, out, qkv_in, probs_in, grads_out, total_out, mixed_grad, *, here, pairs):
    wide = pairs * PAIR
    mixed_grad[...] = mm_nt(grad[...], out[...]).astype(bf16)
    masks = head_masks()
    low_lanes = lax.broadcasted_iota(jnp.int32, (SLOTS, PAIR), 1) < HEAD_DIM
    for g in range(here):
        rows = slice(g * SLOTS, (g + 1) * SLOTS)
        for p in range(pairs):
            spans = [slice(i * wide + p * PAIR, i * wide + (p + 1) * PAIR) for i in range(3)]
            q, k, v = [qkv_in[rows, span] for span in spans]
            probs = probs_in[g, p]
            back = mixed_grad[rows, spans[0]]
            both = mm_tn(probs, back)
            grads_out[rows, spans[2]] = jnp.where(low_lanes, both[:SLOTS], both[SLOTS:]).astype(bf16)
            prob_grad = mm_nt(back, doubled(v, masks))
            weights = probs.astype(f32)
            product = weights * prob_grad
            parts = []
            for h in range(2):
                span = slice(h * SLOTS, (h + 1) * SLOTS)
                total = jnp.sum(product[:, span], axis=-1, keepdims=True)
                parts.append((product[:, span] - weights[:, span] * total).astype(bf16))
            score_grad = jnp.concatenate(parts, axis=1)
            grads_out[rows, spans[0]] = (SCALE * mm(score_grad, doubled(k, masks))).astype(bf16)
            both = SCALE * mm_tn(score_grad, q)
            grads_out[rows, spans[1]] = jnp.where(low_lanes, both[:SLOTS], both[SLOTS:]).astype(bf16)
    total_out[...] = mm(grads_out[...], qkv[...]).astype(bf16)


def attn_weights_kernel(normed_n, normed_f, grad_n, grad_f, mixed_n, mixed_f, dqkv_n, dqkv_f, mine_out, other_out, shifts_out, *, quarter):
    rest = quarter - PAIR
    wide = 2 * quarter
    for i in range(4):
        if i < 3:
            span = slice(i * wide, (i + 1) * wide)
            total = mm_tn(dqkv_n[:, span], normed_n[...]) + mm_tn(dqkv_f[:, span], normed_f[...])
        else:
            total = mm_tn(mixed_n[...], grad_n[...]) + mm_tn(mixed_f[...], grad_f[...])
        total = total.astype(bf16)
        base = i * quarter
        mine_out[base : base + PAIR, :] = total[:PAIR]
        mine_out[base + PAIR : base + quarter, :] = total[2 * PAIR : 2 * PAIR + rest]
        other_out[base : base + PAIR, :] = total[PAIR : 2 * PAIR]
        other_out[base + PAIR : base + quarter, :] = total[2 * PAIR + rest :]
    for j, i in enumerate((0, 2)):
        span = slice(i * wide, (i + 1) * wide)
        shifts_out[j : j + 1, :] = column(dqkv_n[:, span].astype(f32)) + column(dqkv_f[:, span].astype(f32))


def feed_kernel(normed, up_mine, up_other, shift_mine, shift_other, down_mine, down_other, hidden_out, slope_out, total_out, *, layer):
    hq = up_mine.shape[2]
    total = None
    for i, (up, shift, down) in enumerate(((up_mine, shift_mine, down_mine), (up_other, shift_other, down_other))):
        span = slice(i * hq, (i + 1) * hq)
        act, slope = gelu_pair(mm(normed[...], up[layer]) + shift[layer : layer + 1])
        hidden_out[:, span] = act.astype(bf16)
        slope_out[:, span] = slope.astype(bf16)
        part = mm(hidden_out[:, span], down[layer])
        total = part if total is None else total + part
    total_out[...] = total.astype(bf16)


def feed_back_kernel(grad, slope, up_mine, up_other, down_mine, down_other, pre_out, total_out, *, layer):
    hq = up_mine.shape[2]
    total = None
    for i, (up, down) in enumerate(((up_mine, down_mine), (up_other, down_other))):
        span = slice(i * hq, (i + 1) * hq)
        back = mm_nt(grad[...], down[layer]).astype(bf16).astype(f32)
        pre_out[:, span] = (back * slope[:, span].astype(f32)).astype(bf16)
        part = mm_nt(pre_out[:, span], up[layer])
        total = part if total is None else total + part
    total_out[...] = total.astype(bf16)


def down_weights_kernel(hidden_n, hidden_f, grad_n, grad_f, mine, other):
    hq = mine.shape[0]
    for i, out in enumerate((mine, other)):
        span = slice(i * hq, (i + 1) * hq)
        out[...] = (mm_tn(hidden_n[:, span], grad_n[...]) + mm_tn(hidden_f[:, span], grad_f[...])).astype(bf16)


def up_weights_kernel(normed_n, normed_f, pre_n, pre_f, mine, other, shifts_out):
    hq = mine.shape[1]
    for i, out in enumerate((mine, other)):
        span = slice(i * hq, (i + 1) * hq)
        out[...] = (mm_tn(normed_n[...], pre_n[:, span]) + mm_tn(normed_f[...], pre_f[:, span])).astype(bf16)
    shifts_out[...] = column(pre_n[...].astype(f32)) + column(pre_f[...].astype(f32))


def swap(value, axis, size, bit):
    return lax.ppermute(value, axis, [(i, i ^ bit) for i in range(size)])


def added_rows(left, right, start, height):
    return left[pl.ds(start, height), :].astype(f32) + right[pl.ds(start, height), :].astype(f32)


def split_kernel(flags, left, right, keep_out, send_out, *, step):
    half = keep_out.shape[0]
    keep_out[...] = added_rows(left, right, pl.multiple_of(flags[step] * half, 16), half).astype(bf16)
    send_out[...] = added_rows(left, right, pl.multiple_of((1 - flags[step]) * half, 16), half).astype(bf16)


def split_two_kernel(flags, left, left_other, right, right_other, keep_out, send_out):
    first = left[...].astype(f32) + left_other[...].astype(f32)
    second = right[...].astype(f32) + right_other[...].astype(f32)
    upper = flags[0] == 1
    keep_out[...] = jnp.where(upper, second, first).astype(bf16)
    send_out[...] = jnp.where(upper, first, second).astype(bf16)


def add_kernel(left, right, total_out):
    total_out[...] = (left[...].astype(f32) + right[...].astype(f32)).astype(total_out.dtype)


def join_kernel_rows(upper, lower, out):
    out[: upper.shape[0], :] = upper[...]
    out[upper.shape[0] :, :] = lower[...]


def with_cargo(out, rows, total):
    height = total.shape[0]
    high = total.astype(bf16)
    out[rows : rows + height, :] = high
    out[rows + height :, :] = (total - high.astype(f32)).astype(bf16)


def cargo_of(ref, rows):
    height = (ref.shape[0] - rows) // 2
    return ref[rows : rows + height, :].astype(f32) + ref[rows + height :, :].astype(f32)


def add_cargo_kernel(left, right, cargo, out):
    rows = left.shape[0]
    out[:rows, :] = (left[...].astype(f32) + right[...].astype(f32)).astype(bf16)
    with_cargo(out, rows, cargo[...])


def join_cargo_kernel(upper, lower, out, *, rows):
    out[:rows, :] = upper[:rows, :]
    out[rows : 2 * rows, :] = lower[:rows, :]
    with_cargo(out, 2 * rows, cargo_of(upper, rows) + cargo_of(lower, rows))


class Order:
    def __init__(self):
        self.token = None

    def tie(self, *values):
        return self.after(values)

    def after(self, values):
        if self.token is None:
            return values
        values, _ = lax.optimization_barrier((values, self.token))
        return values

    def run(self, kernel, outs, args, **more):
        results = call(kernel, outs, self.after(tuple(args)), **more)
        self.token = results[-1] if isinstance(results, (list, tuple)) else results
        return results


class Lanes:
    def __init__(self, orders, dp_size, tensor_size):
        self.orders, self.dp_size, self.tensor_size = orders, dp_size, tensor_size
        self.steps = len(orders[0])
        place = lax.axis_index("dp")
        odd = lax.axis_index("tensor") % 2
        flags = [jnp.where(odd == 1, (place // b) % 2, (place // a) % 2) for a, b in zip(*orders)]
        self.flags = jnp.stack(flags).astype(jnp.int32)

    def swap(self, value, step):
        pairs = [
            (d * self.tensor_size + t, (d ^ self.orders[t % 2][step]) * self.tensor_size + t)
            for d in range(self.dp_size)
            for t in range(self.tensor_size)
        ]
        return lax.ppermute(value, ("dp", "tensor"), pairs)


class Summed:
    def __init__(self, addends, lanes, order):
        self.addends, self.lanes, self.order = addends, lanes, order
        self.height = sum(entry[0].shape[0] for entry in addends)
        self.step = 0
        self.masks = [0]
        self.cargo = None

    def advance(self):
        lanes, steps, step = self.lanes, self.lanes.steps, self.step
        if step == 0 and len(self.addends) == 2:
            args = [entry for pair in self.addends for entry in pair]
        elif step == 0:
            args = list(self.addends[0])
        else:
            args = [self.held, self.got]
        height, width = args[0].shape
        traffic = 6 * height * width
        if step < steps:
            half = shape((self.height // (2 << step), width), bf16)
            work = split_two_kernel if len(args) == 4 else functools.partial(split_kernel, step=step)
            self.held, send = self.order.run(work, [half, half], (lanes.flags, *args), scalars=1, traffic=traffic)
            self.got = lanes.swap(send, step)
        elif self.cargo is not None:
            extra, rows = 2 * self.cargo.shape[0], self.height >> (2 * steps - step)
            if step == steps:
                work, args, out = add_cargo_kernel, (*args, self.cargo), rows
            else:
                work, out = functools.partial(join_cargo_kernel, rows=rows // 2), rows
            self.held = self.order.run(work, shape((out + extra, width), bf16), args, traffic=traffic)
        elif step == steps:
            self.held = self.order.run(add_kernel, shape((height, width), bf16), args, traffic=traffic)
        else:
            self.held = self.order.run(join_kernel_rows, shape((2 * height, width), bf16), args, traffic=traffic)
        if step >= steps:
            back = 2 * steps - 1 - step
            self.got = lanes.swap(self.held, back)
            self.masks = self.masks + [mask ^ (1 << back) for mask in self.masks]
        self.step += 1

    def finish(self):
        starts = []
        for mask in self.masks:
            start, span = 0, self.height
            for step in range(self.lanes.steps):
                span //= 2
                flag = self.lanes.flags[step]
                start = start + span * ((1 - flag) if mask >> step & 1 else flag)
            starts.append(start)
        return [self.held, self.got], starts


class Whole:
    def __init__(self, addends):
        totals = [call(add_kernel, shape(a.shape, bf16), (a, b)) for a, b in addends]
        self.total = lax.psum(jnp.concatenate(totals, axis=0), "dp")
        self.height = self.total.shape[0]

    def advance(self):
        pass

    def finish(self):
        return [self.total], [0]


def placed_parts(starts, refs, count, total, height):
    part = height // total
    for index in range(total):
        ref, j = refs[index // (total // count)], index % (total // count)
        yield pl.multiple_of(starts[index], 16), ref[j * part : (j + 1) * part, :]


def square_kernel(starts, *refs, count, total):
    down_out, up_out, whole = refs[-3:]
    for start, part in placed_parts(starts, refs[:count], count, total, whole.shape[0]):
        whole[pl.ds(start, part.shape[0]), :] = part
    height = down_out.shape[1]
    down_out[0] = whole[:height, :].astype(f32)
    up_out[0] = whole[height:, :].astype(f32)


def grouped_kernel(starts, *refs, count, total, quarter):
    qkv_out, out_out, whole = refs[-3:]
    for start, part in placed_parts(starts, refs[:count], count, total, whole.shape[0]):
        whole[pl.ds(start, part.shape[0]), :] = part
    for i in range(3):
        qkv_out[0, i] = whole[i * quarter : (i + 1) * quarter, :].astype(f32)
    out_out[0] = whole[3 * quarter :, :].astype(f32)


def at_layer(array_shape, layer):
    zeros = (0,) * (len(array_shape) - 1)
    return pl.BlockSpec((1,) + array_shape[1:], lambda i: (layer,) + zeros)


def layer_output(kernel, outs, item, layer, before, order):
    pieces, starts = item.finish()
    starts = jnp.stack([jnp.asarray(start, jnp.int32) for start in starts])
    count, total = len(pieces), starts.shape[0]
    before = before or []
    whole = [pl.BlockSpec(piece.shape, lambda i: (0, 0)) for piece in pieces]
    results = pl.pallas_call(
        functools.partial(kernel, count=count, total=total),
        out_shape=outs,
        grid=(1,),
        in_specs=[SCALARS] + whole + [pl.BlockSpec(memory_space=pl.ANY)] * len(before),
        out_specs=[at_layer(entry.shape, layer) for entry in outs],
        scratch_shapes=[pltpu.VMEM((item.height, pieces[0].shape[1]), bf16)],
        input_output_aliases={1 + count + i: i for i in range(len(before))},
        compiler_params=pltpu.CompilerParams(vmem_limit_bytes=24 << 20),
        cost_estimate=pl.CostEstimate(flops=0, bytes_accessed=sum(entry.size for entry in outs) * 48, transcendentals=0),
    )(starts, *order.after(tuple(pieces)), *before)
    if not before:
        order.token = results[-1]
    return results


def pack_kernel(*refs, quarter, hq):
    shared_out, mine_out, other_out = refs[-3:]
    rest = quarter - PAIR
    for layer in range(LAYERS):
        end, mid, feed, feed_row, up, qv = refs[layer * 5], refs[layer * 5 + 1], refs[layer * 5 + 2], 2 * (layer == 0), refs[layer * 5 + 3], refs[layer * 5 + 4]
        base = layer * 12
        shared_out[base : base + 1, :] = end[0:1]
        shared_out[base + 1 : base + 2, :] = mid[0:1]
        shared_out[base + 2 : base + 3, :] = end[1:2]
        shared_out[base + 3 : base + 4, :] = mid[1:2]
        shared_out[base + 4 : base + 6, :] = mid[2:4]
        shared_out[base + 6 : base + 8, :] = feed[feed_row : feed_row + 2]
        shared_out[base + 8 : base + 9, :] = mid[4:5]
        shared_out[base + 9 : base + 10, :] = feed[feed_row + 2 : feed_row + 3]
        shared_out[base + 10 : base + 12, :] = jnp.zeros_like(mid[0:2])
        for out, up_start, pair_start, rest_start in (
            (mine_out, 0, 0, 2 * PAIR),
            (other_out, hq, PAIR, 2 * PAIR + rest),
        ):
            base = layer * 4
            out[base : base + 4, :] = jnp.zeros_like(mid[0:4])
            out[base : base + 1, :hq] = up[0:1, up_start : up_start + hq]
            out[base + 1 : base + 3, :PAIR] = qv[0:2, pair_start : pair_start + PAIR]
            out[base + 1 : base + 3, PAIR : PAIR + rest] = qv[0:2, rest_start : rest_start + rest]


def unpack_kernel(held, got, gain, shift, qv, out, gates, up, down, *, quarter, hq, rows):
    total = held[...] if rows is None else cargo_of(held, rows) + cargo_of(got, rows)
    for layer in range(LAYERS):
        base = layer * 12
        gain[layer] = total[base : base + 2, :]
        shift[layer] = total[base + 2 : base + 4, :]
        gates[layer] = total[base + 4 : base + 8, :]
        out[layer : layer + 1, :] = total[base + 8 : base + 9, :]
        down[layer : layer + 1, :] = total[base + 9 : base + 10, :]
        base = LAYERS * 12 + layer * 4
        up[layer : layer + 1, :] = total[base : base + 1, :hq]
        qv[layer] = total[base + 1 : base + 3, :quarter]


def body(
    text_embed,
    vision_embed,
    region_mask,
    modality,
    doc_split,
    norm_gain,
    norm_bias,
    qkv_weight,
    qv_bias,
    out_weight,
    out_bias,
    gates,
    up_weight,
    up_bias,
    down_weight,
    down_bias,
    cotangent,
    dp_size,
    tensor_size,
):
    rows, width = text_embed.shape
    here = rows // SLOTS
    quarter = qkv_weight.shape[3]
    hq = up_weight.shape[2]
    wide = 2 * quarter
    pairs = wide // PAIR
    me = lax.axis_index("tensor")
    place = jnp.stack([me, me ^ 2]).astype(jnp.int32)

    def to_core(value):
        return swap(value, "tensor", tensor_size, 1)

    def to_side(value):
        return swap(value, "tensor", tensor_size, 2)

    kinds = modality.reshape(-1, SLOTS)
    reals = region_mask.reshape(-1, SLOTS)
    row_f32, row_bf16 = shape((rows, width), f32), shape((rows, width), bf16)
    wide_bf16, hidden_bf16 = shape((rows, wide), bf16), shape((rows, 2 * hq), bf16)
    sums = shape((8, width), f32)

    def from_hbm(*values):
        return tuple(pltpu.with_memory_space_constraint(value, pltpu.HBM) for value in values)

    state, normed, kind = call(
        functools.partial(start_kernel, here=here),
        [row_f32, row_bf16, shape((rows, 1), f32)],
        (place, *from_hbm(kinds, text_embed, vision_embed, norm_gain, norm_bias)),
        scalars=1,
        traffic=3 << 20,
    )
    inputs = [normed, to_side(normed)]
    qkv_weight = jnp.swapaxes(qkv_weight, 2, 3)
    qkv_other, out_other, qv_other = to_core(qkv_weight), to_core(out_weight), to_core(qv_bias)
    up_later, down_later, shift_later, inputs[1] = lax.optimization_barrier(
        (up_weight, down_weight, up_bias, inputs[1])
    )
    up_other, down_other, shift_other = to_core(up_later), to_core(down_later), to_core(shift_later)
    qv_all = jnp.concatenate(
        [qv_bias[..., :PAIR], qv_other[..., :PAIR], qv_bias[..., PAIR:], qv_other[..., PAIR:]], axis=-1
    )

    tile = shape((here, SLOTS, SLOTS), f32)
    near_cross, near_self, far_cross, far_self, feed_low = call(
        functools.partial(mask_kernel, here=here, layer=LAYERS - 1),
        [tile, tile, tile, tile, row_bf16],
        (place, doc_split, kinds, reals, cotangent, kind, gates),
        scalars=2,
        traffic=2 << 20,
    )
    masks = [(near_cross, far_cross), (near_self, far_self)]
    feed_far_low, _ = lax.optimization_barrier((feed_low, inputs[1]))
    feed_far_low = to_side(feed_far_low)

    joined_weights = [
        call(
            functools.partial(join_kernel, layer=layer, quarter=quarter),
            [shape((3 * wide, width), bf16), shape((wide, width), bf16)],
            (qkv_weight, qkv_other, out_weight, out_other),
            traffic=6 << 20,
        )
        for layer in range(LAYERS)
    ]
    triple = shape((rows, 3 * wide), bf16)

    def attend(value, layer, allowed):
        qkv, out = joined_weights[layer]
        return call(
            functools.partial(attn_kernel, here=here, pairs=pairs),
            [triple, shape((here, pairs, SLOTS, 2 * SLOTS), bf16), wide_bf16, row_bf16],
            (value, qkv, qv_all[layer], out, allowed),
            flops=2 * rows * width * wide * 4 + 4 * rows * SLOTS * wide * 2,
            traffic=5 << 20,
        )

    def attend_back(grad, layer, kept, run):
        qkv, out = joined_weights[layer]
        return run(
            functools.partial(attn_back_kernel, here=here, pairs=pairs),
            [triple, row_bf16],
            (grad, qkv, out, kept[0], kept[1]),
            flops=2 * rows * width * wide * 4 + 8 * rows * SLOTS * wide * 2,
            traffic=5 << 20,
            scratch=[pltpu.VMEM((rows, wide), bf16)],
        )

    def feed(value, layer):
        return call(
            functools.partial(feed_kernel, layer=layer),
            [hidden_bf16, hidden_bf16, row_bf16],
            (value, up_weight, up_other, up_bias, shift_other, down_weight, down_other),
            flops=2 * rows * width * 2 * hq * 2,
            traffic=7 << 20,
        )

    def feed_back(grad, slope, layer, run):
        return run(
            functools.partial(feed_back_kernel, layer=layer),
            [hidden_bf16, row_bf16],
            (grad, slope, up_weight, up_other, down_weight, down_other),
            flops=2 * rows * width * 2 * hq * 2,
            traffic=7 << 20,
        )

    def down_weights(hidden, grads, run):
        square = shape((hq, width), bf16)
        return run(
            down_weights_kernel,
            [square, square],
            (*hidden, *grads),
            flops=2 * rows * width * 2 * hq * 2,
            traffic=5 << 20,
        )

    def up_weights(normed, pre, run):
        across = shape((width, hq), bf16)
        return run(
            up_weights_kernel,
            [across, across, shape((1, 2 * hq), f32)],
            (*normed, *pre),
            flops=2 * rows * width * 2 * hq * 2,
            traffic=5 << 20,
        )

    def attn_weights(normed, grads, mixed, parts, run):
        grouped = shape((4 * quarter, width), bf16)
        return run(
            functools.partial(attn_weights_kernel, quarter=quarter),
            [grouped, grouped, shape((2, wide), f32)],
            (*normed, *grads, *mixed, *parts),
            flops=2 * 2 * rows * width * wide * 4,
            traffic=7 << 20,
        )

    saved = []
    for layer in range(LAYERS):
        near_mask, far_mask = masks[layer % 2]
        kept_near = attend(inputs[0], layer, near_mask)
        kept_far = attend(inputs[1], layer, far_mask)
        attn = (kept_near[3], to_side(kept_far[3]))
        middle, normed_ff = call(
            functools.partial(mid_kernel, layer=layer, branch=0),
            [row_f32, row_bf16],
            (state, *attn, out_bias, gates, kind, norm_gain, norm_bias),
            traffic=3 << 20,
        )
        inputs_ff = [normed_ff, to_side(normed_ff)]
        feed_near = feed(inputs_ff[0], layer)
        feed_far = feed(inputs_ff[1], layer)
        fed = (feed_near[2], feed_far[2] if layer == LAYERS - 1 else to_side(feed_far[2]))
        saved.append(
            (
                state,
                middle,
                attn,
                fed,
                inputs,
                inputs_ff,
                (kept_near, kept_far),
                (feed_near[0], feed_far[0]),
                (feed_near[1], feed_far[1]),
            )
        )
        if layer + 1 < LAYERS:
            state, normed = call(
                functools.partial(mid_kernel, layer=layer, branch=1),
                [row_f32, row_bf16],
                (middle, *fed, down_bias, gates, kind, norm_gain, norm_bias),
                traffic=3 << 20,
            )
            inputs = [normed, to_side(normed)]
    top = LAYERS - 1

    bits = [1 << b for b in range(dp_size.bit_length() - 1)]
    stepped = dp_size == 1 << len(bits) and width % (16 * dp_size) == 0 and len(bits) > 1
    order = Order()
    lanes = Lanes((bits, [bits[1], bits[0]] + bits[2:]), dp_size, tensor_size) if stepped else None
    straight = Lanes((bits, bits), dp_size, tensor_size) if stepped else None

    def summed(*addends, way=lanes):
        return Summed(addends, way, order) if stepped else Whole(addends)

    squares = [shape((LAYERS, hq, width), f32), shape((LAYERS, width, hq), f32)]
    grouped = [shape((LAYERS, 3, quarter, width), f32), shape((LAYERS, quarter, width), f32)]
    group_work = functools.partial(grouped_kernel, quarter=quarter)

    def back_mid(layer, near, far, upstream):
        _, middle, attn = saved[layer][:3]
        return order.run(
            functools.partial(back_mid_kernel, layer=layer),
            [row_f32, row_bf16, sums],
            (near, far, middle, upstream, kind, gates, norm_gain, *attn, out_bias),
            traffic=5 << 20,
        )

    def do_feed_back(side, layer, grad):
        return feed_back(grad, saved[layer][8][side], layer, order.run)

    def do_feed_weights(layer, grads, pre):
        _, _, _, _, _, inputs_ff, _, hidden, _ = saved[layer]
        down_mine, down_rest = down_weights(hidden, grads, order.run)
        down_rest = to_core(down_rest)
        up_mine, up_rest, shift_grad = up_weights(inputs_ff, pre, order.run)
        return summed((down_mine, down_rest), (up_mine, to_core(up_rest))), shift_grad

    def do_attn_back(side, layer, grad):
        return attend_back(grad, layer, saved[layer][6][side], order.run)

    def do_attn_weights(layer, grads, parts):
        kept, inputs = saved[layer][6], saved[layer][4]
        mine, rest, shift_grad = attn_weights(inputs, grads, (kept[0][2], kept[1][2]), parts, order.run)
        return summed((mine, to_core(rest)), way=straight if layer else lanes), shift_grad

    v = {"up1": cotangent}

    def fb_far(l):
        v["pf"], far = do_feed_back(1, l, v["low"][1])
        v["far"] = to_side(far)

    def fb_near(l):
        v["pn"], v["near"] = do_feed_back(0, l, v["low"][0])

    def down_w(l):
        mine, rest = down_weights(saved[l][7], v["low"], order.run)
        v["d"] = (mine, to_core(rest))

    def up_w(l):
        mine, rest, v["us%d" % l] = up_weights(saved[l][5], (v["pn"], v["pf"]), order.run)
        v["F%d" % l] = summed(v["d"], (mine, to_core(rest)))

    def mid_back(l):
        v["mg"], low, v["ms%d" % l] = back_mid(l, v["near"], v["far"], v["up%d" % l])
        v["low"] = [low, to_side(low)]

    def at_near(l):
        v["an"], v["near"] = do_attn_back(0, l, v["low"][0])

    def at_far(l):
        v["af"], far = do_attn_back(1, l, v["low"][1])
        v["far"] = to_side(far)

    def at_w(l):
        v["A%d" % l], v["qs%d" % l] = do_attn_weights(l, v["low"], (v["an"], v["af"]))

    def end_back(l):
        v["up0"], low, v["es1"] = order.run(
            functools.partial(back_end_kernel, layer=1),
            [row_f32, row_bf16, sums],
            (v["near"], v["far"], saved[1][0], v["mg"], kind, gates, norm_gain, *saved[0][3], down_bias),
            traffic=5 << 20,
        )
        v["low"] = [low, to_side(low)]

    def finish(l):
        v["text"], v["vision"], v["es0"] = order.run(
            finish_kernel,
            [row_f32, row_f32, sums],
            (v["near"], v["far"], saved[0][0], v["mg"], kind, norm_gain),
            traffic=5 << 20,
        )

    def send_fed(l):
        (later,) = order.tie(saved[1][3][1])
        v["fed"] = (saved[1][3][0], to_side(later))

    def last(l):
        v["joined"], v["fs"] = order.run(
            functools.partial(last_kernel, layer=1),
            [row_bf16, sums],
            (saved[1][1], *v["fed"], down_bias, gates, kind, cotangent),
            traffic=3 << 20,
        )

    head = LAYERS * 12

    def pack(l):
        packed = shape((LAYERS * 4, width), f32)
        small, mine, other = order.run(
            functools.partial(pack_kernel, quarter=quarter, hq=hq),
            [shape((head, width), f32), packed, packed],
            (
                v["es0"], v["ms0"], v["es1"], v["us0"], v["qs0"],
                v["es1"], v["ms1"], v["fs"], v["us1"], v["qs1"],
            ),
        )
        v["got"] = to_core(jnp.concatenate([small, other], axis=0))
        v["sum"] = jnp.concatenate([small, mine], axis=0)

    def little(step):
        v["sum"] = order.run(add_kernel, shape(v["sum"].shape, f32), (v["sum"], v["got"]))
        if step == 0:
            side = to_side(v["sum"][:head])
            v["got"] = jnp.concatenate([side, jnp.zeros_like(v["sum"][head:])], axis=0)
        elif stepped:
            v["A0"].cargo = v["sum"]
        else:
            v["sum"] = lax.psum(v["sum"], "dp")

    def out_feed(l):
        v["squares"] = layer_output(square_kernel, squares, v["F%d" % l], l, v.get("squares"), order)

    def out_attn(l):
        v["grouped"] = layer_output(group_work, grouped, v["A%d" % l], l, v.get("grouped"), order)

    v["low"] = [feed_low, feed_far_low]
    work = {
        "ff": fb_far, "fn": fb_near, "dw": down_w, "uw": up_w, "mb": mid_back, "an": at_near,
        "af": at_far, "aw": at_w, "eb": end_back, "fi": finish, "sf": send_fed, "la": last, "pk": pack,
        "s": little, "oF": out_feed, "oA": out_attn,
    }
    plan = (
        "ff1", "fn1", "dw1", "uw1", "mb1", "an1", "F1",
        "af1", "aw1", "F1",
        "eb1", "fn0", "A1", "F1",
        "ff0", "dw0", "uw0", "A1", "F1",
        "mb0", "an0", "A1", "F0", "F1",
        "af0", "aw0", "F0", "A1", "F1", "fi0", "A0", "sf1",
        "F0", "A1", "A0", "la1", "pk0", "s0", "A1", "s1", "oF1", "F0", "A0",
        "oA1", "F0", "A0", "F0", "A0", "A0", "oF0", "oA0",
    )
    for name in plan:
        if name[:-1] in work:
            work[name[:-1]](int(name[-1]))
        else:
            v[name].advance()
    joined, text_grad, vision_grad = v["joined"], v["text"], v["vision"]
    cargo, dp_rows = (v["sum"], v["sum"]), None
    if stepped:
        cargo, dp_rows = (v["A0"].held, v["A0"].got), v["A0"].height // 2
    down_grad, up_grad = v["squares"]
    qkv_grad, out_grad = v["grouped"]
    q = quarter
    flat = shape((LAYERS, width), f32)
    pair = shape((LAYERS, 2, width), f32)
    gain_grad, shift_grad, qv_grad, out_shift, gates_grad, up_shift, down_shift = call(
        functools.partial(unpack_kernel, quarter=q, hq=hq, rows=dp_rows),
        [pair, pair, shape((LAYERS, 2, q), f32), flat, shape((LAYERS, 4, width), f32), shape((LAYERS, hq), f32), flat],
        cargo,
    )
    return (
        joined,
        text_grad,
        vision_grad,
        gain_grad,
        shift_grad,
        jnp.swapaxes(qkv_grad, 2, 3),
        qv_grad,
        out_grad,
        out_shift,
        gates_grad,
        up_grad,
        up_shift,
        down_grad,
        down_shift,
    )


def solution(mesh):
    sizes = dict(mesh.shape)

    def run(*arrays):
        return body(*arrays, dp_size=sizes["dp"], tensor_size=sizes["tensor"])

    placed = (
        P(("dp", "tensor"), None),
        P(("dp", "tensor"), None),
        P("dp"),
        P("dp"),
        P("dp"),
        P(),
        P(),
        P(None, None, None, "tensor"),
        P(None, None, "tensor"),
        P(None, "tensor", None),
        P(),
        P(),
        P(None, None, "tensor"),
        P(None, "tensor"),
        P(None, "tensor", None),
        P(),
        P(("dp", "tensor"), None),
    )
    return jax.shard_map(
        run,
        mesh=mesh,
        in_specs=placed,
        out_specs=(
            P(("dp", "tensor"), None),
            P(("dp", "tensor"), None),
            P(("dp", "tensor"), None),
            P(),
            P(),
            P(None, None, None, "tensor"),
            P(None, None, "tensor"),
            P(None, "tensor", None),
            P(),
            P(),
            P(None, None, "tensor"),
            P(None, "tensor"),
            P(None, "tensor", None),
            P(),
        ),
        check_vma=False,
    )
```

```python
import functools

import jax
import jax.numpy as jnp
from jax import lax
from jax.experimental import pallas as pl
from jax.experimental.pallas import tpu as pltpu
from jax.sharding import PartitionSpec as P

HEAD_DIM = 64
LAYERS = 2
SLOTS = 128
SCALE = HEAD_DIM ** (-0.5)
PAIR = 2 * HEAD_DIM

epsilon = 1e-05
far_value = -1000000000.0
bf16 = jnp.bfloat16
f32 = jnp.float32


def logistic(values):
    return 1.0 / (1.0 + jnp.exp(-values))


def gelu_pair(values):
    size = jnp.abs(values)
    base = 1.0 + 0.23164189 * size
    t = pl.reciprocal(base, approx=True)
    t = t * (2.0 - base * t)
    bell = jnp.exp(-0.5 * (values * values))
    series = 0.5307027145 * t - 0.7265760135
    series = series * t + 0.7107068705
    series = series * t - 0.142248368
    series = series * t + 0.127414796
    tail = series * t * bell
    cdf = jnp.where(values < 0.0, tail, 1.0 - tail)
    return values * cdf, cdf + 0.3989422804014327 * (values * bell)


def norm_parts(values):
    center = values - jnp.mean(values, axis=-1, keepdims=True)
    spread = jnp.mean(center * center, axis=-1, keepdims=True)
    scale = lax.rsqrt(spread + epsilon)
    return center * scale, scale


def norm_back(grad, xhat, scale, gain):
    scaled = grad * gain
    inner = jnp.mean(scaled, axis=-1, keepdims=True)
    cross = jnp.mean(scaled * xhat, axis=-1, keepdims=True)
    return scale * (scaled - inner - xhat * cross)


def column(values):
    return jnp.sum(values, axis=0, keepdims=True)


def mm(left, right):
    return jnp.dot(left, right, preferred_element_type=f32)


def mm_nt(left, right):
    return lax.dot_general(left, right, (((1,), (1,)), ((), ())), preferred_element_type=f32)


def mm_tn(left, right):
    return lax.dot_general(left, right, (((0,), (0,)), ((), ())), preferred_element_type=f32)


def shape(dims, kind):
    return jax.ShapeDtypeStruct(dims, kind)


def call(kernel, outs, args, flops=0, traffic=1 << 20, scalars=0, scratch=(), room=20):
    return pl.pallas_call(
        kernel,
        out_shape=outs,
        in_specs=[SCALARS] * scalars + [WHOLE] * (len(args) - scalars),
        scratch_shapes=scratch,
        compiler_params=pltpu.CompilerParams(vmem_limit_bytes=room << 20),
        cost_estimate=pl.CostEstimate(flops=16 * flops, bytes_accessed=16 * traffic, transcendentals=0),
    )(*args)


SCALARS = pl.BlockSpec(memory_space=pltpu.SMEM)
WHOLE = pl.BlockSpec(memory_space=pltpu.VMEM)


def as_column(row):
    across = lax.broadcasted_iota(jnp.int32, (SLOTS, SLOTS), 1)
    down = lax.broadcasted_iota(jnp.int32, (SLOTS, SLOTS), 0)
    return jnp.sum(jnp.where(across == down, row, 0.0), axis=1, keepdims=True)


def gate_of(gates, layer, index, vision):
    return jnp.where(
        vision, logistic(gates[layer, index + 1 : index + 2]), logistic(gates[layer, index : index + 1])
    )


def start_kernel(place, kinds, text, vision, gain, shift, state_out, normed_out, kind_out, *, here):
    for g in range(here):
        span = slice(g * SLOTS, (g + 1) * SLOTS)
        kind = as_column(kinds[pl.ds(place[0] * here + g, 1), :].astype(f32))
        kind_out[span, :] = kind
        state = jnp.where(kind > 0.5, vision[span, :].astype(f32), text[span, :].astype(f32))
        state_out[span, :] = state
        xhat, _ = norm_parts(state)
        normed_out[span, :] = (xhat * gain[0, 0:1] + shift[0, 0:1]).astype(bf16)


def mask_kernel(place, splits, kinds, reals, cotangent, kind, gates, near_cross, near_self, far_cross, far_self, feed_out, *, here, layer):
    across = lax.broadcasted_iota(jnp.int32, (SLOTS, SLOTS), 1) // (SLOTS // 2)
    down = lax.broadcasted_iota(jnp.int32, (SLOTS, SLOTS), 0) // (SLOTS // 2)
    block = jnp.where(across == down, 1.0, 0.0)
    for side, (cross_out, self_out) in enumerate(((near_cross, near_self), (far_cross, far_self))):
        for g in range(here):
            index = place[side] * here + g
            row = kinds[pl.ds(index, 1), :].astype(f32)
            real = reals[pl.ds(index, 1), :].astype(f32)
            split = (splits[index] != 0).astype(f32)
            within = jnp.maximum(block, 1.0 - split) * jnp.where(real == 1.0, 1.0, 0.0)
            self_out[g] = within
            cross_out[g] = jnp.where(as_column(row) != row, within, 0.0)
    gate = gate_of(gates, layer, 2, kind[...] > 0.5)
    feed_out[...] = (cotangent[...].astype(f32) * gate).astype(bf16)


def mid_kernel(state, near, far, bias, gates, kind, gain, shift, state_out, normed_out, *, layer, branch):
    total = near[...].astype(f32) + far[...].astype(f32) + bias[layer : layer + 1]
    gate = gate_of(gates, layer, 2 * branch, kind[...] > 0.5)
    value = state[...] + gate * total
    state_out[...] = value
    xhat, _ = norm_parts(value)
    nl, ni = (layer, 1) if branch == 0 else (layer + 1, 0)
    normed_out[...] = (xhat * gain[nl, ni : ni + 1] + shift[nl, ni : ni + 1]).astype(bf16)


def gate_sums(grad, total, gate, vision):
    full = grad * total * (1.0 - gate)
    return [column(jnp.where(vision, 0.0, full)), column(jnp.where(vision, full, 0.0))]


def put_rows(out, rows):
    rows = rows + [jnp.zeros_like(rows[0])] * (8 - len(rows))
    for i, row in enumerate(rows):
        out[i : i + 1, :] = row


def last_kernel(state, near, far, bias, gates, kind, cotangent, joined_out, sums_out, *, layer):
    total = near[...].astype(f32) + far[...].astype(f32) + bias[layer : layer + 1]
    vision = kind[...] > 0.5
    gate = gate_of(gates, layer, 2, vision)
    joined_out[...] = (state[...] + gate * total).astype(bf16)
    grad = cotangent[...].astype(f32) * gate
    sums = gate_sums(grad, total, gate, vision)
    put_rows(sums_out, sums + [column(grad.astype(bf16).astype(f32))])


def back_mid_kernel(near, far, middle, upstream, kind, gates, gain, attn_near, attn_far, bias, grad_out, low_out, sums_out, *, layer):
    grad = near[...].astype(f32) + far[...].astype(f32)
    xhat, scale = norm_parts(middle[...])
    total = norm_back(grad, xhat, scale, gain[layer, 1:2]) + upstream[...].astype(f32)
    grad_out[...] = total
    vision = kind[...] > 0.5
    gate = gate_of(gates, layer, 0, vision)
    branch = total * gate
    low = branch.astype(bf16)
    low_out[...] = low
    attn = attn_near[...].astype(f32) + attn_far[...].astype(f32) + bias[layer : layer + 1]
    put_rows(
        sums_out,
        [column(grad * xhat), column(grad)]
        + gate_sums(branch, attn, gate, vision)
        + [column(low.astype(f32))],
    )


def back_end_kernel(near, far, state, middle_grad, kind, gates, gain, feed_near, feed_far, bias, grad_out, low_out, sums_out, *, layer):
    grad = near[...].astype(f32) + far[...].astype(f32)
    xhat, scale = norm_parts(state[...])
    total = norm_back(grad, xhat, scale, gain[layer, 0:1]) + middle_grad[...]
    grad_out[...] = total
    vision = kind[...] > 0.5
    below = layer - 1
    gate = gate_of(gates, below, 2, vision)
    branch = total * gate
    low = branch.astype(bf16)
    low_out[...] = low
    feed = feed_near[...].astype(f32) + feed_far[...].astype(f32) + bias[below : below + 1]
    put_rows(
        sums_out,
        [column(grad * xhat), column(grad)]
        + gate_sums(branch, feed, gate, vision)
        + [column(low.astype(f32))],
    )


def finish_kernel(near, far, state, middle_grad, kind, gain, text_out, vision_out, sums_out):
    grad = near[...].astype(f32) + far[...].astype(f32)
    xhat, scale = norm_parts(state[...])
    total = norm_back(grad, xhat, scale, gain[0, 0:1]) + middle_grad[...]
    vision = kind[...] > 0.5
    text_out[...] = jnp.where(vision, 0.0, total)
    vision_out[...] = jnp.where(vision, total, 0.0)
    put_rows(sums_out, [column(grad * xhat), column(grad)])


def head_masks():
    lane = lax.broadcasted_iota(jnp.int32, (1, PAIR), 1)
    low = (lane < HEAD_DIM).astype(f32)
    return low.astype(bf16), (1.0 - low).astype(bf16)


def doubled(value, masks):
    return jnp.concatenate([value * masks[0], value * masks[1]], axis=0)


def join_kernel(qkv_mine, qkv_other, out_mine, out_other, qkv, out, *, layer, quarter):
    rest = quarter - PAIR
    sources = [(qkv_mine[layer, i], qkv_other[layer, i], qkv, 2 * quarter * i) for i in range(3)]
    sources.append((out_mine[layer], out_other[layer], out, 0))
    for mine, other, joined, base in sources:
        joined[base : base + PAIR, :] = mine[:PAIR]
        joined[base + PAIR : base + 2 * PAIR, :] = other[:PAIR]
        joined[base + 2 * PAIR : base + 2 * PAIR + rest, :] = mine[PAIR:]
        joined[base + 2 * PAIR + rest : base + 2 * quarter, :] = other[PAIR:]


def attn_kernel(normed, qkv, shifts, out, allowed, qkv_out, probs_out, mixed_out, total_out, *, here, pairs):
    wide = pairs * PAIR
    projected = mm_nt(normed[...], qkv[...])
    qkv_out[:, :wide] = (projected[:, :wide] + shifts[0:1]).astype(bf16)
    qkv_out[:, wide : 2 * wide] = projected[:, wide : 2 * wide].astype(bf16)
    qkv_out[:, 2 * wide :] = (projected[:, 2 * wide :] + shifts[1:2]).astype(bf16)
    masks = head_masks()
    for g in range(here):
        rows = slice(g * SLOTS, (g + 1) * SLOTS)
        open_here = allowed[g] > 0.5
        for p in range(pairs):
            q, k, v = [qkv_out[rows, i * wide + p * PAIR : i * wide + (p + 1) * PAIR] for i in range(3)]
            raw = mm_nt(q, doubled(k, masks))
            parts = []
            for h in range(2):
                scores = jnp.where(open_here, raw[:, h * SLOTS : (h + 1) * SLOTS] * SCALE, far_value)
                exponent = jnp.exp(scores - jnp.max(scores, axis=-1, keepdims=True))
                inverse = 1.0 / jnp.sum(exponent, axis=-1, keepdims=True)
                parts.append((exponent * inverse).astype(bf16))
            probs = jnp.concatenate(parts, axis=1)
            probs_out[g, p] = probs
            mixed_out[rows, p * PAIR : (p + 1) * PAIR] = mm(probs, doubled(v, masks)).astype(bf16)
    total_out[...] = mm(mixed_out[...], out[...]).astype(bf16)


def attn_back_kernel(grad, qkv, out, qkv_in, probs_in, grads_out, total_out, mixed_grad, *, here, pairs):
    wide = pairs * PAIR
    mixed_grad[...] = mm_nt(grad[...], out[...]).astype(bf16)
    masks = head_masks()
    low_lanes = lax.broadcasted_iota(jnp.int32, (SLOTS, PAIR), 1) < HEAD_DIM
    for g in range(here):
        rows = slice(g * SLOTS, (g + 1) * SLOTS)
        for p in range(pairs):
            spans = [slice(i * wide + p * PAIR, i * wide + (p + 1) * PAIR) for i in range(3)]
            q, k, v = [qkv_in[rows, span] for span in spans]
            probs = probs_in[g, p]
            back = mixed_grad[rows, spans[0]]
            both = mm_tn(probs, back)
            grads_out[rows, spans[2]] = jnp.where(low_lanes, both[:SLOTS], both[SLOTS:]).astype(bf16)
            prob_grad = mm_nt(back, doubled(v, masks))
            weights = probs.astype(f32)
            product = weights * prob_grad
            parts = []
            for h in range(2):
                span = slice(h * SLOTS, (h + 1) * SLOTS)
                total = jnp.sum(product[:, span], axis=-1, keepdims=True)
                parts.append((product[:, span] - weights[:, span] * total).astype(bf16))
            score_grad = jnp.concatenate(parts, axis=1)
            grads_out[rows, spans[0]] = (SCALE * mm(score_grad, doubled(k, masks))).astype(bf16)
            both = SCALE * mm_tn(score_grad, q)
            grads_out[rows, spans[1]] = jnp.where(low_lanes, both[:SLOTS], both[SLOTS:]).astype(bf16)
    total_out[...] = mm(grads_out[...], qkv[...]).astype(bf16)


def attn_weights_kernel(normed_n, normed_f, grad_n, grad_f, mixed_n, mixed_f, dqkv_n, dqkv_f, mine_out, other_out, shifts_out, *, quarter):
    rest = quarter - PAIR
    wide = 2 * quarter
    for i in range(4):
        if i < 3:
            span = slice(i * wide, (i + 1) * wide)
            total = mm_tn(dqkv_n[:, span], normed_n[...]) + mm_tn(dqkv_f[:, span], normed_f[...])
        else:
            total = mm_tn(mixed_n[...], grad_n[...]) + mm_tn(mixed_f[...], grad_f[...])
        total = total.astype(bf16)
        base = i * quarter
        mine_out[base : base + PAIR, :] = total[:PAIR]
        mine_out[base + PAIR : base + quarter, :] = total[2 * PAIR : 2 * PAIR + rest]
        other_out[base : base + PAIR, :] = total[PAIR : 2 * PAIR]
        other_out[base + PAIR : base + quarter, :] = total[2 * PAIR + rest :]
    for j, i in enumerate((0, 2)):
        span = slice(i * wide, (i + 1) * wide)
        shifts_out[j : j + 1, :] = column(dqkv_n[:, span].astype(f32)) + column(dqkv_f[:, span].astype(f32))


def feed_kernel(normed, up_mine, up_other, shift_mine, shift_other, down_mine, down_other, hidden_out, slope_out, total_out, *, layer):
    hq = up_mine.shape[2]
    total = None
    for i, (up, shift, down) in enumerate(((up_mine, shift_mine, down_mine), (up_other, shift_other, down_other))):
        span = slice(i * hq, (i + 1) * hq)
        act, slope = gelu_pair(mm(normed[...], up[layer]) + shift[layer : layer + 1])
        hidden_out[:, span] = act.astype(bf16)
        slope_out[:, span] = slope.astype(bf16)
        part = mm(hidden_out[:, span], down[layer])
        total = part if total is None else total + part
    total_out[...] = total.astype(bf16)


def feed_back_kernel(grad, slope, up_mine, up_other, down_mine, down_other, pre_out, total_out, *, layer):
    hq = up_mine.shape[2]
    total = None
    for i, (up, down) in enumerate(((up_mine, down_mine), (up_other, down_other))):
        span = slice(i * hq, (i + 1) * hq)
        back = mm_nt(grad[...], down[layer]).astype(bf16).astype(f32)
        pre_out[:, span] = (back * slope[:, span].astype(f32)).astype(bf16)
        part = mm_nt(pre_out[:, span], up[layer])
        total = part if total is None else total + part
    total_out[...] = total.astype(bf16)


def down_weights_kernel(hidden_n, hidden_f, grad_n, grad_f, mine, other):
    hq = mine.shape[0]
    for i, out in enumerate((mine, other)):
        span = slice(i * hq, (i + 1) * hq)
        out[...] = (mm_tn(hidden_n[:, span], grad_n[...]) + mm_tn(hidden_f[:, span], grad_f[...])).astype(bf16)


def up_weights_kernel(normed_n, normed_f, pre_n, pre_f, mine, other, shifts_out):
    hq = mine.shape[1]
    for i, out in enumerate((mine, other)):
        span = slice(i * hq, (i + 1) * hq)
        out[...] = (mm_tn(normed_n[...], pre_n[:, span]) + mm_tn(normed_f[...], pre_f[:, span])).astype(bf16)
    shifts_out[...] = column(pre_n[...].astype(f32)) + column(pre_f[...].astype(f32))


def swap(value, axis, size, bit):
    return lax.ppermute(value, axis, [(i, i ^ bit) for i in range(size)])


def added_rows(left, right, start, height):
    return left[pl.ds(start, height), :].astype(f32) + right[pl.ds(start, height), :].astype(f32)


def split_kernel(flags, left, right, keep_out, send_out, *, step):
    half = keep_out.shape[0]
    keep_out[...] = added_rows(left, right, pl.multiple_of(flags[step] * half, 16), half).astype(bf16)
    send_out[...] = added_rows(left, right, pl.multiple_of((1 - flags[step]) * half, 16), half).astype(bf16)


def split_two_kernel(flags, left, left_other, right, right_other, keep_out, send_out):
    first = left[...].astype(f32) + left_other[...].astype(f32)
    second = right[...].astype(f32) + right_other[...].astype(f32)
    upper = flags[0] == 1
    keep_out[...] = jnp.where(upper, second, first).astype(bf16)
    send_out[...] = jnp.where(upper, first, second).astype(bf16)


def add_kernel(left, right, total_out):
    total_out[...] = (left[...].astype(f32) + right[...].astype(f32)).astype(total_out.dtype)


def join_kernel_rows(upper, lower, out):
    out[: upper.shape[0], :] = upper[...]
    out[upper.shape[0] :, :] = lower[...]


def with_cargo(out, rows, total):
    height = total.shape[0]
    high = total.astype(bf16)
    out[rows : rows + height, :] = high
    out[rows + height :, :] = (total - high.astype(f32)).astype(bf16)


def cargo_of(ref, rows):
    height = (ref.shape[0] - rows) // 2
    return ref[rows : rows + height, :].astype(f32) + ref[rows + height :, :].astype(f32)


def add_cargo_kernel(left, right, cargo, out):
    rows = left.shape[0]
    out[:rows, :] = (left[...].astype(f32) + right[...].astype(f32)).astype(bf16)
    with_cargo(out, rows, cargo[...])


def join_cargo_kernel(upper, lower, out, *, rows):
    out[:rows, :] = upper[:rows, :]
    out[rows : 2 * rows, :] = lower[:rows, :]
    with_cargo(out, 2 * rows, cargo_of(upper, rows) + cargo_of(lower, rows))


class Order:
    def __init__(self):
        self.token = None

    def tie(self, *values):
        return self.after(values)

    def after(self, values):
        if self.token is None:
            return values
        values, _ = lax.optimization_barrier((values, self.token))
        return values

    def run(self, kernel, outs, args, **more):
        results = call(kernel, outs, self.after(tuple(args)), **more)
        self.token = results[-1] if isinstance(results, (list, tuple)) else results
        return results


class Lanes:
    def __init__(self, orders, dp_size, tensor_size):
        self.orders, self.dp_size, self.tensor_size = orders, dp_size, tensor_size
        self.steps = len(orders[0])
        place = lax.axis_index("dp")
        odd = lax.axis_index("tensor") % 2
        flags = [jnp.where(odd == 1, (place // b) % 2, (place // a) % 2) for a, b in zip(*orders)]
        self.flags = jnp.stack(flags).astype(jnp.int32)

    def swap(self, value, step):
        pairs = [
            (d * self.tensor_size + t, (d ^ self.orders[t % 2][step]) * self.tensor_size + t)
            for d in range(self.dp_size)
            for t in range(self.tensor_size)
        ]
        return lax.ppermute(value, ("dp", "tensor"), pairs)


class Summed:
    def __init__(self, addends, lanes, order):
        self.addends, self.lanes, self.order = addends, lanes, order
        self.height = sum(entry[0].shape[0] for entry in addends)
        self.step = 0
        self.masks = [0]
        self.cargo = None

    def advance(self):
        lanes, steps, step = self.lanes, self.lanes.steps, self.step
        if step == 0 and len(self.addends) == 2:
            args = [entry for pair in self.addends for entry in pair]
        elif step == 0:
            args = list(self.addends[0])
        else:
            args = [self.held, self.got]
        height, width = args[0].shape
        traffic = 6 * height * width
        if step < steps:
            half = shape((self.height // (2 << step), width), bf16)
            work = split_two_kernel if len(args) == 4 else functools.partial(split_kernel, step=step)
            self.held, send = self.order.run(work, [half, half], (lanes.flags, *args), scalars=1, traffic=traffic)
            self.got = lanes.swap(send, step)
        elif self.cargo is not None:
            extra, rows = 2 * self.cargo.shape[0], self.height >> (2 * steps - step)
            if step == steps:
                work, args, out = add_cargo_kernel, (*args, self.cargo), rows
            else:
                work, out = functools.partial(join_cargo_kernel, rows=rows // 2), rows
            self.held = self.order.run(work, shape((out + extra, width), bf16), args, traffic=traffic)
        elif step == steps:
            self.held = self.order.run(add_kernel, shape((height, width), bf16), args, traffic=traffic)
        else:
            self.held = self.order.run(join_kernel_rows, shape((2 * height, width), bf16), args, traffic=traffic)
        if step >= steps:
            back = 2 * steps - 1 - step
            self.got = lanes.swap(self.held, back)
            self.masks = self.masks + [mask ^ (1 << back) for mask in self.masks]
        self.step += 1

    def finish(self):
        starts = []
        for mask in self.masks:
            start, span = 0, self.height
            for step in range(self.lanes.steps):
                span //= 2
                flag = self.lanes.flags[step]
                start = start + span * ((1 - flag) if mask >> step & 1 else flag)
            starts.append(start)
        return [self.held, self.got], starts


class Whole:
    def __init__(self, addends):
        totals = [call(add_kernel, shape(a.shape, bf16), (a, b)) for a, b in addends]
        self.total = lax.psum(jnp.concatenate(totals, axis=0), "dp")
        self.height = self.total.shape[0]

    def advance(self):
        pass

    def finish(self):
        return [self.total], [0]


def placed_parts(starts, refs, count, total, height):
    part = height // total
    for index in range(total):
        ref, j = refs[index // (total // count)], index % (total // count)
        yield pl.multiple_of(starts[index], 16), ref[j * part : (j + 1) * part, :]


def square_kernel(starts, *refs, count, total):
    down_out, up_out, whole = refs[-3:]
    for start, part in placed_parts(starts, refs[:count], count, total, whole.shape[0]):
        whole[pl.ds(start, part.shape[0]), :] = part
    height = down_out.shape[1]
    down_out[0] = whole[:height, :].astype(f32)
    up_out[0] = whole[height:, :].astype(f32)


def grouped_kernel(starts, *refs, count, total, quarter):
    qkv_out, out_out, whole = refs[-3:]
    for start, part in placed_parts(starts, refs[:count], count, total, whole.shape[0]):
        whole[pl.ds(start, part.shape[0]), :] = part
    for i in range(3):
        qkv_out[0, i] = whole[i * quarter : (i + 1) * quarter, :].astype(f32)
    out_out[0] = whole[3 * quarter :, :].astype(f32)


def at_layer(array_shape, layer):
    zeros = (0,) * (len(array_shape) - 1)
    return pl.BlockSpec((1,) + array_shape[1:], lambda i: (layer,) + zeros)


def layer_output(kernel, outs, item, layer, before, order):
    pieces, starts = item.finish()
    starts = jnp.stack([jnp.asarray(start, jnp.int32) for start in starts])
    count, total = len(pieces), starts.shape[0]
    before = before or []
    whole = [pl.BlockSpec(piece.shape, lambda i: (0, 0)) for piece in pieces]
    results = pl.pallas_call(
        functools.partial(kernel, count=count, total=total),
        out_shape=outs,
        grid=(1,),
        in_specs=[SCALARS] + whole + [pl.BlockSpec(memory_space=pl.ANY)] * len(before),
        out_specs=[at_layer(entry.shape, layer) for entry in outs],
        scratch_shapes=[pltpu.VMEM((item.height, pieces[0].shape[1]), bf16)],
        input_output_aliases={1 + count + i: i for i in range(len(before))},
        compiler_params=pltpu.CompilerParams(vmem_limit_bytes=24 << 20),
        cost_estimate=pl.CostEstimate(flops=0, bytes_accessed=sum(entry.size for entry in outs) * 48, transcendentals=0),
    )(starts, *order.after(tuple(pieces)), *before)
    if not before:
        order.token = results[-1]
    return results


def pack_kernel(*refs, quarter, hq):
    shared_out, mine_out, other_out = refs[-3:]
    rest = quarter - PAIR
    for layer in range(LAYERS):
        end, mid, feed, feed_row, up, qv = refs[layer * 5], refs[layer * 5 + 1], refs[layer * 5 + 2], 2 * (layer == 0), refs[layer * 5 + 3], refs[layer * 5 + 4]
        base = layer * 12
        shared_out[base : base + 1, :] = end[0:1]
        shared_out[base + 1 : base + 2, :] = mid[0:1]
        shared_out[base + 2 : base + 3, :] = end[1:2]
        shared_out[base + 3 : base + 4, :] = mid[1:2]
        shared_out[base + 4 : base + 6, :] = mid[2:4]
        shared_out[base + 6 : base + 8, :] = feed[feed_row : feed_row + 2]
        shared_out[base + 8 : base + 9, :] = mid[4:5]
        shared_out[base + 9 : base + 10, :] = feed[feed_row + 2 : feed_row + 3]
        shared_out[base + 10 : base + 12, :] = jnp.zeros_like(mid[0:2])
        for out, up_start, pair_start, rest_start in (
            (mine_out, 0, 0, 2 * PAIR),
            (other_out, hq, PAIR, 2 * PAIR + rest),
        ):
            base = layer * 4
            out[base : base + 4, :] = jnp.zeros_like(mid[0:4])
            out[base : base + 1, :hq] = up[0:1, up_start : up_start + hq]
            out[base + 1 : base + 3, :PAIR] = qv[0:2, pair_start : pair_start + PAIR]
            out[base + 1 : base + 3, PAIR : PAIR + rest] = qv[0:2, rest_start : rest_start + rest]


def unpack_kernel(held, got, gain, shift, qv, out, gates, up, down, *, quarter, hq, rows):
    total = held[...] if rows is None else cargo_of(held, rows) + cargo_of(got, rows)
    for layer in range(LAYERS):
        base = layer * 12
        gain[layer] = total[base : base + 2, :]
        shift[layer] = total[base + 2 : base + 4, :]
        gates[layer] = total[base + 4 : base + 8, :]
        out[layer : layer + 1, :] = total[base + 8 : base + 9, :]
        down[layer : layer + 1, :] = total[base + 9 : base + 10, :]
        base = LAYERS * 12 + layer * 4
        up[layer : layer + 1, :] = total[base : base + 1, :hq]
        qv[layer] = total[base + 1 : base + 3, :quarter]


def body(
    text_embed,
    vision_embed,
    region_mask,
    modality,
    doc_split,
    norm_gain,
    norm_bias,
    qkv_weight,
    qv_bias,
    out_weight,
    out_bias,
    gates,
    up_weight,
    up_bias,
    down_weight,
    down_bias,
    cotangent,
    dp_size,
    tensor_size,
):
    rows, width = text_embed.shape
    here = rows // SLOTS
    quarter = qkv_weight.shape[3]
    hq = up_weight.shape[2]
    wide = 2 * quarter
    pairs = wide // PAIR
    me = lax.axis_index("tensor")
    place = jnp.stack([me, me ^ 2]).astype(jnp.int32)

    def to_core(value):
        return swap(value, "tensor", tensor_size, 1)

    def to_side(value):
        return swap(value, "tensor", tensor_size, 2)

    kinds = modality.reshape(-1, SLOTS)
    reals = region_mask.reshape(-1, SLOTS)
    row_f32, row_bf16 = shape((rows, width), f32), shape((rows, width), bf16)
    wide_bf16, hidden_bf16 = shape((rows, wide), bf16), shape((rows, 2 * hq), bf16)
    sums = shape((8, width), f32)

    def from_hbm(*values):
        return tuple(pltpu.with_memory_space_constraint(value, pltpu.HBM) for value in values)

    state, normed, kind = call(
        functools.partial(start_kernel, here=here),
        [row_f32, row_bf16, shape((rows, 1), f32)],
        (place, *from_hbm(kinds, text_embed, vision_embed, norm_gain, norm_bias)),
        scalars=1,
        traffic=3 << 20,
    )
    inputs = [normed, to_side(normed)]
    qkv_weight = jnp.swapaxes(qkv_weight, 2, 3)
    qkv_other, out_other, qv_other = to_core(qkv_weight), to_core(out_weight), to_core(qv_bias)
    up_later, down_later, shift_later, inputs[1] = lax.optimization_barrier(
        (up_weight, down_weight, up_bias, inputs[1])
    )
    up_other, down_other, shift_other = to_core(up_later), to_core(down_later), to_core(shift_later)
    qv_all = jnp.concatenate(
        [qv_bias[..., :PAIR], qv_other[..., :PAIR], qv_bias[..., PAIR:], qv_other[..., PAIR:]], axis=-1
    )

    tile = shape((here, SLOTS, SLOTS), f32)
    near_cross, near_self, far_cross, far_self, feed_low = call(
        functools.partial(mask_kernel, here=here, layer=LAYERS - 1),
        [tile, tile, tile, tile, row_bf16],
        (place, doc_split, kinds, reals, cotangent, kind, gates),
        scalars=2,
        traffic=2 << 20,
    )
    masks = [(near_cross, far_cross), (near_self, far_self)]
    feed_far_low, _ = lax.optimization_barrier((feed_low, inputs[1]))
    feed_far_low = to_side(feed_far_low)

    joined_weights = [
        call(
            functools.partial(join_kernel, layer=layer, quarter=quarter),
            [shape((3 * wide, width), bf16), shape((wide, width), bf16)],
            (qkv_weight, qkv_other, out_weight, out_other),
            traffic=6 << 20,
        )
        for layer in range(LAYERS)
    ]
    triple = shape((rows, 3 * wide), bf16)

    def attend(value, layer, allowed):
        qkv, out = joined_weights[layer]
        return call(
            functools.partial(attn_kernel, here=here, pairs=pairs),
            [triple, shape((here, pairs, SLOTS, 2 * SLOTS), bf16), wide_bf16, row_bf16],
            (value, qkv, qv_all[layer], out, allowed),
            flops=2 * rows * width * wide * 4 + 4 * rows * SLOTS * wide * 2,
            traffic=5 << 20,
        )

    def attend_back(grad, layer, kept, run):
        qkv, out = joined_weights[layer]
        return run(
            functools.partial(attn_back_kernel, here=here, pairs=pairs),
            [triple, row_bf16],
            (grad, qkv, out, kept[0], kept[1]),
            flops=2 * rows * width * wide * 4 + 8 * rows * SLOTS * wide * 2,
            traffic=5 << 20,
            scratch=[pltpu.VMEM((rows, wide), bf16)],
        )

    def feed(value, layer):
        return call(
            functools.partial(feed_kernel, layer=layer),
            [hidden_bf16, hidden_bf16, row_bf16],
            (value, up_weight, up_other, up_bias, shift_other, down_weight, down_other),
            flops=2 * rows * width * 2 * hq * 2,
            traffic=7 << 20,
        )

    def feed_back(grad, slope, layer, run):
        return run(
            functools.partial(feed_back_kernel, layer=layer),
            [hidden_bf16, row_bf16],
            (grad, slope, up_weight, up_other, down_weight, down_other),
            flops=2 * rows * width * 2 * hq * 2,
            traffic=7 << 20,
        )

    def down_weights(hidden, grads, run):
        square = shape((hq, width), bf16)
        return run(
            down_weights_kernel,
            [square, square],
            (*hidden, *grads),
            flops=2 * rows * width * 2 * hq * 2,
            traffic=5 << 20,
        )

    def up_weights(normed, pre, run):
        across = shape((width, hq), bf16)
        return run(
            up_weights_kernel,
            [across, across, shape((1, 2 * hq), f32)],
            (*normed, *pre),
            flops=2 * rows * width * 2 * hq * 2,
            traffic=5 << 20,
        )

    def attn_weights(normed, grads, mixed, parts, run):
        grouped = shape((4 * quarter, width), bf16)
        return run(
            functools.partial(attn_weights_kernel, quarter=quarter),
            [grouped, grouped, shape((2, wide), f32)],
            (*normed, *grads, *mixed, *parts),
            flops=2 * 2 * rows * width * wide * 4,
            traffic=7 << 20,
        )

    saved = []
    for layer in range(LAYERS):
        near_mask, far_mask = masks[layer % 2]
        kept_near = attend(inputs[0], layer, near_mask)
        kept_far = attend(inputs[1], layer, far_mask)
        attn = (kept_near[3], to_side(kept_far[3]))
        middle, normed_ff = call(
            functools.partial(mid_kernel, layer=layer, branch=0),
            [row_f32, row_bf16],
            (state, *attn, out_bias, gates, kind, norm_gain, norm_bias),
            traffic=3 << 20,
        )
        inputs_ff = [normed_ff, to_side(normed_ff)]
        feed_near = feed(inputs_ff[0], layer)
        feed_far = feed(inputs_ff[1], layer)
        fed = (feed_near[2], feed_far[2] if layer == LAYERS - 1 else to_side(feed_far[2]))
        saved.append(
            (
                state,
                middle,
                attn,
                fed,
                inputs,
                inputs_ff,
                (kept_near, kept_far),
                (feed_near[0], feed_far[0]),
                (feed_near[1], feed_far[1]),
            )
        )
        if layer + 1 < LAYERS:
            state, normed = call(
                functools.partial(mid_kernel, layer=layer, branch=1),
                [row_f32, row_bf16],
                (middle, *fed, down_bias, gates, kind, norm_gain, norm_bias),
                traffic=3 << 20,
            )
            inputs = [normed, to_side(normed)]
    top = LAYERS - 1

    bits = [1 << b for b in range(dp_size.bit_length() - 1)]
    stepped = dp_size == 1 << len(bits) and width % (16 * dp_size) == 0 and len(bits) > 1
    order = Order()
    lanes = Lanes((bits, [bits[1], bits[0]] + bits[2:]), dp_size, tensor_size) if stepped else None
    straight = Lanes((bits, bits), dp_size, tensor_size) if stepped else None

    def summed(*addends, way=lanes):
        return Summed(addends, way, order) if stepped else Whole(addends)

    squares = [shape((LAYERS, hq, width), f32), shape((LAYERS, width, hq), f32)]
    grouped = [shape((LAYERS, 3, quarter, width), f32), shape((LAYERS, quarter, width), f32)]
    group_work = functools.partial(grouped_kernel, quarter=quarter)

    def back_mid(layer, near, far, upstream):
        _, middle, attn = saved[layer][:3]
        return order.run(
            functools.partial(back_mid_kernel, layer=layer),
            [row_f32, row_bf16, sums],
            (near, far, middle, upstream, kind, gates, norm_gain, *attn, out_bias),
            traffic=5 << 20,
        )

    def do_feed_back(side, layer, grad):
        return feed_back(grad, saved[layer][8][side], layer, order.run)

    def do_feed_weights(layer, grads, pre):
        _, _, _, _, _, inputs_ff, _, hidden, _ = saved[layer]
        down_mine, down_rest = down_weights(hidden, grads, order.run)
        down_rest = to_core(down_rest)
        up_mine, up_rest, shift_grad = up_weights(inputs_ff, pre, order.run)
        return summed((down_mine, down_rest), (up_mine, to_core(up_rest))), shift_grad

    def do_attn_back(side, layer, grad):
        return attend_back(grad, layer, saved[layer][6][side], order.run)

    def do_attn_weights(layer, grads, parts):
        kept, inputs = saved[layer][6], saved[layer][4]
        mine, rest, shift_grad = attn_weights(inputs, grads, (kept[0][2], kept[1][2]), parts, order.run)
        return summed((mine, to_core(rest)), way=straight if layer else lanes), shift_grad

    v = {"up1": cotangent}

    def fb_far(l):
        v["pf"], far = do_feed_back(1, l, v["low"][1])
        v["far"] = to_side(far)

    def fb_near(l):
        v["pn"], v["near"] = do_feed_back(0, l, v["low"][0])

    def down_w(l):
        mine, rest = down_weights(saved[l][7], v["low"], order.run)
        v["d"] = (mine, to_core(rest))

    def up_w(l):
        mine, rest, v["us%d" % l] = up_weights(saved[l][5], (v["pn"], v["pf"]), order.run)
        v["F%d" % l] = summed(v["d"], (mine, to_core(rest)), way=lanes)

    def mid_back(l):
        v["mg"], low, v["ms%d" % l] = back_mid(l, v["near"], v["far"], v["up%d" % l])
        v["low"] = [low, to_side(low)]

    def at_near(l):
        v["an"], v["near"] = do_attn_back(0, l, v["low"][0])

    def at_far(l):
        v["af"], far = do_attn_back(1, l, v["low"][1])
        v["far"] = to_side(far)

    def at_w(l):
        v["A%d" % l], v["qs%d" % l] = do_attn_weights(l, v["low"], (v["an"], v["af"]))

    def end_back(l):
        v["up0"], low, v["es1"] = order.run(
            functools.partial(back_end_kernel, layer=1),
            [row_f32, row_bf16, sums],
            (v["near"], v["far"], saved[1][0], v["mg"], kind, gates, norm_gain, *saved[0][3], down_bias),
            traffic=5 << 20,
        )
        v["low"] = [low, to_side(low)]

    def finish(l):
        v["text"], v["vision"], v["es0"] = order.run(
            finish_kernel,
            [row_f32, row_f32, sums],
            (v["near"], v["far"], saved[0][0], v["mg"], kind, norm_gain),
            traffic=5 << 20,
        )

    def send_fed(l):
        (later,) = order.tie(saved[1][3][1])
        v["fed"] = (saved[1][3][0], to_side(later))

    def last(l):
        v["joined"], v["fs"] = order.run(
            functools.partial(last_kernel, layer=1),
            [row_bf16, sums],
            (saved[1][1], *v["fed"], down_bias, gates, kind, cotangent),
            traffic=3 << 20,
        )

    head = LAYERS * 12

    def pack(l):
        packed = shape((LAYERS * 4, width), f32)
        small, mine, other = order.run(
            functools.partial(pack_kernel, quarter=quarter, hq=hq),
            [shape((head, width), f32), packed, packed],
            (
                v["es0"], v["ms0"], v["es1"], v["us0"], v["qs0"],
                v["es1"], v["ms1"], v["fs"], v["us1"], v["qs1"],
            ),
        )
        v["got"] = to_core(jnp.concatenate([small, other], axis=0))
        v["sum"] = jnp.concatenate([small, mine], axis=0)

    def little(step):
        v["sum"] = order.run(add_kernel, shape(v["sum"].shape, f32), (v["sum"], v["got"]))
        if step == 0:
            side = to_side(v["sum"][:head])
            v["got"] = jnp.concatenate([side, jnp.zeros_like(v["sum"][head:])], axis=0)
        elif stepped:
            v["A0"].cargo = v["sum"]
        else:
            v["sum"] = lax.psum(v["sum"], "dp")

    def out_feed(l):
        v["squares"] = layer_output(square_kernel, squares, v["F%d" % l], l, v.get("squares"), order)

    def out_attn(l):
        v["grouped"] = layer_output(group_work, grouped, v["A%d" % l], l, v.get("grouped"), order)

    v["low"] = [feed_low, feed_far_low]
    work = {
        "ff": fb_far, "fn": fb_near, "dw": down_w, "uw": up_w, "mb": mid_back, "an": at_near,
        "af": at_far, "aw": at_w, "eb": end_back, "fi": finish, "sf": send_fed, "la": last, "pk": pack,
        "s": little, "oF": out_feed, "oA": out_attn,
    }
    plan = (
        "ff1", "fn1", "dw1", "uw1", "mb1", "an1", "F1", "af1", "aw1", "F1", "eb1", "fn0", "A1", "F1", "ff0", "dw0", "uw0", "A1", "F1", "mb0", "an0", "F0", "F1", "A1", "af0", "aw0", "F0", "A1", "A0", "F0", "fi0", "A0", "sf1", "A1", "F0", "F1", "la1", "pk0", "A1", "s0", "F0", "A0", "s1", "oA1", "A0", "F0", "oF1", "A0", "A0", "oF0", "oA0",
    )
    for name in plan:
        if name[:-1] in work:
            work[name[:-1]](int(name[-1]))
        else:
            v[name].advance()
    joined, text_grad, vision_grad = v["joined"], v["text"], v["vision"]
    cargo, dp_rows = (v["sum"], v["sum"]), None
    if stepped:
        cargo, dp_rows = (v["A0"].held, v["A0"].got), v["A0"].height // 2
    down_grad, up_grad = v["squares"]
    qkv_grad, out_grad = v["grouped"]
    q = quarter
    flat = shape((LAYERS, width), f32)
    pair = shape((LAYERS, 2, width), f32)
    gain_grad, shift_grad, qv_grad, out_shift, gates_grad, up_shift, down_shift = call(
        functools.partial(unpack_kernel, quarter=q, hq=hq, rows=dp_rows),
        [pair, pair, shape((LAYERS, 2, q), f32), flat, shape((LAYERS, 4, width), f32), shape((LAYERS, hq), f32), flat],
        cargo,
    )
    return (
        joined,
        text_grad,
        vision_grad,
        gain_grad,
        shift_grad,
        jnp.swapaxes(qkv_grad, 2, 3),
        qv_grad,
        out_grad,
        out_shift,
        gates_grad,
        up_grad,
        up_shift,
        down_grad,
        down_shift,
    )


def solution(mesh):
    sizes = dict(mesh.shape)

    def run(*arrays):
        return body(*arrays, dp_size=sizes["dp"], tensor_size=sizes["tensor"])

    placed = (
        P(("dp", "tensor"), None),
        P(("dp", "tensor"), None),
        P("dp"),
        P("dp"),
        P("dp"),
        P(),
        P(),
        P(None, None, None, "tensor"),
        P(None, None, "tensor"),
        P(None, "tensor", None),
        P(),
        P(),
        P(None, None, "tensor"),
        P(None, "tensor"),
        P(None, "tensor", None),
        P(),
        P(("dp", "tensor"), None),
    )
    return jax.shard_map(
        run,
        mesh=mesh,
        in_specs=placed,
        out_specs=(
            P(("dp", "tensor"), None),
            P(("dp", "tensor"), None),
            P(("dp", "tensor"), None),
            P(),
            P(),
            P(None, None, None, "tensor"),
            P(None, None, "tensor"),
            P(None, "tensor", None),
            P(),
            P(),
            P(None, None, "tensor"),
            P(None, "tensor"),
            P(None, "tensor", None),
            P(),
        ),
        check_vma=False,
    )
```

```python
import functools

import jax
import jax.numpy as jnp
from jax import lax
from jax.experimental import pallas as pl
from jax.experimental.pallas import tpu as pltpu
from jax.sharding import PartitionSpec as P

HEAD_DIM = 64
LAYERS = 2
SLOTS = 128
SCALE = HEAD_DIM ** (-0.5)
PAIR = 2 * HEAD_DIM

epsilon = 1e-05
far_value = -1000000000.0
bf16 = jnp.bfloat16
f32 = jnp.float32


def logistic(values):
    return 1.0 / (1.0 + jnp.exp(-values))


def gelu_pair(values):
    size = jnp.abs(values)
    base = 1.0 + 0.23164189 * size
    t = pl.reciprocal(base, approx=True)
    t = t * (2.0 - base * t)
    bell = jnp.exp(-0.5 * (values * values))
    series = 0.5307027145 * t - 0.7265760135
    series = series * t + 0.7107068705
    series = series * t - 0.142248368
    series = series * t + 0.127414796
    tail = series * t * bell
    cdf = jnp.where(values < 0.0, tail, 1.0 - tail)
    return values * cdf, cdf + 0.3989422804014327 * (values * bell)


def norm_parts(values):
    center = values - jnp.mean(values, axis=-1, keepdims=True)
    spread = jnp.mean(center * center, axis=-1, keepdims=True)
    scale = lax.rsqrt(spread + epsilon)
    return center * scale, scale


def norm_back(grad, xhat, scale, gain):
    scaled = grad * gain
    inner = jnp.mean(scaled, axis=-1, keepdims=True)
    cross = jnp.mean(scaled * xhat, axis=-1, keepdims=True)
    return scale * (scaled - inner - xhat * cross)


def column(values):
    return jnp.sum(values, axis=0, keepdims=True)


def mm(left, right):
    return jnp.dot(left, right, preferred_element_type=f32)


def mm_nt(left, right):
    return lax.dot_general(left, right, (((1,), (1,)), ((), ())), preferred_element_type=f32)


def mm_tn(left, right):
    return lax.dot_general(left, right, (((0,), (0,)), ((), ())), preferred_element_type=f32)


def shape(dims, kind):
    return jax.ShapeDtypeStruct(dims, kind)


def call(kernel, outs, args, flops=0, traffic=1 << 20, scalars=0, scratch=(), room=20):
    return pl.pallas_call(
        kernel,
        out_shape=outs,
        in_specs=[SCALARS] * scalars + [WHOLE] * (len(args) - scalars),
        scratch_shapes=scratch,
        compiler_params=pltpu.CompilerParams(vmem_limit_bytes=room << 20),
        cost_estimate=pl.CostEstimate(flops=16 * flops, bytes_accessed=16 * traffic, transcendentals=0),
    )(*args)


SCALARS = pl.BlockSpec(memory_space=pltpu.SMEM)
WHOLE = pl.BlockSpec(memory_space=pltpu.VMEM)


def as_column(row):
    across = lax.broadcasted_iota(jnp.int32, (SLOTS, SLOTS), 1)
    down = lax.broadcasted_iota(jnp.int32, (SLOTS, SLOTS), 0)
    return jnp.sum(jnp.where(across == down, row, 0.0), axis=1, keepdims=True)


def gate_of(gates, layer, index, vision):
    return jnp.where(
        vision, logistic(gates[layer, index + 1 : index + 2]), logistic(gates[layer, index : index + 1])
    )


def start_kernel(place, kinds, text, vision, gain, shift, state_out, normed_out, kind_out, *, here):
    for g in range(here):
        span = slice(g * SLOTS, (g + 1) * SLOTS)
        kind = as_column(kinds[pl.ds(place[0] * here + g, 1), :].astype(f32))
        kind_out[span, :] = kind
        state = jnp.where(kind > 0.5, vision[span, :].astype(f32), text[span, :].astype(f32))
        state_out[span, :] = state
        xhat, _ = norm_parts(state)
        normed_out[span, :] = (xhat * gain[0, 0:1] + shift[0, 0:1]).astype(bf16)


def mask_kernel(place, splits, kinds, reals, cotangent, kind, gates, near_cross, near_self, far_cross, far_self, feed_out, *, here, layer):
    across = lax.broadcasted_iota(jnp.int32, (SLOTS, SLOTS), 1) // (SLOTS // 2)
    down = lax.broadcasted_iota(jnp.int32, (SLOTS, SLOTS), 0) // (SLOTS // 2)
    block = jnp.where(across == down, 1.0, 0.0)
    for side, (cross_out, self_out) in enumerate(((near_cross, near_self), (far_cross, far_self))):
        for g in range(here):
            index = place[side] * here + g
            row = kinds[pl.ds(index, 1), :].astype(f32)
            real = reals[pl.ds(index, 1), :].astype(f32)
            split = (splits[index] != 0).astype(f32)
            within = jnp.maximum(block, 1.0 - split) * jnp.where(real == 1.0, 1.0, 0.0)
            self_out[g] = within
            cross_out[g] = jnp.where(as_column(row) != row, within, 0.0)
    gate = gate_of(gates, layer, 2, kind[...] > 0.5)
    feed_out[...] = (cotangent[...].astype(f32) * gate).astype(bf16)


def mid_kernel(state, near, far, bias, gates, kind, gain, shift, state_out, normed_out, *, layer, branch):
    total = near[...].astype(f32) + far[...].astype(f32) + bias[layer : layer + 1]
    gate = gate_of(gates, layer, 2 * branch, kind[...] > 0.5)
    value = state[...] + gate * total
    state_out[...] = value
    xhat, _ = norm_parts(value)
    nl, ni = (layer, 1) if branch == 0 else (layer + 1, 0)
    normed_out[...] = (xhat * gain[nl, ni : ni + 1] + shift[nl, ni : ni + 1]).astype(bf16)


def gate_sums(grad, total, gate, vision):
    full = grad * total * (1.0 - gate)
    return [column(jnp.where(vision, 0.0, full)), column(jnp.where(vision, full, 0.0))]


def put_rows(out, rows):
    rows = rows + [jnp.zeros_like(rows[0])] * (8 - len(rows))
    for i, row in enumerate(rows):
        out[i : i + 1, :] = row


def last_kernel(state, near, far, bias, gates, kind, cotangent, joined_out, sums_out, *, layer):
    total = near[...].astype(f32) + far[...].astype(f32) + bias[layer : layer + 1]
    vision = kind[...] > 0.5
    gate = gate_of(gates, layer, 2, vision)
    joined_out[...] = (state[...] + gate * total).astype(bf16)
    grad = cotangent[...].astype(f32) * gate
    sums = gate_sums(grad, total, gate, vision)
    put_rows(sums_out, sums + [column(grad.astype(bf16).astype(f32))])


def back_mid_kernel(near, far, middle, upstream, kind, gates, gain, attn_near, attn_far, bias, grad_out, low_out, sums_out, *, layer):
    grad = near[...].astype(f32) + far[...].astype(f32)
    xhat, scale = norm_parts(middle[...])
    total = norm_back(grad, xhat, scale, gain[layer, 1:2]) + upstream[...].astype(f32)
    grad_out[...] = total
    vision = kind[...] > 0.5
    gate = gate_of(gates, layer, 0, vision)
    branch = total * gate
    low = branch.astype(bf16)
    low_out[...] = low
    attn = attn_near[...].astype(f32) + attn_far[...].astype(f32) + bias[layer : layer + 1]
    put_rows(
        sums_out,
        [column(grad * xhat), column(grad)]
        + gate_sums(branch, attn, gate, vision)
        + [column(low.astype(f32))],
    )


def back_end_kernel(near, far, state, middle_grad, kind, gates, gain, feed_near, feed_far, bias, grad_out, low_out, sums_out, *, layer):
    grad = near[...].astype(f32) + far[...].astype(f32)
    xhat, scale = norm_parts(state[...])
    total = norm_back(grad, xhat, scale, gain[layer, 0:1]) + middle_grad[...]
    grad_out[...] = total
    vision = kind[...] > 0.5
    below = layer - 1
    gate = gate_of(gates, below, 2, vision)
    branch = total * gate
    low = branch.astype(bf16)
    low_out[...] = low
    feed = feed_near[...].astype(f32) + feed_far[...].astype(f32) + bias[below : below + 1]
    put_rows(
        sums_out,
        [column(grad * xhat), column(grad)]
        + gate_sums(branch, feed, gate, vision)
        + [column(low.astype(f32))],
    )


def finish_kernel(near, far, state, middle_grad, kind, gain, text_out, vision_out, sums_out):
    grad = near[...].astype(f32) + far[...].astype(f32)
    xhat, scale = norm_parts(state[...])
    total = norm_back(grad, xhat, scale, gain[0, 0:1]) + middle_grad[...]
    vision = kind[...] > 0.5
    text_out[...] = jnp.where(vision, 0.0, total)
    vision_out[...] = jnp.where(vision, total, 0.0)
    put_rows(sums_out, [column(grad * xhat), column(grad)])


def head_masks():
    lane = lax.broadcasted_iota(jnp.int32, (1, PAIR), 1)
    low = (lane < HEAD_DIM).astype(f32)
    return low.astype(bf16), (1.0 - low).astype(bf16)


def doubled(value, masks):
    return jnp.concatenate([value * masks[0], value * masks[1]], axis=0)


def join_kernel(qkv_mine, qkv_other, out_mine, out_other, qkv, out, *, layer, quarter):
    rest = quarter - PAIR
    sources = [(qkv_mine[layer, i], qkv_other[layer, i], qkv, 2 * quarter * i) for i in range(3)]
    sources.append((out_mine[layer], out_other[layer], out, 0))
    for mine, other, joined, base in sources:
        joined[base : base + PAIR, :] = mine[:PAIR]
        joined[base + PAIR : base + 2 * PAIR, :] = other[:PAIR]
        joined[base + 2 * PAIR : base + 2 * PAIR + rest, :] = mine[PAIR:]
        joined[base + 2 * PAIR + rest : base + 2 * quarter, :] = other[PAIR:]


def attn_kernel(normed, qkv, shifts, out, allowed, qkv_out, probs_out, mixed_out, total_out, *, here, pairs):
    wide = pairs * PAIR
    projected = mm_nt(normed[...], qkv[...])
    qkv_out[:, :wide] = (projected[:, :wide] + shifts[0:1]).astype(bf16)
    qkv_out[:, wide : 2 * wide] = projected[:, wide : 2 * wide].astype(bf16)
    qkv_out[:, 2 * wide :] = (projected[:, 2 * wide :] + shifts[1:2]).astype(bf16)
    masks = head_masks()
    for g in range(here):
        rows = slice(g * SLOTS, (g + 1) * SLOTS)
        open_here = allowed[g] > 0.5
        for p in range(pairs):
            q, k, v = [qkv_out[rows, i * wide + p * PAIR : i * wide + (p + 1) * PAIR] for i in range(3)]
            raw = mm_nt(q, doubled(k, masks))
            parts = []
            for h in range(2):
                scores = jnp.where(open_here, raw[:, h * SLOTS : (h + 1) * SLOTS] * SCALE, far_value)
                exponent = jnp.exp(scores - jnp.max(scores, axis=-1, keepdims=True))
                inverse = 1.0 / jnp.sum(exponent, axis=-1, keepdims=True)
                parts.append((exponent * inverse).astype(bf16))
            probs = jnp.concatenate(parts, axis=1)
            probs_out[g, p] = probs
            mixed_out[rows, p * PAIR : (p + 1) * PAIR] = mm(probs, doubled(v, masks)).astype(bf16)
    total_out[...] = mm(mixed_out[...], out[...]).astype(bf16)


def attn_back_kernel(grad, qkv, out, qkv_in, probs_in, grads_out, total_out, mixed_grad, *, here, pairs):
    wide = pairs * PAIR
    mixed_grad[...] = mm_nt(grad[...], out[...]).astype(bf16)
    masks = head_masks()
    low_lanes = lax.broadcasted_iota(jnp.int32, (SLOTS, PAIR), 1) < HEAD_DIM
    for g in range(here):
        rows = slice(g * SLOTS, (g + 1) * SLOTS)
        for p in range(pairs):
            spans = [slice(i * wide + p * PAIR, i * wide + (p + 1) * PAIR) for i in range(3)]
            q, k, v = [qkv_in[rows, span] for span in spans]
            probs = probs_in[g, p]
            back = mixed_grad[rows, spans[0]]
            both = mm_tn(probs, back)
            grads_out[rows, spans[2]] = jnp.where(low_lanes, both[:SLOTS], both[SLOTS:]).astype(bf16)
            prob_grad = mm_nt(back, doubled(v, masks))
            weights = probs.astype(f32)
            product = weights * prob_grad
            parts = []
            for h in range(2):
                span = slice(h * SLOTS, (h + 1) * SLOTS)
                total = jnp.sum(product[:, span], axis=-1, keepdims=True)
                parts.append((product[:, span] - weights[:, span] * total).astype(bf16))
            score_grad = jnp.concatenate(parts, axis=1)
            grads_out[rows, spans[0]] = (SCALE * mm(score_grad, doubled(k, masks))).astype(bf16)
            both = SCALE * mm_tn(score_grad, q)
            grads_out[rows, spans[1]] = jnp.where(low_lanes, both[:SLOTS], both[SLOTS:]).astype(bf16)
    total_out[...] = mm(grads_out[...], qkv[...]).astype(bf16)


def attn_weights_kernel(normed_n, normed_f, grad_n, grad_f, mixed_n, mixed_f, dqkv_n, dqkv_f, mine_out, other_out, shifts_out, *, quarter):
    rest = quarter - PAIR
    wide = 2 * quarter
    for i in range(4):
        if i < 3:
            span = slice(i * wide, (i + 1) * wide)
            total = mm_tn(dqkv_n[:, span], normed_n[...]) + mm_tn(dqkv_f[:, span], normed_f[...])
        else:
            total = mm_tn(mixed_n[...], grad_n[...]) + mm_tn(mixed_f[...], grad_f[...])
        total = total.astype(bf16)
        base = i * quarter
        mine_out[base : base + PAIR, :] = total[:PAIR]
        mine_out[base + PAIR : base + quarter, :] = total[2 * PAIR : 2 * PAIR + rest]
        other_out[base : base + PAIR, :] = total[PAIR : 2 * PAIR]
        other_out[base + PAIR : base + quarter, :] = total[2 * PAIR + rest :]
    for j, i in enumerate((0, 2)):
        span = slice(i * wide, (i + 1) * wide)
        shifts_out[j : j + 1, :] = column(dqkv_n[:, span].astype(f32)) + column(dqkv_f[:, span].astype(f32))


def feed_kernel(normed, up_mine, up_other, shift_mine, shift_other, down_mine, down_other, hidden_out, slope_out, total_out, *, layer):
    hq = up_mine.shape[2]
    total = None
    for i, (up, shift, down) in enumerate(((up_mine, shift_mine, down_mine), (up_other, shift_other, down_other))):
        span = slice(i * hq, (i + 1) * hq)
        act, slope = gelu_pair(mm(normed[...], up[layer]) + shift[layer : layer + 1])
        hidden_out[:, span] = act.astype(bf16)
        slope_out[:, span] = slope.astype(bf16)
        part = mm(hidden_out[:, span], down[layer])
        total = part if total is None else total + part
    total_out[...] = total.astype(bf16)


def feed_back_kernel(grad, slope, up_mine, up_other, down_mine, down_other, pre_out, total_out, *, layer):
    hq = up_mine.shape[2]
    total = None
    for i, (up, down) in enumerate(((up_mine, down_mine), (up_other, down_other))):
        span = slice(i * hq, (i + 1) * hq)
        back = mm_nt(grad[...], down[layer]).astype(bf16).astype(f32)
        pre_out[:, span] = (back * slope[:, span].astype(f32)).astype(bf16)
        part = mm_nt(pre_out[:, span], up[layer])
        total = part if total is None else total + part
    total_out[...] = total.astype(bf16)


def down_weights_kernel(hidden_n, hidden_f, grad_n, grad_f, mine, other):
    hq = mine.shape[0]
    for i, out in enumerate((mine, other)):
        span = slice(i * hq, (i + 1) * hq)
        out[...] = (mm_tn(hidden_n[:, span], grad_n[...]) + mm_tn(hidden_f[:, span], grad_f[...])).astype(bf16)


def up_weights_kernel(normed_n, normed_f, pre_n, pre_f, mine, other, shifts_out):
    hq = mine.shape[1]
    for i, out in enumerate((mine, other)):
        span = slice(i * hq, (i + 1) * hq)
        out[...] = (mm_tn(normed_n[...], pre_n[:, span]) + mm_tn(normed_f[...], pre_f[:, span])).astype(bf16)
    shifts_out[...] = column(pre_n[...].astype(f32)) + column(pre_f[...].astype(f32))


def swap(value, axis, size, bit):
    return lax.ppermute(value, axis, [(i, i ^ bit) for i in range(size)])


def added_rows(left, right, start, height):
    return left[pl.ds(start, height), :].astype(f32) + right[pl.ds(start, height), :].astype(f32)


def split_kernel(flags, left, right, keep_out, send_out, *, step):
    half = keep_out.shape[0]
    keep_out[...] = added_rows(left, right, pl.multiple_of(flags[step] * half, 16), half).astype(bf16)
    send_out[...] = added_rows(left, right, pl.multiple_of((1 - flags[step]) * half, 16), half).astype(bf16)


def split_two_kernel(flags, left, left_other, right, right_other, keep_out, send_out):
    first = left[...].astype(f32) + left_other[...].astype(f32)
    second = right[...].astype(f32) + right_other[...].astype(f32)
    upper = flags[0] == 1
    keep_out[...] = jnp.where(upper, second, first).astype(bf16)
    send_out[...] = jnp.where(upper, first, second).astype(bf16)


def add_kernel(left, right, total_out):
    total_out[...] = (left[...].astype(f32) + right[...].astype(f32)).astype(total_out.dtype)


def join_kernel_rows(upper, lower, out):
    out[: upper.shape[0], :] = upper[...]
    out[upper.shape[0] :, :] = lower[...]


def with_cargo(out, rows, total):
    height = total.shape[0]
    high = total.astype(bf16)
    out[rows : rows + height, :] = high
    out[rows + height :, :] = (total - high.astype(f32)).astype(bf16)


def cargo_of(ref, rows):
    height = (ref.shape[0] - rows) // 2
    return ref[rows : rows + height, :].astype(f32) + ref[rows + height :, :].astype(f32)


def add_cargo_kernel(left, right, cargo, out):
    rows = left.shape[0]
    out[:rows, :] = (left[...].astype(f32) + right[...].astype(f32)).astype(bf16)
    with_cargo(out, rows, cargo[...])


def join_cargo_kernel(upper, lower, out, *, rows):
    out[:rows, :] = upper[:rows, :]
    out[rows : 2 * rows, :] = lower[:rows, :]
    with_cargo(out, 2 * rows, cargo_of(upper, rows) + cargo_of(lower, rows))


class Order:
    def __init__(self):
        self.token = None

    def tie(self, *values):
        return self.after(values)

    def after(self, values):
        if self.token is None:
            return values
        values, _ = lax.optimization_barrier((values, self.token))
        return values

    def run(self, kernel, outs, args, **more):
        results = call(kernel, outs, self.after(tuple(args)), **more)
        self.token = results[-1] if isinstance(results, (list, tuple)) else results
        return results


class Lanes:
    def __init__(self, orders, dp_size, tensor_size):
        self.orders, self.dp_size, self.tensor_size = orders, dp_size, tensor_size
        self.steps = len(orders[0])
        place = lax.axis_index("dp")
        odd = lax.axis_index("tensor") % 2
        flags = [jnp.where(odd == 1, (place // b) % 2, (place // a) % 2) for a, b in zip(*orders)]
        self.flags = jnp.stack(flags).astype(jnp.int32)

    def swap(self, value, step):
        pairs = [
            (d * self.tensor_size + t, (d ^ self.orders[t % 2][step]) * self.tensor_size + t)
            for d in range(self.dp_size)
            for t in range(self.tensor_size)
        ]
        return lax.ppermute(value, ("dp", "tensor"), pairs)


class Summed:
    def __init__(self, addends, lanes, order):
        self.addends, self.lanes, self.order = addends, lanes, order
        self.height = sum(entry[0].shape[0] for entry in addends)
        self.step = 0
        self.masks = [0]
        self.cargo = None

    def advance(self):
        lanes, steps, step = self.lanes, self.lanes.steps, self.step
        if step == 0 and len(self.addends) == 2:
            args = [entry for pair in self.addends for entry in pair]
        elif step == 0:
            args = list(self.addends[0])
        else:
            args = [self.held, self.got]
        height, width = args[0].shape
        traffic = 6 * height * width
        if step < steps:
            half = shape((self.height // (2 << step), width), bf16)
            work = split_two_kernel if len(args) == 4 else functools.partial(split_kernel, step=step)
            self.held, send = self.order.run(work, [half, half], (lanes.flags, *args), scalars=1, traffic=traffic)
            self.got = lanes.swap(send, step)
        elif self.cargo is not None:
            extra, rows = 2 * self.cargo.shape[0], self.height >> (2 * steps - step)
            if step == steps:
                work, args, out = add_cargo_kernel, (*args, self.cargo), rows
            else:
                work, out = functools.partial(join_cargo_kernel, rows=rows // 2), rows
            self.held = self.order.run(work, shape((out + extra, width), bf16), args, traffic=traffic)
        elif step == steps:
            self.held = self.order.run(add_kernel, shape((height, width), bf16), args, traffic=traffic)
        else:
            self.held = self.order.run(join_kernel_rows, shape((2 * height, width), bf16), args, traffic=traffic)
        if step >= steps:
            back = 2 * steps - 1 - step
            self.got = lanes.swap(self.held, back)
            self.masks = self.masks + [mask ^ (1 << back) for mask in self.masks]
        self.step += 1

    def finish(self):
        starts = []
        for mask in self.masks:
            start, span = 0, self.height
            for step in range(self.lanes.steps):
                span //= 2
                flag = self.lanes.flags[step]
                start = start + span * ((1 - flag) if mask >> step & 1 else flag)
            starts.append(start)
        return [self.held, self.got], starts


class Whole:
    def __init__(self, addends):
        totals = [call(add_kernel, shape(a.shape, bf16), (a, b)) for a, b in addends]
        self.total = lax.psum(jnp.concatenate(totals, axis=0), "dp")
        self.height = self.total.shape[0]

    def advance(self):
        pass

    def finish(self):
        return [self.total], [0]


def placed_parts(starts, refs, count, total, height):
    part = height // total
    for index in range(total):
        ref, j = refs[index // (total // count)], index % (total // count)
        yield pl.multiple_of(starts[index], 16), ref[j * part : (j + 1) * part, :]


def square_kernel(starts, *refs, count, total):
    down_out, up_out, whole = refs[-3:]
    for start, part in placed_parts(starts, refs[:count], count, total, whole.shape[0]):
        whole[pl.ds(start, part.shape[0]), :] = part
    height = down_out.shape[1]
    down_out[0] = whole[:height, :].astype(f32)
    up_out[0] = whole[height:, :].astype(f32)


def grouped_kernel(starts, *refs, count, total, quarter):
    qkv_out, out_out, whole = refs[-3:]
    for start, part in placed_parts(starts, refs[:count], count, total, whole.shape[0]):
        whole[pl.ds(start, part.shape[0]), :] = part
    for i in range(3):
        qkv_out[0, i] = whole[i * quarter : (i + 1) * quarter, :].astype(f32)
    out_out[0] = whole[3 * quarter :, :].astype(f32)


def at_layer(array_shape, layer):
    zeros = (0,) * (len(array_shape) - 1)
    return pl.BlockSpec((1,) + array_shape[1:], lambda i: (layer,) + zeros)


def layer_output(kernel, outs, item, layer, before, order):
    pieces, starts = item.finish()
    starts = jnp.stack([jnp.asarray(start, jnp.int32) for start in starts])
    count, total = len(pieces), starts.shape[0]
    before = before or []
    whole = [pl.BlockSpec(piece.shape, lambda i: (0, 0)) for piece in pieces]
    results = pl.pallas_call(
        functools.partial(kernel, count=count, total=total),
        out_shape=outs,
        grid=(1,),
        in_specs=[SCALARS] + whole + [pl.BlockSpec(memory_space=pl.ANY)] * len(before),
        out_specs=[at_layer(entry.shape, layer) for entry in outs],
        scratch_shapes=[pltpu.VMEM((item.height, pieces[0].shape[1]), bf16)],
        input_output_aliases={1 + count + i: i for i in range(len(before))},
        compiler_params=pltpu.CompilerParams(vmem_limit_bytes=24 << 20),
        cost_estimate=pl.CostEstimate(flops=0, bytes_accessed=sum(entry.size for entry in outs) * 48, transcendentals=0),
    )(starts, *order.after(tuple(pieces)), *before)
    if not before:
        order.token = results[-1]
    return results


def pack_kernel(*refs, quarter, hq):
    shared_out, mine_out, other_out = refs[-3:]
    rest = quarter - PAIR
    for layer in range(LAYERS):
        end, mid, feed, feed_row, up, qv = refs[layer * 5], refs[layer * 5 + 1], refs[layer * 5 + 2], 2 * (layer == 0), refs[layer * 5 + 3], refs[layer * 5 + 4]
        base = layer * 12
        shared_out[base : base + 1, :] = end[0:1]
        shared_out[base + 1 : base + 2, :] = mid[0:1]
        shared_out[base + 2 : base + 3, :] = end[1:2]
        shared_out[base + 3 : base + 4, :] = mid[1:2]
        shared_out[base + 4 : base + 6, :] = mid[2:4]
        shared_out[base + 6 : base + 8, :] = feed[feed_row : feed_row + 2]
        shared_out[base + 8 : base + 9, :] = mid[4:5]
        shared_out[base + 9 : base + 10, :] = feed[feed_row + 2 : feed_row + 3]
        shared_out[base + 10 : base + 12, :] = jnp.zeros_like(mid[0:2])
        for out, up_start, pair_start, rest_start in (
            (mine_out, 0, 0, 2 * PAIR),
            (other_out, hq, PAIR, 2 * PAIR + rest),
        ):
            base = layer * 4
            out[base : base + 4, :] = jnp.zeros_like(mid[0:4])
            out[base : base + 1, :hq] = up[0:1, up_start : up_start + hq]
            out[base + 1 : base + 3, :PAIR] = qv[0:2, pair_start : pair_start + PAIR]
            out[base + 1 : base + 3, PAIR : PAIR + rest] = qv[0:2, rest_start : rest_start + rest]


def unpack_kernel(held, got, gain, shift, qv, out, gates, up, down, *, quarter, hq, rows):
    total = held[...] if rows is None else cargo_of(held, rows) + cargo_of(got, rows)
    for layer in range(LAYERS):
        base = layer * 12
        gain[layer] = total[base : base + 2, :]
        shift[layer] = total[base + 2 : base + 4, :]
        gates[layer] = total[base + 4 : base + 8, :]
        out[layer : layer + 1, :] = total[base + 8 : base + 9, :]
        down[layer : layer + 1, :] = total[base + 9 : base + 10, :]
        base = LAYERS * 12 + layer * 4
        up[layer : layer + 1, :] = total[base : base + 1, :hq]
        qv[layer] = total[base + 1 : base + 3, :quarter]


def body(
    text_embed,
    vision_embed,
    region_mask,
    modality,
    doc_split,
    norm_gain,
    norm_bias,
    qkv_weight,
    qv_bias,
    out_weight,
    out_bias,
    gates,
    up_weight,
    up_bias,
    down_weight,
    down_bias,
    cotangent,
    dp_size,
    tensor_size,
):
    rows, width = text_embed.shape
    here = rows // SLOTS
    quarter = qkv_weight.shape[3]
    hq = up_weight.shape[2]
    wide = 2 * quarter
    pairs = wide // PAIR
    me = lax.axis_index("tensor")
    place = jnp.stack([me, me ^ 2]).astype(jnp.int32)

    def to_core(value):
        return swap(value, "tensor", tensor_size, 1)

    def to_side(value):
        return swap(value, "tensor", tensor_size, 2)

    kinds = modality.reshape(-1, SLOTS)
    reals = region_mask.reshape(-1, SLOTS)
    row_f32, row_bf16 = shape((rows, width), f32), shape((rows, width), bf16)
    wide_bf16, hidden_bf16 = shape((rows, wide), bf16), shape((rows, 2 * hq), bf16)
    sums = shape((8, width), f32)

    def from_hbm(*values):
        return tuple(pltpu.with_memory_space_constraint(value, pltpu.HBM) for value in values)

    state, normed, kind = call(
        functools.partial(start_kernel, here=here),
        [row_f32, row_bf16, shape((rows, 1), f32)],
        (place, *from_hbm(kinds, text_embed, vision_embed, norm_gain, norm_bias)),
        scalars=1,
        traffic=3 << 20,
    )
    inputs = [normed, to_side(normed)]
    qkv_weight = jnp.swapaxes(qkv_weight, 2, 3)
    qkv_other, out_other, qv_other = to_core(qkv_weight), to_core(out_weight), to_core(qv_bias)
    up_later, down_later, shift_later, inputs[1] = lax.optimization_barrier(
        (up_weight, down_weight, up_bias, inputs[1])
    )
    up_other, down_other, shift_other = to_core(up_later), to_core(down_later), to_core(shift_later)
    qv_all = jnp.concatenate(
        [qv_bias[..., :PAIR], qv_other[..., :PAIR], qv_bias[..., PAIR:], qv_other[..., PAIR:]], axis=-1
    )

    tile = shape((here, SLOTS, SLOTS), f32)
    near_cross, near_self, far_cross, far_self, feed_low = call(
        functools.partial(mask_kernel, here=here, layer=LAYERS - 1),
        [tile, tile, tile, tile, row_bf16],
        (place, doc_split, kinds, reals, cotangent, kind, gates),
        scalars=2,
        traffic=2 << 20,
    )
    masks = [(near_cross, far_cross), (near_self, far_self)]
    feed_far_low, _ = lax.optimization_barrier((feed_low, inputs[1]))
    feed_far_low = to_side(feed_far_low)

    joined_weights = [
        call(
            functools.partial(join_kernel, layer=layer, quarter=quarter),
            [shape((3 * wide, width), bf16), shape((wide, width), bf16)],
            (qkv_weight, qkv_other, out_weight, out_other),
            traffic=6 << 20,
        )
        for layer in range(LAYERS)
    ]
    triple = shape((rows, 3 * wide), bf16)

    def attend(value, layer, allowed):
        qkv, out = joined_weights[layer]
        return call(
            functools.partial(attn_kernel, here=here, pairs=pairs),
            [triple, shape((here, pairs, SLOTS, 2 * SLOTS), bf16), wide_bf16, row_bf16],
            (value, qkv, qv_all[layer], out, allowed),
            flops=2 * rows * width * wide * 4 + 4 * rows * SLOTS * wide * 2,
            traffic=5 << 20,
        )

    def attend_back(grad, layer, kept, run):
        qkv, out = joined_weights[layer]
        return run(
            functools.partial(attn_back_kernel, here=here, pairs=pairs),
            [triple, row_bf16],
            (grad, qkv, out, kept[0], kept[1]),
            flops=2 * rows * width * wide * 4 + 8 * rows * SLOTS * wide * 2,
            traffic=5 << 20,
            scratch=[pltpu.VMEM((rows, wide), bf16)],
        )

    def feed(value, layer):
        return call(
            functools.partial(feed_kernel, layer=layer),
            [hidden_bf16, hidden_bf16, row_bf16],
            (value, up_weight, up_other, up_bias, shift_other, down_weight, down_other),
            flops=2 * rows * width * 2 * hq * 2,
            traffic=7 << 20,
        )

    def feed_back(grad, slope, layer, run):
        return run(
            functools.partial(feed_back_kernel, layer=layer),
            [hidden_bf16, row_bf16],
            (grad, slope, up_weight, up_other, down_weight, down_other),
            flops=2 * rows * width * 2 * hq * 2,
            traffic=7 << 20,
        )

    def down_weights(hidden, grads, run):
        square = shape((hq, width), bf16)
        return run(
            down_weights_kernel,
            [square, square],
            (*hidden, *grads),
            flops=2 * rows * width * 2 * hq * 2,
            traffic=5 << 20,
        )

    def up_weights(normed, pre, run):
        across = shape((width, hq), bf16)
        return run(
            up_weights_kernel,
            [across, across, shape((1, 2 * hq), f32)],
            (*normed, *pre),
            flops=2 * rows * width * 2 * hq * 2,
            traffic=5 << 20,
        )

    def attn_weights(normed, grads, mixed, parts, run):
        grouped = shape((4 * quarter, width), bf16)
        return run(
            functools.partial(attn_weights_kernel, quarter=quarter),
            [grouped, grouped, shape((2, wide), f32)],
            (*normed, *grads, *mixed, *parts),
            flops=2 * 2 * rows * width * wide * 4,
            traffic=7 << 20,
        )

    saved = []
    for layer in range(LAYERS):
        near_mask, far_mask = masks[layer % 2]
        kept_near = attend(inputs[0], layer, near_mask)
        kept_far = attend(inputs[1], layer, far_mask)
        attn = (kept_near[3], to_side(kept_far[3]))
        middle, normed_ff = call(
            functools.partial(mid_kernel, layer=layer, branch=0),
            [row_f32, row_bf16],
            (state, *attn, out_bias, gates, kind, norm_gain, norm_bias),
            traffic=3 << 20,
        )
        inputs_ff = [normed_ff, to_side(normed_ff)]
        feed_near = feed(inputs_ff[0], layer)
        feed_far = feed(inputs_ff[1], layer)
        fed = (feed_near[2], feed_far[2] if layer == LAYERS - 1 else to_side(feed_far[2]))
        saved.append(
            (
                state,
                middle,
                attn,
                fed,
                inputs,
                inputs_ff,
                (kept_near, kept_far),
                (feed_near[0], feed_far[0]),
                (feed_near[1], feed_far[1]),
            )
        )
        if layer + 1 < LAYERS:
            state, normed = call(
                functools.partial(mid_kernel, layer=layer, branch=1),
                [row_f32, row_bf16],
                (middle, *fed, down_bias, gates, kind, norm_gain, norm_bias),
                traffic=3 << 20,
            )
            inputs = [normed, to_side(normed)]
    top = LAYERS - 1

    bits = [1 << b for b in range(dp_size.bit_length() - 1)]
    stepped = dp_size == 1 << len(bits) and width % (16 * dp_size) == 0 and len(bits) > 1
    order = Order()
    lanes = Lanes((bits, [bits[1], bits[0]] + bits[2:]), dp_size, tensor_size) if stepped else None
    straight = Lanes((bits, bits), dp_size, tensor_size) if stepped else None

    def summed(*addends, way=lanes):
        return Summed(addends, way, order) if stepped else Whole(addends)

    squares = [shape((LAYERS, hq, width), f32), shape((LAYERS, width, hq), f32)]
    grouped = [shape((LAYERS, 3, quarter, width), f32), shape((LAYERS, quarter, width), f32)]
    group_work = functools.partial(grouped_kernel, quarter=quarter)

    def back_mid(layer, near, far, upstream):
        _, middle, attn = saved[layer][:3]
        return order.run(
            functools.partial(back_mid_kernel, layer=layer),
            [row_f32, row_bf16, sums],
            (near, far, middle, upstream, kind, gates, norm_gain, *attn, out_bias),
            traffic=5 << 20,
        )

    def do_feed_back(side, layer, grad):
        return feed_back(grad, saved[layer][8][side], layer, order.run)

    def do_feed_weights(layer, grads, pre):
        _, _, _, _, _, inputs_ff, _, hidden, _ = saved[layer]
        down_mine, down_rest = down_weights(hidden, grads, order.run)
        down_rest = to_core(down_rest)
        up_mine, up_rest, shift_grad = up_weights(inputs_ff, pre, order.run)
        return summed((down_mine, down_rest), (up_mine, to_core(up_rest))), shift_grad

    def do_attn_back(side, layer, grad):
        return attend_back(grad, layer, saved[layer][6][side], order.run)

    def do_attn_weights(layer, grads, parts):
        kept, inputs = saved[layer][6], saved[layer][4]
        mine, rest, shift_grad = attn_weights(inputs, grads, (kept[0][2], kept[1][2]), parts, order.run)
        return summed((mine, to_core(rest)), way=straight if layer else lanes), shift_grad

    v = {"up1": cotangent}

    def fb_far(l):
        v["pf"], far = do_feed_back(1, l, v["low"][1])
        v["far"] = to_side(far)

    def fb_near(l):
        v["pn"], v["near"] = do_feed_back(0, l, v["low"][0])

    def down_w(l):
        mine, rest = down_weights(saved[l][7], v["low"], order.run)
        v["d"] = (mine, to_core(rest))

    def up_w(l):
        mine, rest, v["us%d" % l] = up_weights(saved[l][5], (v["pn"], v["pf"]), order.run)
        v["F%d" % l] = summed(v["d"], (mine, to_core(rest)), way=lanes)

    def mid_back(l):
        v["mg"], low, v["ms%d" % l] = back_mid(l, v["near"], v["far"], v["up%d" % l])
        v["low"] = [low, to_side(low)]

    def at_near(l):
        v["an"], v["near"] = do_attn_back(0, l, v["low"][0])

    def at_far(l):
        v["af"], far = do_attn_back(1, l, v["low"][1])
        v["far"] = to_side(far)

    def at_w(l):
        v["A%d" % l], v["qs%d" % l] = do_attn_weights(l, v["low"], (v["an"], v["af"]))

    def end_back(l):
        v["up0"], low, v["es1"] = order.run(
            functools.partial(back_end_kernel, layer=1),
            [row_f32, row_bf16, sums],
            (v["near"], v["far"], saved[1][0], v["mg"], kind, gates, norm_gain, *saved[0][3], down_bias),
            traffic=5 << 20,
        )
        v["low"] = [low, to_side(low)]

    def finish(l):
        v["text"], v["vision"], v["es0"] = order.run(
            finish_kernel,
            [row_f32, row_f32, sums],
            (v["near"], v["far"], saved[0][0], v["mg"], kind, norm_gain),
            traffic=5 << 20,
        )

    def send_fed(l):
        (later,) = order.tie(saved[1][3][1])
        v["fed"] = (saved[1][3][0], to_side(later))

    def last(l):
        v["joined"], v["fs"] = order.run(
            functools.partial(last_kernel, layer=1),
            [row_bf16, sums],
            (saved[1][1], *v["fed"], down_bias, gates, kind, cotangent),
            traffic=3 << 20,
        )

    head = LAYERS * 12

    def pack(l):
        packed = shape((LAYERS * 4, width), f32)
        small, mine, other = order.run(
            functools.partial(pack_kernel, quarter=quarter, hq=hq),
            [shape((head, width), f32), packed, packed],
            (
                v["es0"], v["ms0"], v["es1"], v["us0"], v["qs0"],
                v["es1"], v["ms1"], v["fs"], v["us1"], v["qs1"],
            ),
        )
        v["got"] = to_core(jnp.concatenate([small, other], axis=0))
        v["sum"] = jnp.concatenate([small, mine], axis=0)

    def little(step):
        v["sum"] = order.run(add_kernel, shape(v["sum"].shape, f32), (v["sum"], v["got"]))
        if step == 0:
            side = to_side(v["sum"][:head])
            v["got"] = jnp.concatenate([side, jnp.zeros_like(v["sum"][head:])], axis=0)
        elif stepped:
            v["A0"].cargo = v["sum"]
        else:
            v["sum"] = lax.psum(v["sum"], "dp")

    def out_feed(l):
        v["squares"] = layer_output(square_kernel, squares, v["F%d" % l], l, v.get("squares"), order)

    def out_attn(l):
        v["grouped"] = layer_output(group_work, grouped, v["A%d" % l], l, v.get("grouped"), order)

    v["low"] = [feed_low, feed_far_low]
    work = {
        "ff": fb_far, "fn": fb_near, "dw": down_w, "uw": up_w, "mb": mid_back, "an": at_near,
        "af": at_far, "aw": at_w, "eb": end_back, "fi": finish, "sf": send_fed, "la": last, "pk": pack,
        "s": little, "oF": out_feed, "oA": out_attn,
    }
    plan = (
        "ff1", "fn1", "dw1", "uw1", "mb1", "an1", "F1", "af1", "aw1", "F1", "eb1", "fn0", "A1", "F1", "ff0", "dw0", "uw0", "A1", "F1", "mb0", "an0", "F0", "F1", "A1", "af0", "aw0", "F0", "A1", "A0", "F0", "fi0", "A0", "sf1", "A1", "F0", "F1", "la1", "pk0", "A1", "s0", "A0", "F0", "s1", "oA1", "A0", "F0", "oF1", "A0", "A0", "oF0", "oA0",
    )
    for name in plan:
        if name[:-1] in work:
            work[name[:-1]](int(name[-1]))
        else:
            v[name].advance()
    joined, text_grad, vision_grad = v["joined"], v["text"], v["vision"]
    cargo, dp_rows = (v["sum"], v["sum"]), None
    if stepped:
        cargo, dp_rows = (v["A0"].held, v["A0"].got), v["A0"].height // 2
    down_grad, up_grad = v["squares"]
    qkv_grad, out_grad = v["grouped"]
    q = quarter
    flat = shape((LAYERS, width), f32)
    pair = shape((LAYERS, 2, width), f32)
    gain_grad, shift_grad, qv_grad, out_shift, gates_grad, up_shift, down_shift = call(
        functools.partial(unpack_kernel, quarter=q, hq=hq, rows=dp_rows),
        [pair, pair, shape((LAYERS, 2, q), f32), flat, shape((LAYERS, 4, width), f32), shape((LAYERS, hq), f32), flat],
        cargo,
    )
    return (
        joined,
        text_grad,
        vision_grad,
        gain_grad,
        shift_grad,
        jnp.swapaxes(qkv_grad, 2, 3),
        qv_grad,
        out_grad,
        out_shift,
        gates_grad,
        up_grad,
        up_shift,
        down_grad,
        down_shift,
    )


def solution(mesh):
    sizes = dict(mesh.shape)

    def run(*arrays):
        return body(*arrays, dp_size=sizes["dp"], tensor_size=sizes["tensor"])

    placed = (
        P(("dp", "tensor"), None),
        P(("dp", "tensor"), None),
        P("dp"),
        P("dp"),
        P("dp"),
        P(),
        P(),
        P(None, None, None, "tensor"),
        P(None, None, "tensor"),
        P(None, "tensor", None),
        P(),
        P(),
        P(None, None, "tensor"),
        P(None, "tensor"),
        P(None, "tensor", None),
        P(),
        P(("dp", "tensor"), None),
    )
    return jax.shard_map(
        run,
        mesh=mesh,
        in_specs=placed,
        out_specs=(
            P(("dp", "tensor"), None),
            P(("dp", "tensor"), None),
            P(("dp", "tensor"), None),
            P(),
            P(),
            P(None, None, None, "tensor"),
            P(None, None, "tensor"),
            P(None, "tensor", None),
            P(),
            P(),
            P(None, None, "tensor"),
            P(None, "tensor"),
            P(None, "tensor", None),
            P(),
        ),
        check_vma=False,
    )
```
